32 devices in a mesh: dp: 16 (over z, y, x), head: 2 (over core).
Axes of the slice: x: 2, y: 2, z: 4, core: 2. Of those that a mesh axis runs over, the one named last changes fastest.
Arguments:
- latents: bfloat16 [24576, 1280], P(('dp', 'head')), may hold values from -6 to 6
- lang_ids: int32 [96], P(('dp', 'head')), may hold values from 0 to 15
- lang_table: float32 [16, 1280], replicated, may hold values from -3 to 3
- gain_one: bfloat16 [1280], replicated, may hold values from 0.5 to 1.5
- shift_one: bfloat16 [1280], replicated, may hold values from -3 to 3
- w_query: bfloat16 [1280, 1280], P('dp', 'head'), may hold values from -0.15625 to 0.15625
- b_query: bfloat16 [1280], P('head'), may hold values from -2 to 2
- w_key: bfloat16 [1280, 1280], P('dp', 'head'), may hold values from -0.15625 to 0.15625
- w_value: bfloat16 [1280, 1280], P('dp', 'head'), may hold values from -0.15625 to 0.15625
- b_value: bfloat16 [1280], P('head'), may hold values from -2 to 2
- w_out: bfloat16 [1280, 1280], P('head', 'dp'), may hold values from -0.625 to 0.625
- b_out: bfloat16 [1280], replicated, may hold values from -2 to 2
- gain_two: bfloat16 [1280], replicated, may hold values from 0.5 to 1.5
- shift_two: bfloat16 [1280], replicated, may hold values from -3 to 3
- w_up: bfloat16 [1280, 1280], P('dp', 'head'), may hold values from -0.15625 to 0.15625
- b_up: bfloat16 [1280], P('head'), may hold values from -2 to 2
- w_down: bfloat16 [1280, 1280], P('head', 'dp'), may hold values from -0.25 to 0.25
- b_down: bfloat16 [1280], replicated, may hold values from -2 to 2
- cotangent: bfloat16 [24576, 1280], P(('dp', 'head')), may hold values from -6 to 6
Outputs:
- result: bfloat16 [24576, 1280], P(('dp', 'head'))
- latents_grad: bfloat16 [24576, 1280], P(('dp', 'head'))
- lang_table_grad: float32 [16, 1280], replicated
- gain_one_grad: float32 [1280], replicated
- shift_one_grad: float32 [1280], replicated
- w_query_grad: float32 [1280, 1280], P('dp', 'head')
- b_query_grad: float32 [1280], P('head')
- w_key_grad: float32 [1280, 1280], P('dp', 'head')
- w_value_grad: float32 [1280, 1280], P('dp', 'head')
- b_value_grad: float32 [1280], P('head')
- w_out_grad: float32 [1280, 1280], P('head', 'dp')
- b_out_grad: float32 [1280], replicated
- gain_two_grad: float32 [1280], replicated
- shift_two_grad: float32 [1280], replicated
- w_up_grad: float32 [1280, 1280], P('dp', 'head')
- b_up_grad: float32 [1280], P('head')
- w_down_grad: float32 [1280, 1280], P('head', 'dp')
- b_down_grad: float32 [1280], replicated
The draws below stay inside these ranges and needn't reach their ends.
All inputs are finite; a program needn't handle non-finite values.
Results may differ from the reference program's by a relative error of at most 0.014.
Values may be sent and summed in bfloat16 or wider, within the bound.
A program may use at most 192 MiB of HBM per device.

```python
import math
import jax
import jax.numpy as jnp
from jax import lax

D = 1280
H = 8
HS = 160
FF = 1280
LAT = 256
LANGS = 16
ITEMS = 96
TOKENS = 24576


def set_ends(array, rng, smallest, largest):
    extent = array.shape
    index_at = [jax.random.randint(jax.random.fold_in(rng, axis), (), 0, extent[axis]) for axis in range(len(extent))]
    array = array.at[tuple(index_at)].set(smallest)
    longest = extent.index(max(extent))
    index_at[longest] = (index_at[longest] + 1) % extent[longest]
    return array.at[tuple(index_at)].set(largest)


def shard_levels(stream_key, extent, split, least, largest):
    def one(axis_at, parts):
        draws = jax.random.uniform(jax.random.fold_in(jax.random.fold_in(stream_key, 6), axis_at), (parts,), jnp.float32, least / len(split), largest / len(split))
        return jnp.repeat(jnp.exp(draws), extent[axis_at] // parts).reshape((-1,) + (1,) * (len(extent) - axis_at - 1))

    level = one(*split[0])
    for cut in split[1:]:
        level = level * one(*cut)
    return level


def bell_draw(own_key, shape, scale, bound, shards=(), kind=jnp.bfloat16):
    array = jax.random.normal(own_key, shape, jnp.float32) * scale
    if len(shards) > 0:
        array = shard_levels(own_key, shape, shards, -0.22, 0.18) * array
    return jnp.clip(array, min=-bound, max=bound).astype(kind)


def setup_inputs(seed: int = 0) -> dict:
    seeds = jax.random.split(jax.random.key(seed), 20)
    return {
        "latents": bell_draw(seeds[0], (TOKENS, D), 1.0, 6.0, ((0, 32),)),
        "lang_ids": set_ends(jax.random.randint(seeds[1], (ITEMS,), 0, LANGS), jax.random.fold_in(seeds[1], 1), 0, LANGS - 1).astype(jnp.int32),
        "lang_table": bell_draw(seeds[2], (LANGS, D), 0.5, 3.0, (), jnp.float32),
        "gain_one": jnp.clip(1.0 + 0.1 * jax.random.normal(seeds[3], (D,), jnp.float32), 0.5, 1.5).astype(jnp.bfloat16),
        "shift_one": bell_draw(seeds[4], (D,), 0.5, 3.0),
        "w_query": bell_draw(seeds[5], (D, D), D ** -0.5, 0.15625, ((0, 16), (1, 2))),
        "b_query": bell_draw(seeds[6], (D,), 0.3, 2.0, ((0, 2),)),
        "w_key": bell_draw(seeds[7], (D, D), D ** -0.5, 0.15625, ((0, 16), (1, 2))),
        "w_value": bell_draw(seeds[8], (D, D), D ** -0.5, 0.15625, ((0, 16), (1, 2))),
        "b_value": bell_draw(seeds[9], (D,), 0.3, 2.0, ((0, 2),)),
        "w_out": bell_draw(seeds[10], (D, D), (D // 16) ** -0.5, 0.625, ((0, 2), (1, 16))),
        "b_out": bell_draw(seeds[11], (D,), 0.3, 2.0),
        "gain_two": jnp.clip(1.0 + 0.1 * jax.random.normal(seeds[12], (D,), jnp.float32), 0.5, 1.5).astype(jnp.bfloat16),
        "shift_two": bell_draw(seeds[13], (D,), 0.5, 3.0),
        "w_up": bell_draw(seeds[14], (D, FF), D ** -0.5, 0.15625, ((0, 16), (1, 2))),
        "b_up": bell_draw(seeds[15], (FF,), 0.3, 2.0, ((0, 2),)),
        "w_down": bell_draw(seeds[16], (FF, D), (FF // 2) ** -0.5, 0.25, ((0, 2), (1, 16))),
        "b_down": bell_draw(seeds[17], (D,), 0.3, 2.0),
        "cotangent": bell_draw(seeds[18], (TOKENS, D), 1.0, 6.0, ((0, 32),)),
    }


EPSILON = 1e-05
HIGHEST = lax.Precision.HIGHEST

@jax.custom_vjp
def low(v):
    return lax.optimization_barrier(v.astype(jnp.bfloat16)).astype(jnp.float32)

@jax.custom_vjp
def low_back(v):
    return v

def low_keep(v):
    return (low(v), None)

def low_pass(kept, grad):
    return (grad,)

def back_keep(v):
    return (v, None)

def back_low(kept, grad):
    return (low(grad),)
low.defvjp(low_keep, low_pass)
low_back.defvjp(back_keep, back_low)

def layer_norm(row_block, norm_gain, norm_shift):
    row_mean = lax.optimization_barrier(jnp.mean(row_block, axis=-1, keepdims=True))
    centered = row_block - row_mean
    row_var = lax.optimization_barrier(jnp.mean(centered * centered, axis=-1, keepdims=True))
    return centered * lax.rsqrt(row_var + EPSILON) * norm_gain + norm_shift

def matmul(left, right):
    return jnp.dot(left, right, precision=HIGHEST)

def block_forward(params, lat_block, id_block):
    lang_table, gain_one, shift_one, w_query, b_query, w_key, w_value, b_value, w_out, b_out, gain_two, shift_two, w_up, b_up, w_down, b_down = params
    row_total = lat_block.shape[0]
    item_count = row_total // LAT
    embedded = jnp.take(lang_table, id_block, axis=0)
    start_rows = (lat_block.reshape(item_count, LAT, D) + embedded[:, None, :]).reshape(row_total, D)
    input_one = low(layer_norm(start_rows, gain_one, shift_one))
    query_rows = low_back(low(matmul(input_one, w_query) + b_query)).reshape(item_count, LAT, H, HS)
    key_rows = low_back(low(matmul(input_one, w_key))).reshape(item_count, LAT, H, HS)
    value_rows = low_back(low(matmul(input_one, w_value) + b_value)).reshape(item_count, LAT, H, HS)
    scores = low_back(jnp.einsum('iqhc,ikhc->ihqk', query_rows, key_rows, precision=HIGHEST) * HS ** (-0.5))
    row_max = lax.optimization_barrier(jnp.max(scores, axis=-1, keepdims=True))
    exp_scores = jnp.exp(scores - row_max)
    soft_probs = low(exp_scores / lax.optimization_barrier(jnp.sum(exp_scores, axis=-1, keepdims=True)))
    attended = jnp.einsum('ihqk,ikhc->iqhc', soft_probs, value_rows, precision=HIGHEST)
    attended = low_back(low(attended.reshape(row_total, D)))
    middle_rows = start_rows + low_back(matmul(attended, w_out) + b_out)
    input_two = low(layer_norm(middle_rows, gain_two, shift_two))
    pre_act = low_back(matmul(input_two, w_up) + b_up)
    hidden = low(jax.nn.gelu(pre_act, approximate=False))
    return middle_rows + low_back(matmul(hidden, w_down) + b_down)

def reference(latents, lang_ids, lang_table, gain_one, shift_one, w_query, b_query, w_key, w_value, b_value, w_out, b_out, gain_two, shift_two, w_up, b_up, w_down, b_down, cotangent):
    params = tuple((item.astype(jnp.float32) for item in (lang_table, gain_one, shift_one, w_query, b_query, w_key, w_value, b_value, w_out, b_out, gain_two, shift_two, w_up, b_up, w_down, b_down)))
    block_items = math.gcd(ITEMS, 16)
    block_count = ITEMS // block_items
    lat_blocks = latents.astype(jnp.float32).reshape(block_count, block_items * LAT, D)
    id_blocks = lang_ids.reshape(block_count, block_items)
    cot_blocks = cotangent.astype(jnp.float32).reshape(block_count, block_items * LAT, D)

    def step_block(totals, block_data):
        lat_block, id_block, cot_block = block_data

        def forward_only(param_set, rows_in):
            return block_forward(param_set, rows_in, id_block)
        output, pullback = jax.vjp(forward_only, params, lat_block)
        param_grads, rows_grad = pullback(cot_block)
        totals = jax.tree.map(jnp.add, totals, param_grads)
        return (totals, (output.astype(jnp.bfloat16), rows_grad.astype(jnp.bfloat16)))
    zeros_init = jax.tree.map(jnp.zeros_like, params)
    totals, (outputs, input_grads) = lax.scan(step_block, zeros_init, (lat_blocks, id_blocks, cot_blocks))
    result = outputs.reshape(TOKENS, D)
    latents_grad = input_grads.reshape(TOKENS, D)
    g_table, g_gain_one, g_shift_one, g_w_query, g_b_query, g_w_key, g_w_value, g_b_value, g_w_out, g_b_out, g_gain_two, g_shift_two, g_w_up, g_b_up, g_w_down, g_b_down = totals
    return (result, latents_grad, g_table, g_gain_one, g_shift_one, g_w_query, g_b_query, g_w_key, g_w_value, g_b_value, g_w_out, g_b_out, g_gain_two, g_shift_two, g_w_up, g_b_up, g_w_down, g_b_down)
```

```python
import functools
import jax
import jax.numpy as jnp
from jax import lax
from jax.experimental import pallas as pl
from jax.experimental.pallas import tpu as pltpu
from jax.sharding import PartitionSpec as P

MESH = pl.DeviceIdType.MESH
BF = jnp.bfloat16
F32 = jnp.float32
HS = 160
LAT = 256
LANGS = 16
EPSILON = 1e-05
HIGHEST = lax.Precision.HIGHEST
ROOT_HALF = 0.7071067811865476
INV_ROOT_TWO_PI = 0.3989422804014327
FF = 1280


class Place:
    def __init__(self, zs):
        self.zs = zs
        i = lax.axis_index("dp")
        c = lax.axis_index("head")
        self.i, self.c = i, c
        self.z = i // 4
        self.sa = 1 + c
        self.sb = 2 - c
        x = i % 2
        y = (i // 2) % 2
        self.a = jnp.where(c == 0, x, y)
        self.b = jnp.where(c == 0, y, x)
        self.ia = i + self.sa * (1 - 2 * self.a)
        self.ib = i + self.sb * (1 - 2 * self.b)
        self.up = jnp.minimum(i + 4, 4 * zs - 1)
        self.down = jnp.maximum(i - 4, 0)
        self.has_up = self.z < zs - 1
        self.has_down = self.z > 0

    def barrier(self):
        bar = pltpu.get_barrier_semaphore()
        i, c = self.i, self.c
        for dev in ((self.ia, c), (self.ib, c), (i, 1 - c)):
            pl.semaphore_signal(bar, inc=1, device_id=dev, device_id_type=MESH)

        @pl.when(self.has_up)
        def _():
            pl.semaphore_signal(bar, inc=1, device_id=(self.up, c), device_id_type=MESH)

        @pl.when(self.has_down)
        def _():
            pl.semaphore_signal(bar, inc=1, device_id=(self.down, c), device_id_type=MESH)

        n = 3 + jnp.where(self.has_up, 1, 0) + jnp.where(self.has_down, 1, 0)
        pl.semaphore_wait(bar, n)

    def barrier_wide(self):
        bar = pltpu.get_barrier_semaphore()
        me = self.i % 4
        pl.semaphore_signal(bar, inc=1, device_id=(self.i, 1 - self.c), device_id_type=MESH)
        for j in range(4):
            @pl.when(me != j)
            def _(j=j):
                pl.semaphore_signal(bar, inc=1, device_id=(self.i - me + j, self.c), device_id_type=MESH)
        for zz in range(self.zs):
            @pl.when(self.z != zz)
            def _(zz=zz):
                pl.semaphore_signal(bar, inc=1, device_id=(4 * zz + me, self.c), device_id_type=MESH)
        pl.semaphore_wait(bar, 3 + self.zs)


ORDER_ONE = (
    0, 20, -1, -2, 2, 27, 22, -3, 10, 23, 7, 30, 28, 40, 60, 8, 29, 31, 24, 11,
    67, 9, 42, 12, 62, 68, 32, 25, 80, 100, 50, 63, 69, 70, 47, 13, 64, 33, 1, 21,
    107, 48, -4, 71, 65, -5, 51, 82, 102, 49, -6, 120, 140, 108, 72, 52, 109, 90, 103, 87,
    73, 110, 53, 147, 61, 104, 122, 41, 142, 160, 180, -7, 88, 105, -8, 148, 111, 91, -9, 89,
    149, 143, 112, 127, 130, 187, 92, 150, 200, 220, 113, 162, 182, 128, 93, 144, 101, 188, 145, 81,
    -10, 129, -11, 151, 189, 131, 183, -12, -13, -14, 167, -15, -16, 170, 227, 152, 202, 132, 222, -19,
    184, 190, 153, -17, 168, 133, 228, -20, 141, -18, 185, 121, -21, -22, 169, 229, 191, 171, 223, -23,
    207, 172, 192, 224, 193, 210, -24, 230, 225, 208, 173, 181, 209, 161, -25, 211, 231, -26, 232, 233,
    212, 213, -27, 221, 201,
)
ORDER_TWO = (
    100, 101, 200, 102, 201, 103, 202, 0, 203, 300, 503, 1, 301, 2, 110, 302, 502, 111, 112, 210,
    303, 400, 603, 401, 402, 211, 501, 113, 20, 212, 310, 513, 602, 403, 213, 700, 21, 311, 601, 512,
    312, 800, 410, 613, 22, 511, 313, 900, 411, 412, 120, 121, 413, 612, 122, 710, 123, 611, 220, 30,
    910, 31, 810, 221, 32, 320, 222, 523, 40, 223, 50, 321, 420, 623, 41, 522, 322, 51, 323, 42,
    521, 421, 622, 422, 423, 52, 130, 131, 720, 621, 132, 133, 920, 820, 140, 141, 142, 143, 150, 151,
    230, 152, 153, 231, 60, 330, 533, 232, 331, 430, 633, 233, 61, 532, 332, 431, 240, 333, 531, 632,
    432, 241, 340, 543, 242, 433, 62, 631, 730, 341, 243, 440, 830, 643, 542, 250, 342, 930, 441, 251,
    541, 642, 343, 10, 11, 252, 442, 350, 553, 641, 70, 740, 253, 12, 351, 443, 71, 840, 552, 72,
    352, 450, 940, 653, 73, 551, 353, 451, 452, 74, 453, 652, 750, 75, 651, 950, 850,
)
PARTS = (((True, 0, 48), (False, 48, 32)),) * 6


def nn(a, b):
    return lax.dot_general(a, b, (((1,), (0,)), ((), ())), preferred_element_type=F32)


def nt(a, b):
    return lax.dot_general(a, b, (((1,), (1,)), ((), ())), preferred_element_type=F32)


def tn(a, b):
    return lax.dot_general(a, b, (((0,), (0,)), ((), ())), preferred_element_type=F32)


def item_rows(i):
    return pl.ds(i * LAT, LAT)


def head_window(hh):
    at = lax.broadcasted_iota(jnp.int32, (1, 256), 1) + hh * 128
    return (at >= hh * HS) & (at < (hh + 1) * HS)


class Gather:
    def __init__(self, p, w, sems, streams):
        self.p, self.w, self.streams = p, w, streams
        self.zsend, self.zrecv, self.asend, self.arecv, self.bsend, self.brecv, self.csend, self.crecv = sems
        self.cols = pl.ds(pl.multiple_of(p.c * 640, 128), 640)

    def sub(self, s, j, n=None):
        k, mid, r0, rows = self.streams[s]
        return self.w.at[k, j if n is None else pl.ds(j, n), pl.ds(r0, rows), self.cols]

    def mid(self, s):
        return self.streams[s][1]

    def send(self, s, j, n, dev, ssem, rsem):
        ref = self.sub(s, j) if n == 1 else self.sub(s, j, n)
        pltpu.make_async_remote_copy(ref, ref, ssem, rsem, device_id=dev, device_id_type=MESH).start()

    def arrived(self, s, n, sem):
        ref = self.sub(s, 0, n)
        pltpu.make_async_copy(ref, ref, sem).wait()

    def members(self, s, zz):
        p = self.p
        base = zz * 4 + p.b * p.sb
        return (base, base + p.sa) if self.mid(s) else (base + p.a * p.sa,)

    def z_send(self, s, zz, upward):
        p = self.p
        dev, d = ((p.up, p.c), 0) if upward else ((p.down, p.c), 1)
        for j in self.members(s, zz):
            self.send(s, j, 1, dev, self.zsend.at[s, d, zz], self.zrecv.at[s, zz])

    def z_first(self, s):
        p = self.p
        pl.when(p.has_up)(lambda: self.z_send(s, p.z, True))
        pl.when(p.has_down)(lambda: self.z_send(s, p.z, False))

    def at_distance(self, d, f):
        p = self.p
        pl.when(p.z - d >= 0)(lambda: f(p.z - d, True))
        pl.when(p.z + d <= p.zs - 1)(lambda: f(p.z + d, False))

    def around(self, d, f):
        if d == 0:
            f(self.p.z)
        else:
            self.at_distance(d, lambda zz, below: f(zz))

    def z_arrive(self, s, d, then):
        p = self.p
        n = len(self.members(s, 0))

        def f(zz, below):
            self.arrived(s, n, self.zrecv.at[s, zz])
            if d < p.zs - 1:
                if below:
                    pl.when(p.has_up)(lambda: self.z_send(s, zz, True))
                else:
                    pl.when(p.has_down)(lambda: self.z_send(s, zz, False))
            then(s, zz)

        self.at_distance(d, f)

    def a_send(self, s, zz):
        p = self.p
        j = zz * 4 + p.b * p.sb + p.a * p.sa
        self.send(s, j, 1, (p.ia, p.c), self.asend.at[s], self.arecv.at[s, zz])

    def a_arrive(self, s, zz, then):
        self.arrived(s, 1, self.arecv.at[s, zz])
        then(s, zz)

    def b_send(self, s, zz):
        p = self.p
        base = zz * 4 + p.b * p.sb
        for j in (base, base + p.sa):
            self.send(s, j, 1, (p.ib, p.c), self.bsend.at[s], self.brecv.at[s, zz])

    def b_arrive(self, s, zz):
        p = self.p
        self.arrived(s, 2, self.brecv.at[s, zz])
        self.send(s, zz * 4, 4, (p.i, 1 - p.c), self.csend.at[s], self.crecv.at[s])

    def do(self, s, ev):
        p = self.p
        if ev == 0:
            if not self.mid(s):
                self.z_first(s)
            self.a_send(s, p.z)
        elif ev == 1:
            self.arrived(s, 4 * p.zs, self.crecv.at[s])
        elif ev >= 10:
            self.around(ev - 10, lambda zz: self.b_arrive(s, zz))
        elif ev >= 6:
            self.z_arrive(s, ev - 6, self.b_send if self.mid(s) else self.a_send)
        elif self.mid(s):
            self.arrived(s, 1, self.arecv.at[s, p.z])
            self.z_first(s)
            self.b_send(s, p.z)
        else:
            self.around(ev - 2, lambda zz: self.a_arrive(s, zz, self.b_send))

    def drain(self, s):
        p = self.p
        n = len(self.members(s, 0))
        for zz in range(p.zs):
            @pl.when(jnp.logical_and(p.has_up, zz <= p.z))
            def _(zz=zz):
                self.arrived(s, n, self.zsend.at[s, 0, zz])

            @pl.when(jnp.logical_and(p.has_down, zz >= p.z))
            def _(zz=zz):
                self.arrived(s, n, self.zsend.at[s, 1, zz])
        self.arrived(s, 1 if self.mid(s) else p.zs, self.asend.at[s])
        self.arrived(s, 2 * p.zs, self.bsend.at[s])
        self.arrived(s, 4 * p.zs, self.csend.at[s])


STREAMS = tuple((k, m, r0, r) for k in range(6) for m, r0, r in ((True, 0, 48), (False, 48, 32)))
SAVED = ("one_t", "q", "k", "v", "att", "hid", "slope", "two_t", "cot_t", "u1", "u2")
TALL = ("one_t", "two_t", "cot_t")


def forward_kernel(zs, *refs):
    lat_in, cot_in, ids, table = refs[:4]
    vectors, shards = refs[4:12], refs[12:18]
    at = 18
    outs = dict(zip(("w",) + SAVED + ("mid", "inv", "probs"), refs[at:at + 15]))
    at += 15
    bufs = dict(zip(("w",) + SAVED + ("mid", "inv", "probs", "lat", "cot", "one", "two", "hb", "fulls"), refs[at:at + 21]))
    at += 21
    gsems = refs[at:at + 8]
    own, load, save, hsem = refs[at + 8:at + 12]
    p = Place(zs)
    w = bufs["w"]
    g = Gather(p, w, gsems, STREAMS)
    hb = bufs["hb"]
    copies = [pltpu.make_async_copy(shards[k], w.at[k, p.i, :, g.cols], own.at[k]) for k in range(6)]
    for cp in copies:
        cp.start()
    loads = [pltpu.make_async_copy(src.at[item_rows(i)], bufs[n].at[item_rows(i)], load.at[j, i])
             for j, (src, n) in enumerate(((lat_in, "lat"), (cot_in, "cot"))) for i in range(3)]
    for cp in loads:
        cp.start()
    fulls = bufs["fulls"]
    for n in range(5):
        fulls[n:n + 1, :] = vectors[n][...].astype(F32)[None, :]
    for n in range(3):
        hb[n:n + 1, g.cols] = vectors[5 + n][...].astype(F32)[None, :]
    p.barrier()
    half_send = pltpu.make_async_remote_copy(hb.at[:, g.cols], hb.at[:, g.cols], hsem.at[0], hsem.at[1],
                                             device_id=(p.i, 1 - p.c), device_id_type=MESH)
    half_send.start()
    names = ("w",) + SAVED + ("mid", "inv", "probs")
    saves = []

    def keep(name, index=None):
        src, dst = bufs[name], outs[name]
        if index is not None:
            src, dst = src.at[index], dst.at[index]
        n = len(saves)
        assert n < save.shape[0]
        cp = pltpu.make_async_copy(src, dst, save.at[n])
        cp.start()
        saves.append(cp)

    def start_of(i):
        return bufs["lat"][item_rows(i)].astype(F32) + table[pl.ds(ids[i], 1), :]

    def norm(v):
        mean = jnp.mean(v, axis=1, keepdims=True)
        cen = v - mean
        inv = lax.rsqrt(jnp.mean(cen * cen, axis=1, keepdims=True) + EPSILON)
        return cen * inv, inv

    def norm_rows(i, n, rows_of, u_name, out_name, tall_name):
        gain, shift = fulls[2 * n:2 * n + 1, :], fulls[2 * n + 1:2 * n + 2, :]

        def body(r, carry):
            rows = pl.ds(pl.multiple_of(i * LAT + r * 64, 64), 64)
            unit, inv = norm(rows_of(rows))
            bufs[u_name][rows, :] = unit.astype(BF)
            bufs[out_name][rows, :] = (unit * gain + shift).astype(BF)
            bufs["inv"][n, rows, :] = jnp.broadcast_to(inv, (64, 128))
            return carry

        lax.fori_loop(0, 4, body, 0)
        bufs[tall_name][:, item_rows(i)] = bufs[out_name][item_rows(i), :].T

    def whole(k):
        return w[k].reshape(1280, 1280)

    def ln1(i):
        loads[i].wait()
        emb = table[pl.ds(ids[i], 1), :]
        norm_rows(i, 0, lambda rows: bufs["lat"][rows, :].astype(F32) + emb, "u1", "one", "one_t")

    def project(name, k, bias):
        def f(i):
            y = nn(bufs["one"][item_rows(i), :], whole(k))
            if bias is not None:
                y = y + hb[bias:bias + 1, :]
            bufs[name][item_rows(i), :] = y.astype(BF)
        return f

    def cot(i):
        loads[3 + i].wait()
        bufs["cot_t"][:, item_rows(i)] = bufs["cot"][item_rows(i), :].T

    def attend(half):
        def f(i):
            rows = item_rows(i)
            zero = jnp.zeros((), BF)
            acc = [None] * 5
            for hh in range(4):
                lanes = pl.ds(half * 640 + hh * 128, 256)
                mask = head_window(hh)
                qm = jnp.where(mask, bufs["q"][rows, lanes], zero)
                s = nt(qm, bufs["k"][rows, lanes]) * (HS ** -0.5)
                e = jnp.exp(s - jnp.max(s, axis=1, keepdims=True))
                pr = (e / jnp.sum(e, axis=1, keepdims=True)).astype(BF)
                bufs["probs"][i * 8 + half * 4 + hh] = pr
                vm = jnp.where(mask, bufs["v"][rows, lanes], zero)
                a = nn(pr, vm)
                for t in (0, 1):
                    piece = a[:, t * 128:(t + 1) * 128]
                    acc[hh + t] = piece if acc[hh + t] is None else acc[hh + t] + piece
            for t in range(5):
                bufs["att"][rows, pl.ds(half * 640 + t * 128, 128)] = acc[t].astype(BF)
        return f

    def out(i):
        rows = item_rows(i)
        emb = table[pl.ds(ids[i], 1), :]
        y = nt(bufs["att"][rows, :], whole(3))
        bufs["mid"][rows, :] = y + fulls[4:5, :] + (bufs["lat"][rows, :].astype(F32) + emb)
        norm_rows(i, 1, lambda r: bufs["mid"][r, :], "u2", "two", "two_t")

    def up(i):
        rows = item_rows(i)
        pre = nn(bufs["two"][rows, :], whole(4)) + hb[2:3, :]
        cdf = 0.5 * (1.0 + lax.erf(pre * ROOT_HALF))
        bufs["hid"][rows, :] = (pre * cdf).astype(BF)
        bufs["slope"][rows, :] = (cdf + pre * jnp.exp(-0.5 * pre * pre) * INV_ROOT_TWO_PI).astype(BF)

    units = (ln1, project("q", 0, 0), project("k", 1, None), project("v", 2, 1), cot, attend(0), attend(1), out, up)
    after = (("u1", "one_t"), ("q",), ("k",), ("v",), ("cot_t",), (), ("att", "probs"), ("u2", "two_t", "mid", "inv"), ("hid", "slope"))
    seen, full = set(), {}
    for code in ORDER_ONE:
        if code < 0:
            n, i = (-code - 1) // 3, (-code - 1) % 3
            if n == 1 and i == 0:
                half_send.wait_recv()
            units[n](i)
            if i == 2:
                for name in after[n]:
                    keep(name)
            continue
        s, ev = code // 20, code % 20
        k = STREAMS[s][0]
        if k not in seen:
            copies[k].wait()
            seen.add(k)
        g.do(s, ev)
        if ev == 1:
            full[k] = full.get(k, 0) + 1
            if full[k] == 2:
                keep("w", k)
    half_send.wait_send()
    for s in range(len(STREAMS)):
        g.drain(s)
    for cp in saves:
        cp.wait()


def forward(latents, cotangent, ids, table, vectors, shards, zs):
    n = 4 * zs
    rows, width = latents.shape
    s = len(STREAMS)
    DMA = pltpu.SemaphoreType.DMA
    shape = {k: ((width, rows) if k in TALL else (rows, width), BF) for k in SAVED}
    shape["w"] = ((6, n, shards[0].shape[0], width), BF)
    shape["mid"] = ((rows, width), F32)
    shape["inv"] = ((2, rows, 128), F32)
    shape["probs"] = ((24, LAT, LAT), BF)
    for k in ("lat", "cot", "one", "two"):
        shape[k] = ((rows, width), BF)
    shape["hb"] = shape["fulls"] = ((8, width), F32)
    names = ("w",) + SAVED + ("mid", "inv", "probs")
    got = pl.pallas_call(
        functools.partial(forward_kernel, zs),
        out_shape=[jax.ShapeDtypeStruct(*shape[k]) for k in names],
        in_specs=[pl.BlockSpec(memory_space=pl.ANY)] * 2 + [pl.BlockSpec(memory_space=pltpu.SMEM)]
        + [pl.BlockSpec(memory_space=pltpu.VMEM)] * 9 + [pl.BlockSpec(memory_space=pl.ANY)] * 6,
        out_specs=[pl.BlockSpec(memory_space=pl.ANY)] * len(names),
        scratch_shapes=[pltpu.VMEM(*shape[k]) for k in names + ("lat", "cot", "one", "two", "hb", "fulls")] + [
            DMA((s, 2, zs)), DMA((s, zs)), DMA((s,)), DMA((s, zs)), DMA((s,)), DMA((s, zs)), DMA((s,)), DMA((s,)),
            DMA((6,)), DMA((2, 3)), DMA((24,)), DMA((2,)),
        ],
        compiler_params=pltpu.CompilerParams(collective_id=0, has_side_effects=True, vmem_limit_bytes=62 << 20),
        name="gather_and_forward",
    )(latents, cotangent, ids, table, *vectors, *shards)
    return dict(zip(names, got))


NAMES_TWO = ("pool", "tall", "flat", "mg", "probs", "inv", "yb", "sm", "rc", "rb", "rz", "ra", "arc", "arp", "arz", "tot")


class Scatter:
    def __init__(self, p, g, bufs, outs, sems, parts):
        self.p, self.g, self.parts, self.outs = p, g, parts, outs
        self.rc, self.rb, self.rz, self.ra = (bufs[n] for n in ("rc", "rb", "rz", "ra"))
        (self.csend, self.crecv, self.bsend, self.brecv, self.zsend, self.zrecv, self.asend, self.arecv, self.credit) = sems
        self.cols = pl.ds(pl.multiple_of(p.c * 640, 128), 640)
        self.others = pl.ds(pl.multiple_of((1 - p.c) * 640, 128), 640)

    def plane(self, t):
        val = jnp.int32(FAR[0][t])
        for s in range(1, self.p.zs):
            val = jnp.where(self.p.z == s, FAR[s][t], val)
        return val

    def rows(self, j, r0, n):
        return pl.ds(pl.multiple_of(j * 80 + r0, 16), n)

    def own(self, k, j, r0, n):
        return self.g(k).at[self.rows(j, r0, n), self.cols]

    def move(self, src, dst, dev, ssem, rsem):
        pltpu.make_async_remote_copy(src, dst, ssem, rsem, device_id=dev, device_id_type=MESH).start()

    def wait(self, ref, sem):
        pltpu.make_async_copy(ref, ref, sem).wait()

    def add(self, ref, val):
        ref[...] = ref[...] + val

    def group(self, t):
        return pl.ds(pl.multiple_of(self.plane(t) * 320, 320), 320)

    def c_send(self, k, t):
        p = self.p
        if k >= 3 and t == 0:
            pl.semaphore_wait(self.credit, 1)
        rows = self.group(t)
        self.move(self.g(k).at[rows, self.others], self.rc.at[k % 3, rows], (p.i, 1 - p.c), self.csend.at[k], self.crecv.at[k, self.plane(t)])

    def c_arrive(self, k, t):
        p = self.p
        zz = self.plane(t)
        rows = self.group(t)
        src = self.rc.at[k % 3, rows]
        self.wait(src, self.crecv.at[k, zz])
        self.add(self.g(k).at[rows, self.cols], src[...])
        if k < 3 and t == 3:
            pl.semaphore_signal(self.credit, inc=1, device_id=(p.i, 1 - p.c), device_id_type=MESH)
        away = zz * 4 + (1 - p.b) * p.sb
        for n, j in enumerate((away, away + p.sa)):
            self.move(self.own(k, j, 0, 80), self.rb.at[k, zz * 2 + n], (p.ib, p.c), self.bsend.at[k], self.brecv.at[k, zz])

    def b_arrive(self, k, t):
        p = self.p
        zz = self.plane(t)
        self.wait(self.rb.at[k, pl.ds(zz * 2, 2)], self.brecv.at[k, zz])
        base = zz * 4 + p.b * p.sb
        for n, j in enumerate((base, base + p.sa)):
            self.add(self.own(k, j, 0, 80), self.rb[k, zz * 2 + n])
        for mid, r0, n in self.parts[k]:
            if not mid:
                self.move(self.own(k, base + (1 - p.a) * p.sa, r0, n), self.ra.at[k, zz, pl.ds(r0, n)], (p.ia, p.c),
                          self.asend.at[k, 0], self.arecv.at[k, 0, zz])

    def part(self, k, mid):
        for m, r0, n in self.parts[k]:
            if m == mid:
                return r0, n
        return None

    def a_arrive(self, k, t):
        p = self.p
        if self.part(k, False) is None:
            return
        r0, n = self.part(k, False)
        zz = self.plane(t)
        src = self.ra.at[k, zz, pl.ds(r0, n)]
        self.wait(src, self.arecv.at[k, 0, zz])
        self.add(self.own(k, zz * 4 + p.b * p.sb + p.a * p.sa, r0, n), src[...])

    def members(self, mid, zz):
        p = self.p
        base = zz * 4 + p.b * p.sb
        return (base, base + p.sa) if mid else (base + p.a * p.sa,)

    def slot(self, zz, up, end):
        return zz if up or not end else self.p.zs

    def landing(self, k, mid, zz, up, end):
        r0, n = self.part(k, mid)
        return self.rz.at[k, self.slot(zz, up, end), pl.ds(0 if mid else 2 * r0, 2 * n if mid else n)]

    def z_take(self, k, mid, zz, up, end):
        m = 0 if mid else 1
        r0, n = self.part(k, mid)
        src = self.landing(k, mid, zz, up, end)
        self.wait(src, self.zrecv.at[k, m, self.slot(zz, up, end)])
        for q, j in enumerate(self.members(mid, zz)):
            self.add(self.own(k, j, r0, n), src[q * n:(q + 1) * n])

    def z_pass(self, k, mid, zz, up, end):
        p = self.p
        m = 0 if mid else 1
        r0, n = self.part(k, mid)
        at = self.slot(zz, up, end)
        dev = (p.up if up else p.down, p.c)
        for q, j in enumerate(self.members(mid, zz)):
            self.move(self.own(k, j, r0, n), self.rz.at[k, at, pl.ds(q * n if mid else 2 * r0, n)], dev, self.zsend.at[k, m, zz], self.zrecv.at[k, m, at])

    def z_step(self, k, mid, d):
        p = self.p
        if self.part(k, mid) is None:
            return

        @pl.when(p.z + d <= p.zs - 1)
        def _():
            if d < p.zs - 1:
                pl.when(p.has_down)(lambda: self.z_take(k, mid, p.z + d, True, False))
            self.z_pass(k, mid, p.z + d, True, d == 1)

        @pl.when(p.z - d >= 0)
        def _():
            if d < p.zs - 1:
                pl.when(p.has_up)(lambda: self.z_take(k, mid, p.z - d, False, False))
            self.z_pass(k, mid, p.z - d, False, d == 1)

    def z_end(self, k, mid):
        p = self.p
        if self.part(k, mid) is None:
            return
        r0, n = self.part(k, mid)
        pl.when(p.has_down)(lambda: self.z_take(k, mid, p.z, True, True))
        pl.when(p.has_up)(lambda: self.z_take(k, mid, p.z, False, True))
        if mid:
            base = p.z * 4 + p.b * p.sb
            self.move(self.own(k, base + (1 - p.a) * p.sa, r0, n), self.ra.at[k, 0, pl.ds(r0, n)], (p.ia, p.c),
                      self.asend.at[k, 1], self.arecv.at[k, 1, 0])
        else:
            self.outs[k][r0:r0 + n, :] = self.own(k, p.i, r0, n)[...].astype(F32)

    def finish(self, k):
        if self.part(k, True) is None:
            return
        r0, n = self.part(k, True)
        src = self.ra.at[k, 0, pl.ds(r0, n)]
        self.wait(src, self.arecv.at[k, 1, 0])
        self.outs[k][r0:r0 + n, :] = self.own(k, self.p.i, r0, n)[...].astype(F32) + src[...].astype(F32)

    def drain(self, k):
        p = self.p
        zs = p.zs
        self.wait(self.rc.at[k % 3], self.csend.at[k])
        self.wait(self.rb.at[k], self.bsend.at[k])
        for m, mid in enumerate((True, False)):
            if self.part(k, mid) is None:
                continue
            r0, n = self.part(k, mid)
            if mid:
                self.wait(self.ra.at[k, 0, pl.ds(r0, n)], self.asend.at[k, 1])
            else:
                self.wait(self.ra.at[k, :, pl.ds(r0, n)], self.asend.at[k, 0])
            for zz in range(zs):
                @pl.when(p.z != zz)
                def _(zz=zz, mid=mid, m=m):
                    self.wait(self.landing(k, mid, zz, True, False), self.zsend.at[k, m, zz])


FAR = ((3, 2, 1, 0), (3, 0, 2, 1), (0, 3, 1, 2), (0, 1, 2, 3))
GRADS = ("down", "up", "out", "value", "key", "query")


def backward_kernel(zs, *refs):
    ids, gain_one, gain_two, b_down = refs[:4]
    ins = dict(zip(("w",) + SAVED + ("mid", "inv", "probs", "cot"), refs[4:20]))
    outs = refs[20:26]
    res_out, lat_out, sm_out = refs[26:29]
    bufs = dict(zip(NAMES_TWO, refs[29:45]))
    rsems = refs[45:54]
    lsem, osem, tsem = refs[54:57]
    p = Place(zs)
    pool, tall, flat, mg, probs, inv, yb, sm = (bufs[n] for n in NAMES_TWO[:8])
    tokens = 768
    seat = (2, 3, 4, 5, 2, 3)
    s = Scatter(p, lambda k: pool.at[seat[k]], bufs, outs, rsems, PARTS)
    count = [0]

    def load(src, dst):
        assert count[0] < lsem.shape[0]
        cp = pltpu.make_async_copy(src, dst, lsem.at[count[0]])
        count[0] += 1
        cp.start()
        return cp

    def slot(n, i=None):
        return flat.at[pl.ds(n * tokens, tokens)] if i is None else flat.at[pl.ds(n * tokens + i * LAT, LAT)]

    hid, pre, cot, u2, att, ky = range(6)
    ag, bg, qy, vy, u1 = hid, pre, cot, u2, att
    ready = {}

    def fetch(name, src, dst):
        ready[name] = load(src, dst)

    def need(name):
        cp = ready.pop(name, None)
        if cp is not None:
            cp.wait()

    fetch("hid", ins["hid"], slot(hid))
    fetch("cot_t", ins["cot_t"], tall.at[0])
    fetch("wd", ins["w"].at[5], pool.at[0])
    fetch("cot", ins["cot"], slot(cot))
    fetch("pre", ins["slope"], slot(pre))
    fetch("two_t", ins["two_t"], tall.at[1])
    fetch("wu", ins["w"].at[4], pool.at[1])
    fetch("u2", ins["u2"], slot(u2))
    fetch("inv", ins["inv"], inv)
    fetch("att", ins["att"], slot(att))
    fetch("ky", ins["k"], slot(ky))
    fetch("probs", ins["probs"], probs)
    sm[...] = jnp.zeros(sm.shape, F32)
    p.barrier_wide()
    results = []

    def col_sum(row, val):
        sm[row:row + 1, :] += jnp.sum(val, axis=0, keepdims=True)

    def blocks(i, f):
        def body(r, carry):
            f(pl.ds(pl.multiple_of(r * 64, 64), 64), pl.multiple_of(i * LAT + r * 64, 64))
            return carry
        lax.fori_loop(0, 4, body, 0)

    def at(n, start, size=64):
        return flat.at[pl.ds(n * tokens + start, size)]

    left = {"g0": (0, hid), "g1": (1, pre), "g2": (0, att), "g3": (1, vy), "g4": (1, ky), "g5": (1, qy)}
    before = (("hid", "cot_t"), ("two_t",), ("att",), ("one_t",), (), ())

    def grad(k, t):
        if t == 0:
            for n in before[k]:
                need(n)
            if k >= 4:
                s.drain(k - 4)
        a, b = left["g%d" % k]
        rows = s.group(t)
        pool[seat[k], rows, :] = nn(tall[a, rows, :], slot(b)[...]).astype(BF)
        s.c_send(k, t)

    def unit_p(i):
        for n in ("wd", "cot", "pre"):
            need(n)
        yb[...] = nn(slot(cot, i)[...], pool[0])

        def f(r, start):
            ref = at(pre, start)
            v = (yb[r, :] * ref[...].astype(F32)).astype(BF)
            ref[...] = v
            col_sum(2, v.astype(F32))
            col_sum(4, at(cot, start)[...].astype(F32))

        blocks(i, f)

    def unit_n(i):
        for n in ("wd", "hid", "mid%d" % i):
            need(n)
        yb[...] = nt(slot(vy, i)[...], pool[0])

        def f(r, start):
            at(vy, start)[...] = (mg[pl.ds(start, 64), :] + (yb[r, :] + b_down[...].astype(F32)[None, :])).astype(BF)

        blocks(i, f)
        cp = pltpu.make_async_copy(slot(vy, i), res_out.at[item_rows(i)], osem.at[i])
        cp.start()
        results.append(cp)

    def norm_back(r, n, unit, start, gain_row, shift_row, gain):
        y = yb[r, :]
        v = unit[...].astype(F32)
        sc = y * gain
        m1 = jnp.mean(sc, axis=1, keepdims=True)
        m2 = jnp.mean(sc * v, axis=1, keepdims=True)
        col_sum(gain_row, y * v)
        col_sum(shift_row, y)
        iv = inv[n, pl.ds(start, 64), :][:, 0:1]
        return (sc - m1 - v * m2) * iv

    def unit_t(i):
        for n in ("wu", "u2", "inv"):
            need(n)
        yb[...] = nt(slot(pre, i)[...], pool[1])

        def f(r, start):
            back = norm_back(r, 1, at(u2, start), start, 7, 8, gain_two[...].astype(F32)[None, :])
            m = at(cot, start)[...].astype(F32) + back
            mg[pl.ds(start, 64), :] = m
            b = m.astype(BF)
            at(bg, start)[...] = b
            col_sum(3, b.astype(F32))

        blocks(i, f)
        if i == 0:
            fetch("wo", ins["w"].at[3], pool.at[0])
        tall[0, :, item_rows(i)] = slot(bg, i)[...].T
        if i == 2:
            fetch("wv", ins["w"].at[2], pool.at[1])
            fetch("qy", ins["q"], slot(qy))
            fetch("vy", ins["v"], slot(vy))
            fetch("one_t", ins["one_t"], tall.at[1])

    def unit_y(i):
        need("wo")
        slot(ag, i)[...] = nn(slot(bg, i)[...], pool[0]).astype(BF)
        if i == 2:
            fetch("wk", ins["w"].at[1], pool.at[0])

    def unit_w(half):
        def f(i):
            for n in ("qy", "vy", "ky", "probs"):
                need(n)
            zero = jnp.zeros((), BF)
            accs = [[None] * 5 for _ in range(3)]
            qr, kr, vr, gr = slot(qy, i), slot(ky, i), slot(vy, i), slot(ag, i)
            for hh in range(4):
                lanes = pl.ds(half * 640 + hh * 128, 256)
                mask = head_window(hh)
                gm = jnp.where(mask, gr[:, lanes], zero)
                pb = probs[i * 8 + half * 4 + hh]
                dp = nt(gm, vr[:, lanes])
                pf = pb.astype(F32)
                inner = jnp.sum(dp * pf, axis=1, keepdims=True)
                ds = (pf * (dp - inner)).astype(BF)
                dv = tn(pb, gm)
                dq = nn(ds, jnp.where(mask, kr[:, lanes], zero)) * (HS ** -0.5)
                dk = tn(ds, jnp.where(mask, qr[:, lanes], zero)) * (HS ** -0.5)
                for acc, val in zip(accs, (dq, dk, dv)):
                    for t in (0, 1):
                        piece = val[:, t * 128:(t + 1) * 128]
                        acc[hh + t] = piece if acc[hh + t] is None else acc[hh + t] + piece
            for acc, ref, row in zip(accs, (qr, kr, vr), (0, None, 1)):
                for t in range(5):
                    lanes = pl.ds(half * 640 + t * 128, 128)
                    b = acc[t].astype(BF)
                    ref[:, lanes] = b
                    if row is not None:
                        sm[row:row + 1, lanes] += jnp.sum(b.astype(F32), axis=0, keepdims=True)
            if i == 2 and half == 1:
                fetch("wq", ins["w"].at[0], flat.at[pl.ds(0, 1280)])
                fetch("u1", ins["u1"], slot(u1))
        return f

    def unit_s(i):
        for n in ("wq", "wk", "wv", "u1"):
            need(n)
        yb[...] = nt(slot(qy, i)[...], flat[0:1280, :])
        yb[...] += nt(slot(ky, i)[...], pool[0])
        yb[...] += nt(slot(vy, i)[...], pool[1])
        mark = lax.broadcasted_iota(jnp.int32, (16, 1), 0) == ids[i]

        def f(r, start):
            back = norm_back(r, 0, at(u1, start), start, 5, 6, gain_one[...].astype(F32)[None, :])
            g = mg[pl.ds(start, 64), :] + back
            at(qy, start)[...] = g.astype(BF)
            total = jnp.sum(g, axis=0, keepdims=True)
            sm[16:32, :] += jnp.where(mark, total, 0.0)

        blocks(i, f)
        fetch("mid%d" % i, ins["mid"].at[item_rows(i)], mg.at[item_rows(i)])
        if i == 2:
            fetch("wd", ins["w"].at[5], pool.at[0])
            fetch("hid", ins["hid"], slot(vy))
        cp = pltpu.make_async_copy(slot(qy, i), lat_out.at[item_rows(i)], osem.at[3 + i])
        cp.start()
        results.append(cp)

    arc, arp, arz, tot = (bufs[n] for n in ("arc", "arp", "arz", "tot"))
    pair = (p.i, 1 - p.c)
    me = p.i % 4
    mine = pl.ds(pl.multiple_of(me * 8, 8), 8)

    def others(count, self_at, f):
        for j in range(count):
            pl.when(self_at != j)(functools.partial(f, j))

    def copy(src, dst, dev, n, m):
        return pltpu.make_async_remote_copy(src, dst, tsem.at[n], tsem.at[m], device_id=dev, device_id_type=MESH)

    def local(ref, n):
        pltpu.make_async_copy(ref, ref, tsem.at[n]).wait()

    def total(n):
        half = sm.at[mine, s.cols]
        if n == 0:
            copy(sm.at[:, s.others], arc, pair, 0, 1).start()
        elif n == 1:
            local(arc, 1)
            sm[:, s.cols] += arc[...]
            others(4, me, lambda j: copy(sm.at[pl.ds(8 * j, 8), s.cols], arp.at[me], (p.i - me + j, p.c), 2, 4 + me).start())
            arp[me] = half[...]
        elif n == 2:
            others(4, me, lambda j: local(arp.at[j], 4 + j))
            arz[p.z] = arp[0] + arp[1] + arp[2] + arp[3]
            others(zs, p.z, lambda j: copy(arz.at[p.z], arz.at[p.z], (4 * j + me, p.c), 3, 8 + p.z).start())
        elif n == 3:
            others(zs, p.z, lambda j: local(arz.at[j], 8 + j))
            tot[mine, s.cols] = arz[0] + arz[1] + arz[2] + arz[3]
            part = tot.at[mine, s.cols]
            others(4, me, lambda j: copy(part, part, (p.i - me + j, p.c), 12, 16 + me).start())
        elif n == 4:
            others(4, me, lambda j: local(tot.at[pl.ds(8 * j, 8), s.cols], 16 + j))
            copy(tot.at[:, s.cols], tot.at[:, s.cols], pair, 13, 14).start()
        else:
            local(arc, 14)
            sm_out[...] = tot[...]
            local(arc, 0)
            three = pl.ds(0, 3)
            local(arp.at[three], 2)
            local(arp.at[three], 3)
            local(arp.at[three], 12)
            local(arc, 13)

    units = (unit_p, unit_n, unit_t, unit_y, unit_w(0), unit_w(1), unit_s, total)
    for code in ORDER_TWO:
        kind, k, t = code // 100, code // 10 % 10, code % 10
        if kind == 0:
            units[k](t)
        elif kind == 1:
            grad(k, t)
        elif kind == 2:
            s.c_arrive(k, t)
        elif kind == 3:
            s.b_arrive(k, t)
        elif kind == 4:
            s.a_arrive(k, t)
        elif kind == 5:
            s.z_step(k, True, t)
        elif kind == 6:
            s.z_step(k, False, t)
        elif kind == 7:
            s.z_end(k, True)
        elif kind == 8:
            s.z_end(k, False)
        else:
            s.finish(k)
    for k in range(2, 6):
        s.drain(k)
    for cp in results:
        cp.wait()


def backward(r, cotangent, ids, vectors, zs):
    rows, width = cotangent.shape
    DMA = pltpu.SemaphoreType.DMA
    n = 4 * zs
    grow = width // n
    half = width // 2
    ins = [r["w"].reshape(6, width, width)] + [r[k] for k in SAVED] + [r["mid"], r["inv"], r["probs"], cotangent]
    shapes = dict(
        pool=((6, width, width), BF), tall=((2, width, rows), BF), flat=((6 * rows, width), BF), mg=((rows, width), F32),
        probs=((24, LAT, LAT), BF), inv=((2, rows, 128), F32), yb=((LAT, width), F32), sm=((32, width), F32),
        rc=((3, width, half), BF), rb=((6, 2 * zs, grow, half), BF), rz=((6, zs + 1, 2 * PARTS[0][0][2] + PARTS[0][1][2], half), BF), ra=((6, zs, grow, half), BF),
        arc=((32, half), F32), arp=((4, 8, half), F32), arz=((zs, 8, half), F32), tot=((32, width), F32))
    ANY, VM = pl.BlockSpec(memory_space=pl.ANY), pl.BlockSpec(memory_space=pltpu.VMEM)
    return pl.pallas_call(
        functools.partial(backward_kernel, zs),
        out_shape=[jax.ShapeDtypeStruct((grow, half), F32)] * 6 + [jax.ShapeDtypeStruct((rows, width), BF)] * 2
        + [jax.ShapeDtypeStruct((32, width), F32)],
        in_specs=[pl.BlockSpec(memory_space=pltpu.SMEM)] + [VM] * 3 + [ANY] * len(ins),
        out_specs=[VM] * 6 + [ANY] * 2 + [VM],
        scratch_shapes=[pltpu.VMEM(*shapes[k]) for k in NAMES_TWO] + [
            DMA((6,)), DMA((6, zs)), DMA((6,)), DMA((6, zs)), DMA((6, 2, zs)), DMA((6, 2, zs + 1)), DMA((6, 2)), DMA((6, 2, zs)),
            pltpu.SemaphoreType.REGULAR, DMA((32,)), DMA((6,)), DMA((20,)),
        ],
        compiler_params=pltpu.CompilerParams(collective_id=1, has_side_effects=True, vmem_limit_bytes=63 << 20),
        name="backward_and_scatter",
    )(ids, *vectors, *ins)


def hand_out_kernel(*refs):
    res, lat, small, sems = refs[0], refs[1], refs[2], refs[-1]
    grads = refs[3:9]
    res_out, lat_out, table = refs[9:12]
    wide, narrow, grads_out = refs[12:18], refs[18:21], refs[21:27]
    copies = [pltpu.make_async_copy(a, b, sems.at[n]) for n, (a, b) in enumerate(zip((res, lat) + grads, (res_out, lat_out) + grads_out))]
    for cp in copies:
        cp.start()
    table[...] = small[16:32, :]
    for n, ref in enumerate(wide):
        ref[...] = small[3 + n:4 + n, :].reshape(ref.shape)
    half = narrow[0].shape[0]
    c = lax.axis_index("head")
    cols = pl.ds(pl.multiple_of(c * half, 128), half)
    for n, ref in enumerate(narrow):
        ref[...] = small[n:n + 1, cols].reshape(ref.shape)
    for cp in copies:
        cp.wait()


def hand_out(result, latents_grad, small, grads):
    width = result.shape[1]
    ANY, VM = pl.BlockSpec(memory_space=pl.ANY), pl.BlockSpec(memory_space=pltpu.VMEM)
    like = lambda a: jax.ShapeDtypeStruct(a.shape, a.dtype)
    return pl.pallas_call(
        hand_out_kernel,
        out_shape=[like(result), like(latents_grad), jax.ShapeDtypeStruct((16, width), F32)]
        + [jax.ShapeDtypeStruct((width,), F32)] * 6 + [jax.ShapeDtypeStruct((width // 2,), F32)] * 3 + [like(g) for g in grads],
        in_specs=[ANY, ANY, VM] + [ANY] * 6,
        out_specs=[ANY, ANY] + [VM] * 10 + [ANY] * 6,
        scratch_shapes=[pltpu.SemaphoreType.DMA((8,))],
        compiler_params=pltpu.CompilerParams(vmem_limit_bytes=63 << 20),
        name="hand_out",
    )(result, latents_grad, small, *grads)


def in_blocks(x, dim, length):
    before, after = (x.shape[:dim], x.shape[dim + 1 :])
    return jnp.moveaxis(x.reshape(*before, length, -1, *after), dim, 0)


def sent_and_summed(x, axis, dim):
    tiles = in_blocks(x, dim, lax.axis_size(axis))
    arrived = lax.all_to_all(tiles, axis, split_axis=0, concat_axis=0, tiled=True)
    return arrived.astype(jnp.float32).sum(axis=0)


def side_by_side(arrays, axis, dim, along):
    ends, at = ([], 0)
    for a in arrays[:-1]:
        at += a.shape[along]
        ends.append(at)
    both = jnp.concatenate(arrays, axis=along)
    return tuple(jnp.split(sent_and_summed(both, axis, dim), ends, axis=along))


def norm_forward(row_block, norm_gain, norm_shift):
    row_mean = jnp.mean(row_block, axis=1, keepdims=True)
    centered = row_block - row_mean
    row_var = jnp.mean(centered * centered, axis=1, keepdims=True)
    inverse = lax.rsqrt(row_var + EPSILON)
    normed = centered * inverse
    return (normed * norm_gain + norm_shift, normed, inverse)


def norm_backward(grad_rows, normed, inverse, norm_gain):
    scaled = grad_rows * norm_gain
    first_moment = jnp.mean(scaled, axis=1, keepdims=True)
    second_moment = jnp.mean(scaled * normed, axis=1, keepdims=True)
    grad_input = (scaled - first_moment - normed * second_moment) * inverse
    return (grad_input, jnp.sum(grad_rows * normed, axis=0), jnp.sum(grad_rows, axis=0))


def contract_rows(left, right):
    return lax.dot_general(
        left, right, (((0,), (0,)), ((), ())), preferred_element_type=jnp.float32
    )


def contract_cols(left, right):
    return lax.dot_general(
        left, right, (((1,), (1,)), ((), ())), preferred_element_type=jnp.float32
    )


def split_heads(matrix):
    item_count = matrix.shape[0] // LAT
    return matrix.reshape(item_count, LAT, matrix.shape[1] // HS, HS)


def attend_forward(query_rows, key_rows, value_rows):
    factor = HS ** (-0.5)
    scores = (
        jnp.einsum(
            "iqhc,ikhc->ihqk",
            split_heads(query_rows),
            split_heads(key_rows),
            preferred_element_type=jnp.float32,
        )
        * factor
    )
    row_max = jnp.max(scores, axis=-1, keepdims=True)
    exp_scores = jnp.exp(scores - row_max)
    row_total = jnp.sum(exp_scores, axis=-1, keepdims=True)
    soft_probs = (exp_scores / row_total).astype(jnp.bfloat16)
    attended = jnp.einsum(
        "ihqk,ikhc->iqhc", soft_probs, split_heads(value_rows), preferred_element_type=jnp.float32
    )
    return (attended.reshape(query_rows.shape).astype(jnp.bfloat16), row_max + jnp.log(row_total))


def attend_backward(query_rows, key_rows, value_rows, log_total, attended_grad):
    factor = HS ** (-0.5)
    query_heads = split_heads(query_rows)
    key_heads = split_heads(key_rows)
    value_heads = split_heads(value_rows)
    grad_heads = split_heads(attended_grad)
    scores = (
        jnp.einsum("iqhc,ikhc->ihqk", query_heads, key_heads, preferred_element_type=jnp.float32)
        * factor
    )
    soft_probs = jnp.exp(scores - log_total)
    value_grad = jnp.einsum(
        "ihqk,iqhc->ikhc",
        soft_probs.astype(jnp.bfloat16),
        grad_heads,
        preferred_element_type=jnp.float32,
    )
    probs_grad = jnp.einsum(
        "iqhc,ikhc->ihqk", grad_heads, value_heads, preferred_element_type=jnp.float32
    )
    inner_sum = jnp.sum(probs_grad * soft_probs, axis=-1, keepdims=True)
    score_grad = (soft_probs * (probs_grad - inner_sum)).astype(jnp.bfloat16)
    query_grad = (
        jnp.einsum("ihqk,ikhc->iqhc", score_grad, key_heads, preferred_element_type=jnp.float32)
        * factor
    )
    key_grad = (
        jnp.einsum("ihqk,iqhc->ikhc", score_grad, query_heads, preferred_element_type=jnp.float32)
        * factor
    )
    full_shape = query_rows.shape
    return (
        query_grad.reshape(full_shape).astype(jnp.bfloat16),
        key_grad.reshape(full_shape).astype(jnp.bfloat16),
        value_grad.reshape(full_shape).astype(jnp.bfloat16),
    )


def gelu_value(pre_act):
    return 0.5 * pre_act * (1.0 + lax.erf(pre_act * ROOT_HALF))


def gelu_slope(pre_act):
    return (
        0.5 * (1.0 + lax.erf(pre_act * ROOT_HALF))
        + pre_act * jnp.exp(-0.5 * pre_act * pre_act) * INV_ROOT_TWO_PI
    )


def place_slot(piece, head_index, full_len):
    empty = jnp.zeros((full_len,), jnp.float32)
    return lax.dynamic_update_slice_in_dim(empty, piece, head_index * piece.shape[0], 0)


def on_any_mesh(
    latents,
    lang_ids,
    lang_table,
    gain_one,
    shift_one,
    w_query,
    b_query,
    w_key,
    w_value,
    b_value,
    w_out,
    b_out,
    gain_two,
    shift_two,
    w_up,
    b_up,
    w_down,
    b_down,
    cotangent,
):
    own_rows = latents.shape[0]
    model_width = latents.shape[1]
    item_count = lang_ids.shape[0]
    head_index = lax.axis_index("head")
    head_count = lax.axis_size("head")
    w_query, w_key, w_value, w_up, w_out, w_down = (
        lax.all_gather(w_query, "dp", axis=0, tiled=True),
        lax.all_gather(w_key, "dp", axis=0, tiled=True),
        lax.all_gather(w_value, "dp", axis=0, tiled=True),
        lax.all_gather(w_up, "dp", axis=0, tiled=True),
        lax.all_gather(w_out, "dp", axis=1, tiled=True),
        lax.all_gather(w_down, "dp", axis=1, tiled=True),
    )
    one_hot = (lang_ids[:, None] == jnp.arange(LANGS, dtype=jnp.int32)[None, :]).astype(jnp.float32)
    embedded = jnp.dot(one_hot, lang_table, precision=HIGHEST)
    start_rows = (
        latents.astype(jnp.float32).reshape(item_count, LAT, model_width) + embedded[:, None, :]
    ).reshape(own_rows, model_width)
    gain_first = gain_one.astype(jnp.float32)
    gain_second = gain_two.astype(jnp.float32)
    normed_one, unit_one, inverse_one = norm_forward(
        start_rows, gain_first, shift_one.astype(jnp.float32)
    )
    input_one = normed_one.astype(jnp.bfloat16)
    group_one = lax.all_gather(input_one, "head", axis=0, tiled=True)
    query_rows = (
        jnp.dot(group_one, w_query, preferred_element_type=jnp.float32)
        + b_query.astype(jnp.float32)
    ).astype(jnp.bfloat16)
    key_rows = jnp.dot(group_one, w_key, preferred_element_type=jnp.float32).astype(jnp.bfloat16)
    value_rows = (
        jnp.dot(group_one, w_value, preferred_element_type=jnp.float32)
        + b_value.astype(jnp.float32)
    ).astype(jnp.bfloat16)
    attended, log_total = attend_forward(query_rows, key_rows, value_rows)
    attn_branch = lax.psum_scatter(
        jnp.dot(attended, w_out, preferred_element_type=jnp.float32),
        "head",
        scatter_dimension=0,
        tiled=True,
    )
    middle_rows = start_rows + (attn_branch + b_out.astype(jnp.float32))
    normed_two, unit_two, inverse_two = norm_forward(
        middle_rows, gain_second, shift_two.astype(jnp.float32)
    )
    input_two = normed_two.astype(jnp.bfloat16)
    group_two = lax.all_gather(input_two, "head", axis=0, tiled=True)
    pre_act = jnp.dot(group_two, w_up, preferred_element_type=jnp.float32) + b_up.astype(
        jnp.float32
    )
    hidden = gelu_value(pre_act).astype(jnp.bfloat16)
    down_branch = lax.psum_scatter(
        jnp.dot(hidden, w_down, preferred_element_type=jnp.float32).astype(jnp.bfloat16),
        "head",
        scatter_dimension=0,
        tiled=True,
    ).astype(jnp.float32)
    result = (middle_rows + (down_branch + b_down.astype(jnp.float32))).astype(jnp.bfloat16)
    group_cot = lax.all_gather(cotangent, "head", axis=0, tiled=True)
    grad_w_down = contract_rows(hidden, group_cot)
    grad_b_down = jnp.sum(cotangent.astype(jnp.float32), axis=0)
    pre_grad = (contract_cols(group_cot, w_down) * gelu_slope(pre_act)).astype(jnp.bfloat16)
    grad_w_up = contract_rows(group_two, pre_grad)
    grad_b_up = jnp.sum(pre_grad.astype(jnp.float32), axis=0)
    grad_two = lax.psum_scatter(
        contract_cols(pre_grad, w_up), "head", scatter_dimension=0, tiled=True
    )
    back_two, grad_gain_two, grad_shift_two = norm_backward(
        grad_two, unit_two, inverse_two, gain_second
    )
    middle_grad = cotangent.astype(jnp.float32) + back_two
    branch_grad = middle_grad.astype(jnp.bfloat16)
    grad_b_out = jnp.sum(branch_grad.astype(jnp.float32), axis=0)
    group_branch = lax.all_gather(branch_grad, "head", axis=0, tiled=True)
    grad_w_out = contract_rows(attended, group_branch)
    attended_grad = contract_cols(group_branch, w_out).astype(jnp.bfloat16)
    query_grad, key_grad, value_grad = attend_backward(
        query_rows, key_rows, value_rows, log_total, attended_grad
    )
    grad_w_query = contract_rows(group_one, query_grad)
    grad_w_key = contract_rows(group_one, key_grad)
    grad_w_value = contract_rows(group_one, value_grad)
    grad_b_query = jnp.sum(query_grad.astype(jnp.float32), axis=0)
    grad_b_value = jnp.sum(value_grad.astype(jnp.float32), axis=0)
    total_term = contract_cols(query_grad, w_query)
    total_term = total_term + contract_cols(key_grad, w_key)
    grad_one = lax.psum_scatter(
        (total_term + contract_cols(value_grad, w_value)).astype(jnp.bfloat16),
        "head",
        scatter_dimension=0,
        tiled=True,
    ).astype(jnp.float32)
    back_one, grad_gain_one, grad_shift_one = norm_backward(
        grad_one, unit_one, inverse_one, gain_first
    )
    start_grad = middle_grad + back_one
    latents_grad = start_grad.astype(jnp.bfloat16)
    item_sums = jnp.sum(start_grad.reshape(item_count, LAT, model_width), axis=1)
    grad_table = jnp.dot(one_hot.T, item_sums, precision=HIGHEST)
    full_b_query = place_slot(grad_b_query, head_index, model_width)
    full_b_value = place_slot(grad_b_value, head_index, model_width)
    full_b_up = place_slot(grad_b_up, head_index, FF)
    grad_w_query, grad_w_key, grad_w_value, grad_w_up, grad_w_out, grad_w_down = (
        *side_by_side(
            (
                grad_w_query.astype(jnp.bfloat16),
                grad_w_key.astype(jnp.bfloat16),
                grad_w_value.astype(jnp.bfloat16),
                grad_w_up.astype(jnp.bfloat16),
            ),
            "dp",
            0,
            1,
        ),
        *side_by_side(
            (grad_w_out.astype(jnp.bfloat16), grad_w_down.astype(jnp.bfloat16)), "dp", 1, 0
        ),
    )
    summed = lax.psum(
        (
            full_b_query,
            full_b_value,
            full_b_up,
            grad_b_out,
            grad_b_down,
            grad_gain_one,
            grad_shift_one,
            grad_gain_two,
            grad_shift_two,
            grad_table,
        ),
        ("dp", "head"),
    )
    local_width = model_width // head_count
    local_hidden = FF // head_count
    out_b_query = lax.dynamic_slice_in_dim(summed[0], head_index * local_width, local_width, 0)
    out_b_value = lax.dynamic_slice_in_dim(summed[1], head_index * local_width, local_width, 0)
    out_b_up = lax.dynamic_slice_in_dim(summed[2], head_index * local_hidden, local_hidden, 0)
    return (
        result,
        latents_grad,
        summed[9],
        summed[5],
        summed[6],
        grad_w_query,
        out_b_query,
        grad_w_key,
        grad_w_value,
        out_b_value,
        grad_w_out,
        summed[3],
        summed[7],
        summed[8],
        grad_w_up,
        out_b_up,
        grad_w_down,
        summed[4],
    )


def on_device(
    latents, lang_ids, lang_table, gain_one, shift_one, w_query, b_query, w_key, w_value, b_value, w_out, b_out,
    gain_two, shift_two, w_up, b_up, w_down, b_down, cotangent,
):
    zs = lax.axis_size("dp") // 4
    r = forward(
        latents, cotangent, lang_ids, lang_table, (gain_one, shift_one, gain_two, shift_two, b_out, b_query, b_value, b_up),
        (w_query, w_key, w_value, w_out.T, w_up, w_down.T), zs)
    *grads, result, latents_grad, small = backward(r, cotangent, lang_ids, (gain_one, gain_two, b_down), zs)
    got = hand_out(result, latents_grad, small, grads)
    result, latents_grad, table = got[:3]
    b_out_g, b_down_g, gain_one_g, shift_one_g, gain_two_g, shift_two_g = got[3:9]
    b_query_g, b_value_g, b_up_g = got[9:12]
    down, up, out, value, key, query = got[12:]
    return (
        result, latents_grad, table, gain_one_g, shift_one_g, query, b_query_g, key, value, b_value_g, out.T, b_out_g,
        gain_two_g, shift_two_g, up, b_up_g, down.T, b_down_g,
    )

def solution(mesh):
    in_specs = (
        P(("dp", "head"), None),
        P(("dp", "head")),
        P(),
        P(),
        P(),
        P("dp", "head"),
        P("head"),
        P("dp", "head"),
        P("dp", "head"),
        P("head"),
        P("head", "dp"),
        P(),
        P(),
        P(),
        P("dp", "head"),
        P("head"),
        P("head", "dp"),
        P(),
        P(("dp", "head"), None),
    )
    out_specs = (
        P(("dp", "head"), None),
        P(("dp", "head"), None),
        P(),
        P(),
        P(),
        P("dp", "head"),
        P("head"),
        P("dp", "head"),
        P("dp", "head"),
        P("head"),
        P("head", "dp"),
        P(),
        P(),
        P(),
        P("dp", "head"),
        P("head"),
        P("head", "dp"),
        P(),
    )
    fast = mesh.shape["dp"] == 16 and mesh.shape["head"] == 2
    return jax.shard_map(
        on_device if fast else on_any_mesh, mesh=mesh, in_specs=in_specs, out_specs=out_specs, check_vma=False
    )
```

```python
import functools
import jax
import jax.numpy as jnp
from jax import lax
from jax.experimental import pallas as pl
from jax.experimental.pallas import tpu as pltpu
from jax.sharding import PartitionSpec as P

MESH = pl.DeviceIdType.MESH
BF = jnp.bfloat16
F32 = jnp.float32
HS = 160
LAT = 256
LANGS = 16
EPSILON = 1e-05
HIGHEST = lax.Precision.HIGHEST
ROOT_HALF = 0.7071067811865476
INV_ROOT_TWO_PI = 0.3989422804014327
FF = 1280


class Place:
    def __init__(self, zs):
        self.zs = zs
        i = lax.axis_index("dp")
        c = lax.axis_index("head")
        self.i, self.c = i, c
        self.z = i // 4
        self.sa = 1 + c
        self.sb = 2 - c
        x = i % 2
        y = (i // 2) % 2
        self.a = jnp.where(c == 0, x, y)
        self.b = jnp.where(c == 0, y, x)
        self.ia = i + self.sa * (1 - 2 * self.a)
        self.ib = i + self.sb * (1 - 2 * self.b)
        self.up = jnp.minimum(i + 4, 4 * zs - 1)
        self.down = jnp.maximum(i - 4, 0)
        self.has_up = self.z < zs - 1
        self.has_down = self.z > 0

    def barrier(self):
        bar = pltpu.get_barrier_semaphore()
        i, c = self.i, self.c
        for dev in ((self.ia, c), (self.ib, c), (i, 1 - c)):
            pl.semaphore_signal(bar, inc=1, device_id=dev, device_id_type=MESH)

        @pl.when(self.has_up)
        def _():
            pl.semaphore_signal(bar, inc=1, device_id=(self.up, c), device_id_type=MESH)

        @pl.when(self.has_down)
        def _():
            pl.semaphore_signal(bar, inc=1, device_id=(self.down, c), device_id_type=MESH)

        n = 3 + jnp.where(self.has_up, 1, 0) + jnp.where(self.has_down, 1, 0)
        pl.semaphore_wait(bar, n)

    def barrier_wide(self):
        bar = pltpu.get_barrier_semaphore()
        me = self.i % 4
        pl.semaphore_signal(bar, inc=1, device_id=(self.i, 1 - self.c), device_id_type=MESH)
        for j in range(4):
            @pl.when(me != j)
            def _(j=j):
                pl.semaphore_signal(bar, inc=1, device_id=(self.i - me + j, self.c), device_id_type=MESH)
        for zz in range(self.zs):
            @pl.when(self.z != zz)
            def _(zz=zz):
                pl.semaphore_signal(bar, inc=1, device_id=(4 * zz + me, self.c), device_id_type=MESH)
        pl.semaphore_wait(bar, 3 + self.zs)


ORDER_ONE = (
    0, 20, -1, -2, 2, 27, 22, -3, 10, 23, 7, 30, 28, 40, 60, 8, 29, 31, 24, 11,
    67, 9, 42, 12, 62, 68, 32, 25, 80, 100, 50, 63, 69, 70, 47, 13, 64, 33, 1, 21,
    107, 48, -4, 71, 65, -5, 51, 82, 102, 49, -6, 120, 140, 108, 72, 52, 109, 90, 103, 87,
    73, 110, 53, 147, 61, 104, 122, 41, 142, 160, 180, -7, 88, 105, -8, 148, 111, 91, -9, 89,
    149, 143, 112, 127, 130, 187, 92, 150, 200, 220, 113, 162, 182, 128, 93, 144, 101, 188, 145, 81,
    -10, 129, -11, 151, 189, 131, 183, -12, -13, -14, 167, -15, -16, 170, 227, 152, 202, 132, 222, -19,
    184, 190, 153, -17, 168, 133, 228, -20, 141, -18, 185, 121, -21, -22, 169, 229, 191, 171, 223, -23,
    207, 172, 192, 224, 193, 210, -24, 230, 225, 208, 173, 181, 209, 161, -25, 211, 231, -26, 232, 233,
    212, 213, -27, 221, 201,
)
ORDER_TWO = (
    100, 101, 200, 102, 201, 103, 202, 0, 203, 300, 503, 1, 301, 2, 110, 302, 502, 111, 112, 210,
    303, 400, 603, 401, 402, 211, 501, 113, 20, 212, 310, 513, 602, 403, 213, 700, 21, 311, 601, 512,
    312, 800, 410, 613, 22, 511, 313, 900, 411, 412, 120, 121, 413, 612, 122, 710, 123, 611, 220, 30,
    910, 31, 810, 221, 32, 320, 222, 523, 40, 223, 50, 321, 420, 623, 41, 522, 322, 51, 323, 42,
    521, 421, 622, 422, 423, 52, 130, 131, 720, 621, 132, 133, 920, 820, 140, 141, 142, 143, 150, 151,
    230, 152, 153, 231, 60, 330, 533, 232, 331, 430, 633, 233, 61, 532, 332, 431, 240, 333, 531, 632,
    432, 241, 340, 543, 242, 433, 62, 631, 730, 341, 243, 440, 830, 643, 542, 250, 342, 930, 441, 251,
    541, 642, 343, 10, 11, 252, 442, 350, 553, 641, 70, 740, 253, 12, 351, 443, 71, 840, 552, 72,
    352, 450, 940, 653, 73, 551, 353, 451, 452, 74, 453, 652, 750, 75, 651, 950, 850,
)
PARTS = (((True, 0, 48), (False, 48, 32)),) * 6


def nn(a, b):
    return lax.dot_general(a, b, (((1,), (0,)), ((), ())), preferred_element_type=F32)


def nt(a, b):
    return lax.dot_general(a, b, (((1,), (1,)), ((), ())), preferred_element_type=F32)


def tn(a, b):
    return lax.dot_general(a, b, (((0,), (0,)), ((), ())), preferred_element_type=F32)


def item_rows(i):
    return pl.ds(i * LAT, LAT)


def head_window(hh):
    at = lax.broadcasted_iota(jnp.int32, (1, 256), 1) + hh * 128
    return (at >= hh * HS) & (at < (hh + 1) * HS)


class Gather:
    def __init__(self, p, w, sems, streams):
        self.p, self.w, self.streams = p, w, streams
        self.zsend, self.zrecv, self.asend, self.arecv, self.bsend, self.brecv, self.csend, self.crecv = sems
        self.cols = pl.ds(pl.multiple_of(p.c * 640, 128), 640)

    def sub(self, s, j, n=None):
        k, mid, r0, rows = self.streams[s]
        return self.w.at[k, j if n is None else pl.ds(j, n), pl.ds(r0, rows), self.cols]

    def mid(self, s):
        return self.streams[s][1]

    def send(self, s, j, n, dev, ssem, rsem):
        ref = self.sub(s, j) if n == 1 else self.sub(s, j, n)
        pltpu.make_async_remote_copy(ref, ref, ssem, rsem, device_id=dev, device_id_type=MESH).start()

    def arrived(self, s, n, sem):
        ref = self.sub(s, 0, n)
        pltpu.make_async_copy(ref, ref, sem).wait()

    def members(self, s, zz):
        p = self.p
        base = zz * 4 + p.b * p.sb
        return (base, base + p.sa) if self.mid(s) else (base + p.a * p.sa,)

    def z_send(self, s, zz, upward):
        p = self.p
        dev, d = ((p.up, p.c), 0) if upward else ((p.down, p.c), 1)
        for j in self.members(s, zz):
            self.send(s, j, 1, dev, self.zsend.at[s, d, zz], self.zrecv.at[s, zz])

    def z_first(self, s):
        p = self.p
        pl.when(p.has_up)(lambda: self.z_send(s, p.z, True))
        pl.when(p.has_down)(lambda: self.z_send(s, p.z, False))

    def at_distance(self, d, f):
        p = self.p
        pl.when(p.z - d >= 0)(lambda: f(p.z - d, True))
        pl.when(p.z + d <= p.zs - 1)(lambda: f(p.z + d, False))

    def around(self, d, f):
        if d == 0:
            f(self.p.z)
        else:
            self.at_distance(d, lambda zz, below: f(zz))

    def z_arrive(self, s, d, then):
        p = self.p
        n = len(self.members(s, 0))

        def f(zz, below):
            self.arrived(s, n, self.zrecv.at[s, zz])
            if d < p.zs - 1:
                if below:
                    pl.when(p.has_up)(lambda: self.z_send(s, zz, True))
                else:
                    pl.when(p.has_down)(lambda: self.z_send(s, zz, False))
            then(s, zz)

        self.at_distance(d, f)

    def a_send(self, s, zz):
        p = self.p
        j = zz * 4 + p.b * p.sb + p.a * p.sa
        self.send(s, j, 1, (p.ia, p.c), self.asend.at[s], self.arecv.at[s, zz])

    def a_arrive(self, s, zz, then):
        self.arrived(s, 1, self.arecv.at[s, zz])
        then(s, zz)

    def b_send(self, s, zz):
        p = self.p
        base = zz * 4 + p.b * p.sb
        for j in (base, base + p.sa):
            self.send(s, j, 1, (p.ib, p.c), self.bsend.at[s], self.brecv.at[s, zz])

    def b_arrive(self, s, zz):
        p = self.p
        self.arrived(s, 2, self.brecv.at[s, zz])
        self.send(s, zz * 4, 4, (p.i, 1 - p.c), self.csend.at[s], self.crecv.at[s])

    def do(self, s, ev):
        p = self.p
        if ev == 0:
            if not self.mid(s):
                self.z_first(s)
            self.a_send(s, p.z)
        elif ev == 1:
            self.arrived(s, 4 * p.zs, self.crecv.at[s])
        elif ev >= 10:
            self.around(ev - 10, lambda zz: self.b_arrive(s, zz))
        elif ev >= 6:
            self.z_arrive(s, ev - 6, self.b_send if self.mid(s) else self.a_send)
        elif self.mid(s):
            self.arrived(s, 1, self.arecv.at[s, p.z])
            self.z_first(s)
            self.b_send(s, p.z)
        else:
            self.around(ev - 2, lambda zz: self.a_arrive(s, zz, self.b_send))

    def drain(self, s):
        p = self.p
        n = len(self.members(s, 0))
        for zz in range(p.zs):
            @pl.when(jnp.logical_and(p.has_up, zz <= p.z))
            def _(zz=zz):
                self.arrived(s, n, self.zsend.at[s, 0, zz])

            @pl.when(jnp.logical_and(p.has_down, zz >= p.z))
            def _(zz=zz):
                self.arrived(s, n, self.zsend.at[s, 1, zz])
        self.arrived(s, 1 if self.mid(s) else p.zs, self.asend.at[s])
        self.arrived(s, 2 * p.zs, self.bsend.at[s])
        self.arrived(s, 4 * p.zs, self.csend.at[s])


STREAMS = tuple((k, m, r0, r) for k in range(6) for m, r0, r in ((True, 0, 48), (False, 48, 32)))
SAVED = ("one_t", "q", "k", "v", "att", "hid", "slope", "two_t", "cot_t", "u1", "u2")
TALL = ("one_t", "two_t", "cot_t")


def forward_kernel(zs, *refs):
    lat_in, cot_in, ids, table = refs[:4]
    vectors, shards = refs[4:12], refs[12:18]
    at = 18
    outs = dict(zip(("w",) + SAVED + ("mid", "inv", "probs"), refs[at:at + 15]))
    at += 15
    bufs = dict(zip(("w",) + SAVED + ("mid", "inv", "probs", "lat", "cot", "one", "two", "hb", "fulls"), refs[at:at + 21]))
    at += 21
    gsems = refs[at:at + 8]
    own, load, save, hsem = refs[at + 8:at + 12]
    p = Place(zs)
    w = bufs["w"]
    g = Gather(p, w, gsems, STREAMS)
    hb = bufs["hb"]
    copies = [pltpu.make_async_copy(shards[k], w.at[k, p.i, :, g.cols], own.at[k]) for k in range(6)]
    for cp in copies:
        cp.start()
    loads = [pltpu.make_async_copy(src.at[item_rows(i)], bufs[n].at[item_rows(i)], load.at[j, i])
             for j, (src, n) in enumerate(((lat_in, "lat"), (cot_in, "cot"))) for i in range(3)]
    for cp in loads:
        cp.start()
    fulls = bufs["fulls"]
    for n in range(5):
        fulls[n:n + 1, :] = vectors[n][...].astype(F32)[None, :]
    for n in range(3):
        hb[n:n + 1, g.cols] = vectors[5 + n][...].astype(F32)[None, :]
    p.barrier()
    half_send = pltpu.make_async_remote_copy(hb.at[:, g.cols], hb.at[:, g.cols], hsem.at[0], hsem.at[1],
                                             device_id=(p.i, 1 - p.c), device_id_type=MESH)
    half_send.start()
    names = ("w",) + SAVED + ("mid", "inv", "probs")
    saves = []

    def keep(name, index=None):
        src, dst = bufs[name], outs[name]
        if index is not None:
            src, dst = src.at[index], dst.at[index]
        n = len(saves)
        assert n < save.shape[0]
        cp = pltpu.make_async_copy(src, dst, save.at[n])
        cp.start()
        saves.append(cp)

    def start_of(i):
        return bufs["lat"][item_rows(i)].astype(F32) + table[pl.ds(ids[i], 1), :]

    def norm(v):
        mean = jnp.mean(v, axis=1, keepdims=True)
        cen = v - mean
        inv = lax.rsqrt(jnp.mean(cen * cen, axis=1, keepdims=True) + EPSILON)
        return cen * inv, inv

    def norm_rows(i, n, rows_of, u_name, out_name, tall_name):
        gain, shift = fulls[2 * n:2 * n + 1, :], fulls[2 * n + 1:2 * n + 2, :]

        def body(r, carry):
            rows = pl.ds(pl.multiple_of(i * LAT + r * 64, 64), 64)
            unit, inv = norm(rows_of(rows))
            bufs[u_name][rows, :] = unit.astype(BF)
            bufs[out_name][rows, :] = (unit * gain + shift).astype(BF)
            bufs["inv"][n, rows, :] = jnp.broadcast_to(inv, (64, 128))
            return carry

        lax.fori_loop(0, 4, body, 0)
        bufs[tall_name][:, item_rows(i)] = bufs[out_name][item_rows(i), :].T

    def whole(k):
        return w[k].reshape(1280, 1280)

    def ln1(i):
        loads[i].wait()
        emb = table[pl.ds(ids[i], 1), :]
        norm_rows(i, 0, lambda rows: bufs["lat"][rows, :].astype(F32) + emb, "u1", "one", "one_t")

    def project(name, k, bias):
        def f(i):
            y = nn(bufs["one"][item_rows(i), :], whole(k))
            if bias is not None:
                y = y + hb[bias:bias + 1, :]
            bufs[name][item_rows(i), :] = y.astype(BF)
        return f

    def cot(i):
        loads[3 + i].wait()
        bufs["cot_t"][:, item_rows(i)] = bufs["cot"][item_rows(i), :].T

    def attend(half):
        def f(i):
            rows = item_rows(i)
            zero = jnp.zeros((), BF)
            acc = [None] * 5
            for hh in range(4):
                lanes = pl.ds(half * 640 + hh * 128, 256)
                mask = head_window(hh)
                qm = jnp.where(mask, bufs["q"][rows, lanes], zero)
                s = nt(qm, bufs["k"][rows, lanes]) * (HS ** -0.5)
                e = jnp.exp(s - jnp.max(s, axis=1, keepdims=True))
                pr = (e / jnp.sum(e, axis=1, keepdims=True)).astype(BF)
                bufs["probs"][i * 8 + half * 4 + hh] = pr
                vm = jnp.where(mask, bufs["v"][rows, lanes], zero)
                a = nn(pr, vm)
                for t in (0, 1):
                    piece = a[:, t * 128:(t + 1) * 128]
                    acc[hh + t] = piece if acc[hh + t] is None else acc[hh + t] + piece
            for t in range(5):
                bufs["att"][rows, pl.ds(half * 640 + t * 128, 128)] = acc[t].astype(BF)
        return f

    def out(i):
        rows = item_rows(i)
        emb = table[pl.ds(ids[i], 1), :]
        y = nt(bufs["att"][rows, :], whole(3))
        bufs["mid"][rows, :] = y + fulls[4:5, :] + (bufs["lat"][rows, :].astype(F32) + emb)
        norm_rows(i, 1, lambda r: bufs["mid"][r, :], "u2", "two", "two_t")

    def up(i):
        rows = item_rows(i)
        pre = nn(bufs["two"][rows, :], whole(4)) + hb[2:3, :]
        cdf = 0.5 * (1.0 + lax.erf(pre * ROOT_HALF))
        bufs["hid"][rows, :] = (pre * cdf).astype(BF)
        bufs["slope"][rows, :] = (cdf + pre * jnp.exp(-0.5 * pre * pre) * INV_ROOT_TWO_PI).astype(BF)

    units = (ln1, project("q", 0, 0), project("k", 1, None), project("v", 2, 1), cot, attend(0), attend(1), out, up)
    after = (("u1", "one_t"), ("q",), ("k",), ("v",), ("cot_t",), (), ("att", "probs"), ("u2", "two_t", "mid", "inv"), ("hid", "slope"))
    seen, full = set(), {}
    for code in ORDER_ONE:
        if code < 0:
            n, i = (-code - 1) // 3, (-code - 1) % 3
            if n == 1 and i == 0:
                half_send.wait_recv()
            units[n](i)
            if i == 2:
                for name in after[n]:
                    keep(name)
            continue
        s, ev = code // 20, code % 20
        k = STREAMS[s][0]
        if k not in seen:
            copies[k].wait()
            seen.add(k)
        g.do(s, ev)
        if ev == 1:
            full[k] = full.get(k, 0) + 1
            if full[k] == 2:
                keep("w", k)
    half_send.wait_send()
    for s in range(len(STREAMS)):
        g.drain(s)
    for cp in saves:
        cp.wait()


def forward(latents, cotangent, ids, table, vectors, shards, zs):
    n = 4 * zs
    rows, width = latents.shape
    s = len(STREAMS)
    DMA = pltpu.SemaphoreType.DMA
    shape = {k: ((width, rows) if k in TALL else (rows, width), BF) for k in SAVED}
    shape["w"] = ((6, n, shards[0].shape[0], width), BF)
    shape["mid"] = ((rows, width), F32)
    shape["inv"] = ((2, rows, 128), F32)
    shape["probs"] = ((24, LAT, LAT), BF)
    for k in ("lat", "cot", "one", "two"):
        shape[k] = ((rows, width), BF)
    shape["hb"] = shape["fulls"] = ((8, width), F32)
    names = ("w",) + SAVED + ("mid", "inv", "probs")
    got = pl.pallas_call(
        functools.partial(forward_kernel, zs),
        out_shape=[jax.ShapeDtypeStruct(*shape[k]) for k in names],
        in_specs=[pl.BlockSpec(memory_space=pl.ANY)] * 2 + [pl.BlockSpec(memory_space=pltpu.SMEM)]
        + [pl.BlockSpec(memory_space=pltpu.VMEM)] * 9 + [pl.BlockSpec(memory_space=pl.ANY)] * 6,
        out_specs=[pl.BlockSpec(memory_space=pl.ANY)] * len(names),
        scratch_shapes=[pltpu.VMEM(*shape[k]) for k in names + ("lat", "cot", "one", "two", "hb", "fulls")] + [
            DMA((s, 2, zs)), DMA((s, zs)), DMA((s,)), DMA((s, zs)), DMA((s,)), DMA((s, zs)), DMA((s,)), DMA((s,)),
            DMA((6,)), DMA((2, 3)), DMA((24,)), DMA((2,)),
        ],
        compiler_params=pltpu.CompilerParams(collective_id=0, has_side_effects=True, vmem_limit_bytes=62 << 20),
        name="gather_and_forward",
    )(latents, cotangent, ids, table, *vectors, *shards)
    return dict(zip(names, got))


NAMES_TWO = ("pool", "tall", "flat", "mg", "probs", "inv", "yb", "sm", "rc", "rb", "rz", "ra", "arc", "arp", "arz", "tot")


class Scatter:
    def __init__(self, p, g, bufs, outs, sems, parts):
        self.p, self.g, self.parts, self.outs = p, g, parts, outs
        self.rc, self.rb, self.rz, self.ra = (bufs[n] for n in ("rc", "rb", "rz", "ra"))
        (self.csend, self.crecv, self.bsend, self.brecv, self.zsend, self.zrecv, self.asend, self.arecv, self.credit) = sems
        self.cols = pl.ds(pl.multiple_of(p.c * 640, 128), 640)
        self.others = pl.ds(pl.multiple_of((1 - p.c) * 640, 128), 640)

    def plane(self, t):
        val = jnp.int32(FAR[0][t])
        for s in range(1, self.p.zs):
            val = jnp.where(self.p.z == s, FAR[s][t], val)
        return val

    def rows(self, j, r0, n):
        return pl.ds(pl.multiple_of(j * 80 + r0, 16), n)

    def own(self, k, j, r0, n):
        return self.g(k).at[self.rows(j, r0, n), self.cols]

    def move(self, src, dst, dev, ssem, rsem):
        pltpu.make_async_remote_copy(src, dst, ssem, rsem, device_id=dev, device_id_type=MESH).start()

    def wait(self, ref, sem):
        pltpu.make_async_copy(ref, ref, sem).wait()

    def add(self, ref, val):
        ref[...] = ref[...] + val

    def group(self, t):
        return pl.ds(pl.multiple_of(self.plane(t) * 320, 320), 320)

    def c_send(self, k, t):
        p = self.p
        if k >= 3 and t == 0:
            pl.semaphore_wait(self.credit, 1)
        rows = self.group(t)
        self.move(self.g(k).at[rows, self.others], self.rc.at[k % 3, rows], (p.i, 1 - p.c), self.csend.at[k], self.crecv.at[k, self.plane(t)])

    def c_arrive(self, k, t):
        p = self.p
        zz = self.plane(t)
        rows = self.group(t)
        src = self.rc.at[k % 3, rows]
        self.wait(src, self.crecv.at[k, zz])
        self.add(self.g(k).at[rows, self.cols], src[...])
        if k < 3 and t == 3:
            pl.semaphore_signal(self.credit, inc=1, device_id=(p.i, 1 - p.c), device_id_type=MESH)
        away = zz * 4 + (1 - p.b) * p.sb
        for n, j in enumerate((away, away + p.sa)):
            self.move(self.own(k, j, 0, 80), self.rb.at[k, zz * 2 + n], (p.ib, p.c), self.bsend.at[k], self.brecv.at[k, zz])

    def b_arrive(self, k, t):
        p = self.p
        zz = self.plane(t)
        self.wait(self.rb.at[k, pl.ds(zz * 2, 2)], self.brecv.at[k, zz])
        base = zz * 4 + p.b * p.sb
        for n, j in enumerate((base, base + p.sa)):
            self.add(self.own(k, j, 0, 80), self.rb[k, zz * 2 + n])
        for mid, r0, n in self.parts[k]:
            if not mid:
                self.move(self.own(k, base + (1 - p.a) * p.sa, r0, n), self.ra.at[k, zz, pl.ds(r0, n)], (p.ia, p.c),
                          self.asend.at[k, 0], self.arecv.at[k, 0, zz])

    def part(self, k, mid):
        for m, r0, n in self.parts[k]:
            if m == mid:
                return r0, n
        return None

    def a_arrive(self, k, t):
        p = self.p
        if self.part(k, False) is None:
            return
        r0, n = self.part(k, False)
        zz = self.plane(t)
        src = self.ra.at[k, zz, pl.ds(r0, n)]
        self.wait(src, self.arecv.at[k, 0, zz])
        self.add(self.own(k, zz * 4 + p.b * p.sb + p.a * p.sa, r0, n), src[...])

    def members(self, mid, zz):
        p = self.p
        base = zz * 4 + p.b * p.sb
        return (base, base + p.sa) if mid else (base + p.a * p.sa,)

    def slot(self, zz, up, end):
        return zz if up or not end else self.p.zs

    def landing(self, k, mid, zz, up, end):
        r0, n = self.part(k, mid)
        return self.rz.at[k, self.slot(zz, up, end), pl.ds(0 if mid else 2 * r0, 2 * n if mid else n)]

    def z_take(self, k, mid, zz, up, end):
        m = 0 if mid else 1
        r0, n = self.part(k, mid)
        src = self.landing(k, mid, zz, up, end)
        self.wait(src, self.zrecv.at[k, m, self.slot(zz, up, end)])
        for q, j in enumerate(self.members(mid, zz)):
            self.add(self.own(k, j, r0, n), src[q * n:(q + 1) * n])

    def z_pass(self, k, mid, zz, up, end):
        p = self.p
        m = 0 if mid else 1
        r0, n = self.part(k, mid)
        at = self.slot(zz, up, end)
        dev = (p.up if up else p.down, p.c)
        for q, j in enumerate(self.members(mid, zz)):
            self.move(self.own(k, j, r0, n), self.rz.at[k, at, pl.ds(q * n if mid else 2 * r0, n)], dev, self.zsend.at[k, m, zz], self.zrecv.at[k, m, at])

    def z_step(self, k, mid, d):
        p = self.p
        if self.part(k, mid) is None:
            return

        @pl.when(p.z + d <= p.zs - 1)
        def _():
            if d < p.zs - 1:
                pl.when(p.has_down)(lambda: self.z_take(k, mid, p.z + d, True, False))
            self.z_pass(k, mid, p.z + d, True, d == 1)

        @pl.when(p.z - d >= 0)
        def _():
            if d < p.zs - 1:
                pl.when(p.has_up)(lambda: self.z_take(k, mid, p.z - d, False, False))
            self.z_pass(k, mid, p.z - d, False, d == 1)

    def z_end(self, k, mid):
        p = self.p
        if self.part(k, mid) is None:
            return
        r0, n = self.part(k, mid)
        pl.when(p.has_down)(lambda: self.z_take(k, mid, p.z, True, True))
        pl.when(p.has_up)(lambda: self.z_take(k, mid, p.z, False, True))
        if mid:
            base = p.z * 4 + p.b * p.sb
            self.move(self.own(k, base + (1 - p.a) * p.sa, r0, n), self.ra.at[k, 0, pl.ds(r0, n)], (p.ia, p.c),
                      self.asend.at[k, 1], self.arecv.at[k, 1, 0])
        else:
            self.outs[k][r0:r0 + n, :] = self.own(k, p.i, r0, n)[...].astype(F32)

    def finish(self, k):
        if self.part(k, True) is None:
            return
        r0, n = self.part(k, True)
        src = self.ra.at[k, 0, pl.ds(r0, n)]
        self.wait(src, self.arecv.at[k, 1, 0])
        self.outs[k][r0:r0 + n, :] = self.own(k, self.p.i, r0, n)[...].astype(F32) + src[...].astype(F32)

    def drain(self, k):
        p = self.p
        zs = p.zs
        self.wait(self.rc.at[k % 3], self.csend.at[k])
        self.wait(self.rb.at[k], self.bsend.at[k])
        for m, mid in enumerate((True, False)):
            if self.part(k, mid) is None:
                continue
            r0, n = self.part(k, mid)
            if mid:
                self.wait(self.ra.at[k, 0, pl.ds(r0, n)], self.asend.at[k, 1])
            else:
                self.wait(self.ra.at[k, :, pl.ds(r0, n)], self.asend.at[k, 0])
            for zz in range(zs):
                @pl.when(p.z != zz)
                def _(zz=zz, mid=mid, m=m):
                    self.wait(self.landing(k, mid, zz, True, False), self.zsend.at[k, m, zz])


FAR = ((3, 2, 1, 0), (3, 0, 2, 1), (0, 3, 1, 2), (0, 1, 2, 3))
GRADS = ("down", "up", "out", "value", "key", "query")


def backward_kernel(zs, *refs):
    ids, gain_one, gain_two, b_down = refs[:4]
    ins = dict(zip(("w",) + SAVED + ("mid", "inv", "probs", "cot"), refs[4:20]))
    outs = refs[20:26]
    res_out, lat_out, sm_out = refs[26:29]
    bufs = dict(zip(NAMES_TWO, refs[29:45]))
    rsems = refs[45:54]
    lsem, osem, tsem = refs[54:57]
    p = Place(zs)
    pool, tall, flat, mg, probs, inv, yb, sm = (bufs[n] for n in NAMES_TWO[:8])
    tokens = 768
    seat = (2, 3, 4, 5, 2, 3)
    s = Scatter(p, lambda k: pool.at[seat[k]], bufs, outs, rsems, PARTS)
    count = [0]

    def load(src, dst):
        assert count[0] < lsem.shape[0]
        cp = pltpu.make_async_copy(src, dst, lsem.at[count[0]])
        count[0] += 1
        cp.start()
        return cp

    def slot(n, i=None):
        return flat.at[pl.ds(n * tokens, tokens)] if i is None else flat.at[pl.ds(n * tokens + i * LAT, LAT)]

    hid, pre, cot, u2, att, ky = range(6)
    ag, bg, qy, vy, u1 = hid, pre, cot, u2, att
    ready = {}

    def fetch(name, src, dst):
        ready[name] = load(src, dst)

    def need(name):
        cp = ready.pop(name, None)
        if cp is not None:
            cp.wait()

    fetch("hid", ins["hid"], slot(hid))
    fetch("cot_t", ins["cot_t"], tall.at[0])
    fetch("wd", ins["w"].at[5], pool.at[0])
    fetch("cot", ins["cot"], slot(cot))
    fetch("pre", ins["slope"], slot(pre))
    fetch("two_t", ins["two_t"], tall.at[1])
    fetch("wu", ins["w"].at[4], pool.at[1])
    fetch("u2", ins["u2"], slot(u2))
    fetch("inv", ins["inv"], inv)
    fetch("att", ins["att"], slot(att))
    fetch("ky", ins["k"], slot(ky))
    fetch("probs", ins["probs"], probs)
    sm[...] = jnp.zeros(sm.shape, F32)
    p.barrier_wide()
    results = []

    def col_sum(row, val):
        sm[row:row + 1, :] += jnp.sum(val, axis=0, keepdims=True)

    def blocks(i, f):
        def body(r, carry):
            f(pl.ds(pl.multiple_of(r * 64, 64), 64), pl.multiple_of(i * LAT + r * 64, 64))
            return carry
        lax.fori_loop(0, 4, body, 0)

    def at(n, start, size=64):
        return flat.at[pl.ds(n * tokens + start, size)]

    left = {"g0": (0, hid), "g1": (1, pre), "g2": (0, att), "g3": (1, vy), "g4": (1, ky), "g5": (1, qy)}
    before = (("hid", "cot_t"), ("two_t",), ("att",), ("one_t",), (), ())

    def grad(k, t):
        if t == 0:
            for n in before[k]:
                need(n)
            if k >= 4:
                s.drain(k - 4)
        a, b = left["g%d" % k]
        rows = s.group(t)
        pool[seat[k], rows, :] = nn(tall[a, rows, :], slot(b)[...]).astype(BF)
        s.c_send(k, t)

    def unit_p(i):
        for n in ("wd", "cot", "pre"):
            need(n)
        yb[...] = nn(slot(cot, i)[...], pool[0])

        def f(r, start):
            ref = at(pre, start)
            v = (yb[r, :] * ref[...].astype(F32)).astype(BF)
            ref[...] = v
            col_sum(2, v.astype(F32))
            col_sum(4, at(cot, start)[...].astype(F32))

        blocks(i, f)

    def unit_n(i):
        for n in ("wd", "hid", "mid%d" % i):
            need(n)
        yb[...] = nt(slot(vy, i)[...], pool[0])

        def f(r, start):
            at(vy, start)[...] = (mg[pl.ds(start, 64), :] + (yb[r, :] + b_down[...].astype(F32)[None, :])).astype(BF)

        blocks(i, f)
        cp = pltpu.make_async_copy(slot(vy, i), res_out.at[item_rows(i)], osem.at[i])
        cp.start()
        results.append(cp)

    def norm_back(r, n, unit, start, gain_row, shift_row, gain):
        y = yb[r, :]
        v = unit[...].astype(F32)
        sc = y * gain
        m1 = jnp.mean(sc, axis=1, keepdims=True)
        m2 = jnp.mean(sc * v, axis=1, keepdims=True)
        col_sum(gain_row, y * v)
        col_sum(shift_row, y)
        iv = inv[n, pl.ds(start, 64), :][:, 0:1]
        return (sc - m1 - v * m2) * iv

    def unit_t(i):
        for n in ("wu", "u2", "inv"):
            need(n)
        yb[...] = nt(slot(pre, i)[...], pool[1])

        def f(r, start):
            back = norm_back(r, 1, at(u2, start), start, 7, 8, gain_two[...].astype(F32)[None, :])
            m = at(cot, start)[...].astype(F32) + back
            mg[pl.ds(start, 64), :] = m
            b = m.astype(BF)
            at(bg, start)[...] = b
            col_sum(3, b.astype(F32))

        blocks(i, f)
        if i == 0:
            fetch("wo", ins["w"].at[3], pool.at[0])
        tall[0, :, item_rows(i)] = slot(bg, i)[...].T
        if i == 2:
            fetch("wv", ins["w"].at[2], pool.at[1])
            fetch("qy", ins["q"], slot(qy))
            fetch("vy", ins["v"], slot(vy))
            fetch("one_t", ins["one_t"], tall.at[1])

    def unit_y(i):
        need("wo")
        slot(ag, i)[...] = nn(slot(bg, i)[...], pool[0]).astype(BF)
        if i == 2:
            fetch("wk", ins["w"].at[1], pool.at[0])

    def unit_w(half):
        def f(i):
            for n in ("qy", "vy", "ky", "probs"):
                need(n)
            zero = jnp.zeros((), BF)
            accs = [[None] * 5 for _ in range(3)]
            qr, kr, vr, gr = slot(qy, i), slot(ky, i), slot(vy, i), slot(ag, i)
            for hh in range(4):
                lanes = pl.ds(half * 640 + hh * 128, 256)
                mask = head_window(hh)
                gm = jnp.where(mask, gr[:, lanes], zero)
                pb = probs[i * 8 + half * 4 + hh]
                dp = nt(gm, vr[:, lanes])
                pf = pb.astype(F32)
                inner = jnp.sum(dp * pf, axis=1, keepdims=True)
                ds = (pf * (dp - inner)).astype(BF)
                dv = tn(pb, gm)
                dq = nn(ds, jnp.where(mask, kr[:, lanes], zero)) * (HS ** -0.5)
                dk = tn(ds, jnp.where(mask, qr[:, lanes], zero)) * (HS ** -0.5)
                for acc, val in zip(accs, (dq, dk, dv)):
                    for t in (0, 1):
                        piece = val[:, t * 128:(t + 1) * 128]
                        acc[hh + t] = piece if acc[hh + t] is None else acc[hh + t] + piece
            for acc, ref, row in zip(accs, (qr, kr, vr), (0, None, 1)):
                for t in range(5):
                    lanes = pl.ds(half * 640 + t * 128, 128)
                    b = acc[t].astype(BF)
                    ref[:, lanes] = b
                    if row is not None:
                        sm[row:row + 1, lanes] += jnp.sum(b.astype(F32), axis=0, keepdims=True)
            if i == 2 and half == 1:
                fetch("wq", ins["w"].at[0], flat.at[pl.ds(0, 1280)])
                fetch("u1", ins["u1"], slot(u1))
        return f

    def unit_s(i):
        for n in ("wq", "wk", "wv", "u1"):
            need(n)
        yb[...] = nt(slot(qy, i)[...], flat[0:1280, :])
        yb[...] += nt(slot(ky, i)[...], pool[0])
        yb[...] += nt(slot(vy, i)[...], pool[1])
        mark = lax.broadcasted_iota(jnp.int32, (16, 1), 0) == ids[i]

        def f(r, start):
            back = norm_back(r, 0, at(u1, start), start, 5, 6, gain_one[...].astype(F32)[None, :])
            g = mg[pl.ds(start, 64), :] + back
            at(qy, start)[...] = g.astype(BF)
            total = jnp.sum(g, axis=0, keepdims=True)
            sm[16:32, :] += jnp.where(mark, total, 0.0)

        blocks(i, f)
        fetch("mid%d" % i, ins["mid"].at[item_rows(i)], mg.at[item_rows(i)])
        if i == 2:
            fetch("wd", ins["w"].at[5], pool.at[0])
            fetch("hid", ins["hid"], slot(vy))
        cp = pltpu.make_async_copy(slot(qy, i), lat_out.at[item_rows(i)], osem.at[3 + i])
        cp.start()
        results.append(cp)

    arc, arp, arz, tot = (bufs[n] for n in ("arc", "arp", "arz", "tot"))
    pair = (p.i, 1 - p.c)
    me = p.i % 4
    mine = pl.ds(pl.multiple_of(me * 8, 8), 8)

    def others(count, self_at, f):
        for j in range(count):
            pl.when(self_at != j)(functools.partial(f, j))

    def copy(src, dst, dev, n, m):
        return pltpu.make_async_remote_copy(src, dst, tsem.at[n], tsem.at[m], device_id=dev, device_id_type=MESH)

    def local(ref, n):
        pltpu.make_async_copy(ref, ref, tsem.at[n]).wait()

    def total(n):
        half = sm.at[mine, s.cols]
        if n == 0:
            copy(sm.at[:, s.others], arc, pair, 0, 1).start()
        elif n == 1:
            local(arc, 1)
            sm[:, s.cols] += arc[...]
            others(4, me, lambda j: copy(sm.at[pl.ds(8 * j, 8), s.cols], arp.at[me], (p.i - me + j, p.c), 2, 4 + me).start())
            arp[me] = half[...]
        elif n == 2:
            others(4, me, lambda j: local(arp.at[j], 4 + j))
            arz[p.z] = arp[0] + arp[1] + arp[2] + arp[3]
            others(zs, p.z, lambda j: copy(arz.at[p.z], arz.at[p.z], (4 * j + me, p.c), 3, 8 + p.z).start())
        elif n == 3:
            others(zs, p.z, lambda j: local(arz.at[j], 8 + j))
            tot[mine, s.cols] = arz[0] + arz[1] + arz[2] + arz[3]
            part = tot.at[mine, s.cols]
            others(4, me, lambda j: copy(part, part, (p.i - me + j, p.c), 12, 16 + me).start())
        elif n == 4:
            others(4, me, lambda j: local(tot.at[pl.ds(8 * j, 8), s.cols], 16 + j))
            copy(tot.at[:, s.cols], tot.at[:, s.cols], pair, 13, 14).start()
        else:
            local(arc, 14)
            sm_out[...] = tot[...]
            local(arc, 0)
            three = pl.ds(0, 3)
            local(arp.at[three], 2)
            local(arp.at[three], 3)
            local(arp.at[three], 12)
            local(arc, 13)

    units = (unit_p, unit_n, unit_t, unit_y, unit_w(0), unit_w(1), unit_s, total)
    for code in ORDER_TWO:
        kind, k, t = code // 100, code // 10 % 10, code % 10
        if kind == 0:
            units[k](t)
        elif kind == 1:
            grad(k, t)
        elif kind == 2:
            s.c_arrive(k, t)
        elif kind == 3:
            s.b_arrive(k, t)
        elif kind == 4:
            s.a_arrive(k, t)
        elif kind == 5:
            s.z_step(k, True, t)
        elif kind == 6:
            s.z_step(k, False, t)
        elif kind == 7:
            s.z_end(k, True)
        elif kind == 8:
            s.z_end(k, False)
        else:
            s.finish(k)
    for k in range(2, 6):
        s.drain(k)
    for cp in results:
        cp.wait()


def backward(r, cotangent, ids, vectors, zs):
    rows, width = cotangent.shape
    DMA = pltpu.SemaphoreType.DMA
    n = 4 * zs
    grow = width // n
    half = width // 2
    ins = [r["w"].reshape(6, width, width)] + [r[k] for k in SAVED] + [r["mid"], r["inv"], r["probs"], cotangent]
    shapes = dict(
        pool=((6, width, width), BF), tall=((2, width, rows), BF), flat=((6 * rows, width), BF), mg=((rows, width), F32),
        probs=((24, LAT, LAT), BF), inv=((2, rows, 128), F32), yb=((LAT, width), F32), sm=((32, width), F32),
        rc=((3, width, half), BF), rb=((6, 2 * zs, grow, half), BF), rz=((6, zs + 1, 2 * PARTS[0][0][2] + PARTS[0][1][2], half), BF), ra=((6, zs, grow, half), BF),
        arc=((32, half), F32), arp=((4, 8, half), F32), arz=((zs, 8, half), F32), tot=((32, width), F32))
    ANY, VM = pl.BlockSpec(memory_space=pl.ANY), pl.BlockSpec(memory_space=pltpu.VMEM)
    return pl.pallas_call(
        functools.partial(backward_kernel, zs),
        out_shape=[jax.ShapeDtypeStruct((grow, half), F32)] * 6 + [jax.ShapeDtypeStruct((rows, width), BF)] * 2
        + [jax.ShapeDtypeStruct((32, width), F32)],
        in_specs=[pl.BlockSpec(memory_space=pltpu.SMEM)] + [VM] * 3 + [ANY] * len(ins),
        out_specs=[VM] * 6 + [ANY] * 2 + [VM],
        scratch_shapes=[pltpu.VMEM(*shapes[k]) for k in NAMES_TWO] + [
            DMA((6,)), DMA((6, zs)), DMA((6,)), DMA((6, zs)), DMA((6, 2, zs)), DMA((6, 2, zs + 1)), DMA((6, 2)), DMA((6, 2, zs)),
            pltpu.SemaphoreType.REGULAR, DMA((32,)), DMA((6,)), DMA((20,)),
        ],
        compiler_params=pltpu.CompilerParams(collective_id=1, has_side_effects=True, vmem_limit_bytes=63 << 20),
        name="backward_and_scatter",
    )(ids, *vectors, *ins)


def hand_out_kernel(*refs):
    small, table, wide, narrow = refs[8], refs[17], refs[18:24], refs[24:27]
    stage, isem, osem = refs[27:35], refs[35], refs[36]
    copies = [(pltpu.make_async_copy(a, v, isem.at[n]), pltpu.make_async_copy(v, b, osem.at[n]))
              for n, (a, v, b) in enumerate(zip(refs[:8], stage, refs[9:17]))]
    for cp, _ in copies:
        cp.start()
    table[...] = small[16:32, :]
    for n, ref in enumerate(wide):
        ref[...] = small[3 + n:4 + n, :].reshape(ref.shape)
    half = narrow[0].shape[0]
    c = lax.axis_index("head")
    cols = pl.ds(pl.multiple_of(c * half, 128), half)
    for n, ref in enumerate(narrow):
        ref[...] = small[n:n + 1, cols].reshape(ref.shape)
    for cp, back in copies:
        cp.wait()
        back.start()
    for _, back in copies:
        back.wait()


def hand_out(large, small):
    width = small.shape[1]
    ANY, VM = pl.BlockSpec(memory_space=pl.ANY), pl.BlockSpec(memory_space=pltpu.VMEM)
    n = len(large)
    like = [jax.ShapeDtypeStruct(a.shape, a.dtype) for a in large]
    return pl.pallas_call(
        hand_out_kernel,
        out_shape=like + [jax.ShapeDtypeStruct((16, width), F32)]
        + [jax.ShapeDtypeStruct((width,), F32)] * 6 + [jax.ShapeDtypeStruct((width // 2,), F32)] * 3,
        in_specs=[ANY] * n + [VM],
        out_specs=[ANY] * n + [VM] * 10,
        scratch_shapes=[pltpu.VMEM(a.shape, a.dtype) for a in large] + [pltpu.SemaphoreType.DMA((n,))] * 2,
        compiler_params=pltpu.CompilerParams(vmem_limit_bytes=63 << 20),
        name="hand_out",
    )(*large, small)


def in_blocks(x, dim, length):
    before, after = (x.shape[:dim], x.shape[dim + 1 :])
    return jnp.moveaxis(x.reshape(*before, length, -1, *after), dim, 0)


def sent_and_summed(x, axis, dim):
    tiles = in_blocks(x, dim, lax.axis_size(axis))
    arrived = lax.all_to_all(tiles, axis, split_axis=0, concat_axis=0, tiled=True)
    return arrived.astype(jnp.float32).sum(axis=0)


def side_by_side(arrays, axis, dim, along):
    ends, at = ([], 0)
    for a in arrays[:-1]:
        at += a.shape[along]
        ends.append(at)
    both = jnp.concatenate(arrays, axis=along)
    return tuple(jnp.split(sent_and_summed(both, axis, dim), ends, axis=along))


def norm_forward(row_block, norm_gain, norm_shift):
    row_mean = jnp.mean(row_block, axis=1, keepdims=True)
    centered = row_block - row_mean
    row_var = jnp.mean(centered * centered, axis=1, keepdims=True)
    inverse = lax.rsqrt(row_var + EPSILON)
    normed = centered * inverse
    return (normed * norm_gain + norm_shift, normed, inverse)


def norm_backward(grad_rows, normed, inverse, norm_gain):
    scaled = grad_rows * norm_gain
    first_moment = jnp.mean(scaled, axis=1, keepdims=True)
    second_moment = jnp.mean(scaled * normed, axis=1, keepdims=True)
    grad_input = (scaled - first_moment - normed * second_moment) * inverse
    return (grad_input, jnp.sum(grad_rows * normed, axis=0), jnp.sum(grad_rows, axis=0))


def contract_rows(left, right):
    return lax.dot_general(
        left, right, (((0,), (0,)), ((), ())), preferred_element_type=jnp.float32
    )


def contract_cols(left, right):
    return lax.dot_general(
        left, right, (((1,), (1,)), ((), ())), preferred_element_type=jnp.float32
    )


def split_heads(matrix):
    item_count = matrix.shape[0] // LAT
    return matrix.reshape(item_count, LAT, matrix.shape[1] // HS, HS)


def attend_forward(query_rows, key_rows, value_rows):
    factor = HS ** (-0.5)
    scores = (
        jnp.einsum(
            "iqhc,ikhc->ihqk",
            split_heads(query_rows),
            split_heads(key_rows),
            preferred_element_type=jnp.float32,
        )
        * factor
    )
    row_max = jnp.max(scores, axis=-1, keepdims=True)
    exp_scores = jnp.exp(scores - row_max)
    row_total = jnp.sum(exp_scores, axis=-1, keepdims=True)
    soft_probs = (exp_scores / row_total).astype(jnp.bfloat16)
    attended = jnp.einsum(
        "ihqk,ikhc->iqhc", soft_probs, split_heads(value_rows), preferred_element_type=jnp.float32
    )
    return (attended.reshape(query_rows.shape).astype(jnp.bfloat16), row_max + jnp.log(row_total))


def attend_backward(query_rows, key_rows, value_rows, log_total, attended_grad):
    factor = HS ** (-0.5)
    query_heads = split_heads(query_rows)
    key_heads = split_heads(key_rows)
    value_heads = split_heads(value_rows)
    grad_heads = split_heads(attended_grad)
    scores = (
        jnp.einsum("iqhc,ikhc->ihqk", query_heads, key_heads, preferred_element_type=jnp.float32)
        * factor
    )
    soft_probs = jnp.exp(scores - log_total)
    value_grad = jnp.einsum(
        "ihqk,iqhc->ikhc",
        soft_probs.astype(jnp.bfloat16),
        grad_heads,
        preferred_element_type=jnp.float32,
    )
    probs_grad = jnp.einsum(
        "iqhc,ikhc->ihqk", grad_heads, value_heads, preferred_element_type=jnp.float32
    )
    inner_sum = jnp.sum(probs_grad * soft_probs, axis=-1, keepdims=True)
    score_grad = (soft_probs * (probs_grad - inner_sum)).astype(jnp.bfloat16)
    query_grad = (
        jnp.einsum("ihqk,ikhc->iqhc", score_grad, key_heads, preferred_element_type=jnp.float32)
        * factor
    )
    key_grad = (
        jnp.einsum("ihqk,iqhc->ikhc", score_grad, query_heads, preferred_element_type=jnp.float32)
        * factor
    )
    full_shape = query_rows.shape
    return (
        query_grad.reshape(full_shape).astype(jnp.bfloat16),
        key_grad.reshape(full_shape).astype(jnp.bfloat16),
        value_grad.reshape(full_shape).astype(jnp.bfloat16),
    )


def gelu_value(pre_act):
    return 0.5 * pre_act * (1.0 + lax.erf(pre_act * ROOT_HALF))


def gelu_slope(pre_act):
    return (
        0.5 * (1.0 + lax.erf(pre_act * ROOT_HALF))
        + pre_act * jnp.exp(-0.5 * pre_act * pre_act) * INV_ROOT_TWO_PI
    )


def place_slot(piece, head_index, full_len):
    empty = jnp.zeros((full_len,), jnp.float32)
    return lax.dynamic_update_slice_in_dim(empty, piece, head_index * piece.shape[0], 0)


def on_any_mesh(
    latents,
    lang_ids,
    lang_table,
    gain_one,
    shift_one,
    w_query,
    b_query,
    w_key,
    w_value,
    b_value,
    w_out,
    b_out,
    gain_two,
    shift_two,
    w_up,
    b_up,
    w_down,
    b_down,
    cotangent,
):
    own_rows = latents.shape[0]
    model_width = latents.shape[1]
    item_count = lang_ids.shape[0]
    head_index = lax.axis_index("head")
    head_count = lax.axis_size("head")
    w_query, w_key, w_value, w_up, w_out, w_down = (
        lax.all_gather(w_query, "dp", axis=0, tiled=True),
        lax.all_gather(w_key, "dp", axis=0, tiled=True),
        lax.all_gather(w_value, "dp", axis=0, tiled=True),
        lax.all_gather(w_up, "dp", axis=0, tiled=True),
        lax.all_gather(w_out, "dp", axis=1, tiled=True),
        lax.all_gather(w_down, "dp", axis=1, tiled=True),
    )
    one_hot = (lang_ids[:, None] == jnp.arange(LANGS, dtype=jnp.int32)[None, :]).astype(jnp.float32)
    embedded = jnp.dot(one_hot, lang_table, precision=HIGHEST)
    start_rows = (
        latents.astype(jnp.float32).reshape(item_count, LAT, model_width) + embedded[:, None, :]
    ).reshape(own_rows, model_width)
    gain_first = gain_one.astype(jnp.float32)
    gain_second = gain_two.astype(jnp.float32)
    normed_one, unit_one, inverse_one = norm_forward(
        start_rows, gain_first, shift_one.astype(jnp.float32)
    )
    input_one = normed_one.astype(jnp.bfloat16)
    group_one = lax.all_gather(input_one, "head", axis=0, tiled=True)
    query_rows = (
        jnp.dot(group_one, w_query, preferred_element_type=jnp.float32)
        + b_query.astype(jnp.float32)
    ).astype(jnp.bfloat16)
    key_rows = jnp.dot(group_one, w_key, preferred_element_type=jnp.float32).astype(jnp.bfloat16)
    value_rows = (
        jnp.dot(group_one, w_value, preferred_element_type=jnp.float32)
        + b_value.astype(jnp.float32)
    ).astype(jnp.bfloat16)
    attended, log_total = attend_forward(query_rows, key_rows, value_rows)
    attn_branch = lax.psum_scatter(
        jnp.dot(attended, w_out, preferred_element_type=jnp.float32),
        "head",
        scatter_dimension=0,
        tiled=True,
    )
    middle_rows = start_rows + (attn_branch + b_out.astype(jnp.float32))
    normed_two, unit_two, inverse_two = norm_forward(
        middle_rows, gain_second, shift_two.astype(jnp.float32)
    )
    input_two = normed_two.astype(jnp.bfloat16)
    group_two = lax.all_gather(input_two, "head", axis=0, tiled=True)
    pre_act = jnp.dot(group_two, w_up, preferred_element_type=jnp.float32) + b_up.astype(
        jnp.float32
    )
    hidden = gelu_value(pre_act).astype(jnp.bfloat16)
    down_branch = lax.psum_scatter(
        jnp.dot(hidden, w_down, preferred_element_type=jnp.float32).astype(jnp.bfloat16),
        "head",
        scatter_dimension=0,
        tiled=True,
    ).astype(jnp.float32)
    result = (middle_rows + (down_branch + b_down.astype(jnp.float32))).astype(jnp.bfloat16)
    group_cot = lax.all_gather(cotangent, "head", axis=0, tiled=True)
    grad_w_down = contract_rows(hidden, group_cot)
    grad_b_down = jnp.sum(cotangent.astype(jnp.float32), axis=0)
    pre_grad = (contract_cols(group_cot, w_down) * gelu_slope(pre_act)).astype(jnp.bfloat16)
    grad_w_up = contract_rows(group_two, pre_grad)
    grad_b_up = jnp.sum(pre_grad.astype(jnp.float32), axis=0)
    grad_two = lax.psum_scatter(
        contract_cols(pre_grad, w_up), "head", scatter_dimension=0, tiled=True
    )
    back_two, grad_gain_two, grad_shift_two = norm_backward(
        grad_two, unit_two, inverse_two, gain_second
    )
    middle_grad = cotangent.astype(jnp.float32) + back_two
    branch_grad = middle_grad.astype(jnp.bfloat16)
    grad_b_out = jnp.sum(branch_grad.astype(jnp.float32), axis=0)
    group_branch = lax.all_gather(branch_grad, "head", axis=0, tiled=True)
    grad_w_out = contract_rows(attended, group_branch)
    attended_grad = contract_cols(group_branch, w_out).astype(jnp.bfloat16)
    query_grad, key_grad, value_grad = attend_backward(
        query_rows, key_rows, value_rows, log_total, attended_grad
    )
    grad_w_query = contract_rows(group_one, query_grad)
    grad_w_key = contract_rows(group_one, key_grad)
    grad_w_value = contract_rows(group_one, value_grad)
    grad_b_query = jnp.sum(query_grad.astype(jnp.float32), axis=0)
    grad_b_value = jnp.sum(value_grad.astype(jnp.float32), axis=0)
    total_term = contract_cols(query_grad, w_query)
    total_term = total_term + contract_cols(key_grad, w_key)
    grad_one = lax.psum_scatter(
        (total_term + contract_cols(value_grad, w_value)).astype(jnp.bfloat16),
        "head",
        scatter_dimension=0,
        tiled=True,
    ).astype(jnp.float32)
    back_one, grad_gain_one, grad_shift_one = norm_backward(
        grad_one, unit_one, inverse_one, gain_first
    )
    start_grad = middle_grad + back_one
    latents_grad = start_grad.astype(jnp.bfloat16)
    item_sums = jnp.sum(start_grad.reshape(item_count, LAT, model_width), axis=1)
    grad_table = jnp.dot(one_hot.T, item_sums, precision=HIGHEST)
    full_b_query = place_slot(grad_b_query, head_index, model_width)
    full_b_value = place_slot(grad_b_value, head_index, model_width)
    full_b_up = place_slot(grad_b_up, head_index, FF)
    grad_w_query, grad_w_key, grad_w_value, grad_w_up, grad_w_out, grad_w_down = (
        *side_by_side(
            (
                grad_w_query.astype(jnp.bfloat16),
                grad_w_key.astype(jnp.bfloat16),
                grad_w_value.astype(jnp.bfloat16),
                grad_w_up.astype(jnp.bfloat16),
            ),
            "dp",
            0,
            1,
        ),
        *side_by_side(
            (grad_w_out.astype(jnp.bfloat16), grad_w_down.astype(jnp.bfloat16)), "dp", 1, 0
        ),
    )
    summed = lax.psum(
        (
            full_b_query,
            full_b_value,
            full_b_up,
            grad_b_out,
            grad_b_down,
            grad_gain_one,
            grad_shift_one,
            grad_gain_two,
            grad_shift_two,
            grad_table,
        ),
        ("dp", "head"),
    )
    local_width = model_width // head_count
    local_hidden = FF // head_count
    out_b_query = lax.dynamic_slice_in_dim(summed[0], head_index * local_width, local_width, 0)
    out_b_value = lax.dynamic_slice_in_dim(summed[1], head_index * local_width, local_width, 0)
    out_b_up = lax.dynamic_slice_in_dim(summed[2], head_index * local_hidden, local_hidden, 0)
    return (
        result,
        latents_grad,
        summed[9],
        summed[5],
        summed[6],
        grad_w_query,
        out_b_query,
        grad_w_key,
        grad_w_value,
        out_b_value,
        grad_w_out,
        summed[3],
        summed[7],
        summed[8],
        grad_w_up,
        out_b_up,
        grad_w_down,
        summed[4],
    )


def on_device(
    latents, lang_ids, lang_table, gain_one, shift_one, w_query, b_query, w_key, w_value, b_value, w_out, b_out,
    gain_two, shift_two, w_up, b_up, w_down, b_down, cotangent,
):
    zs = lax.axis_size("dp") // 4
    r = forward(
        latents, cotangent, lang_ids, lang_table, (gain_one, shift_one, gain_two, shift_two, b_out, b_query, b_value, b_up),
        (w_query, w_key, w_value, w_out.T, w_up, w_down.T), zs)
    *large, small = backward(r, cotangent, lang_ids, (gain_one, gain_two, b_down), zs)
    got = hand_out(large, small)
    down, up, out, value, key, query, result, latents_grad, table = got[:9]
    b_out_g, b_down_g, gain_one_g, shift_one_g, gain_two_g, shift_two_g = got[9:15]
    b_query_g, b_value_g, b_up_g = got[15:]
    return (
        result, latents_grad, table, gain_one_g, shift_one_g, query, b_query_g, key, value, b_value_g, out.T, b_out_g,
        gain_two_g, shift_two_g, up, b_up_g, down.T, b_down_g,
    )

def solution(mesh):
    in_specs = (
        P(("dp", "head"), None),
        P(("dp", "head")),
        P(),
        P(),
        P(),
        P("dp", "head"),
        P("head"),
        P("dp", "head"),
        P("dp", "head"),
        P("head"),
        P("head", "dp"),
        P(),
        P(),
        P(),
        P("dp", "head"),
        P("head"),
        P("head", "dp"),
        P(),
        P(("dp", "head"), None),
    )
    out_specs = (
        P(("dp", "head"), None),
        P(("dp", "head"), None),
        P(),
        P(),
        P(),
        P("dp", "head"),
        P("head"),
        P("dp", "head"),
        P("dp", "head"),
        P("head"),
        P("head", "dp"),
        P(),
        P(),
        P(),
        P("dp", "head"),
        P("head"),
        P("head", "dp"),
        P(),
    )
    fast = mesh.shape["dp"] == 16 and mesh.shape["head"] == 2
    return jax.shard_map(
        on_device if fast else on_any_mesh, mesh=mesh, in_specs=in_specs, out_specs=out_specs, check_vma=False
    )
```

```python
import functools
import jax
import jax.numpy as jnp
from jax import lax
from jax.experimental import pallas as pl
from jax.experimental.pallas import tpu as pltpu
from jax.sharding import PartitionSpec as P

MESH = pl.DeviceIdType.MESH
BF = jnp.bfloat16
F32 = jnp.float32
HS = 160
LAT = 256
LANGS = 16
EPSILON = 1e-05
HIGHEST = lax.Precision.HIGHEST
ROOT_HALF = 0.7071067811865476
INV_ROOT_TWO_PI = 0.3989422804014327
FF = 1280


class Place:
    def __init__(self, zs):
        self.zs = zs
        i = lax.axis_index("dp")
        c = lax.axis_index("head")
        self.i, self.c = i, c
        self.z = i // 4
        self.sa = 1 + c
        self.sb = 2 - c
        x = i % 2
        y = (i // 2) % 2
        self.a = jnp.where(c == 0, x, y)
        self.b = jnp.where(c == 0, y, x)
        self.ia = i + self.sa * (1 - 2 * self.a)
        self.ib = i + self.sb * (1 - 2 * self.b)
        self.up = jnp.minimum(i + 4, 4 * zs - 1)
        self.down = jnp.maximum(i - 4, 0)
        self.has_up = self.z < zs - 1
        self.has_down = self.z > 0

    def barrier(self):
        bar = pltpu.get_barrier_semaphore()
        i, c = self.i, self.c
        for dev in ((self.ia, c), (self.ib, c), (i, 1 - c)):
            pl.semaphore_signal(bar, inc=1, device_id=dev, device_id_type=MESH)

        @pl.when(self.has_up)
        def _():
            pl.semaphore_signal(bar, inc=1, device_id=(self.up, c), device_id_type=MESH)

        @pl.when(self.has_down)
        def _():
            pl.semaphore_signal(bar, inc=1, device_id=(self.down, c), device_id_type=MESH)

        n = 3 + jnp.where(self.has_up, 1, 0) + jnp.where(self.has_down, 1, 0)
        pl.semaphore_wait(bar, n)

    def barrier_wide(self):
        bar = pltpu.get_barrier_semaphore()
        me = self.i % 4
        pl.semaphore_signal(bar, inc=1, device_id=(self.i, 1 - self.c), device_id_type=MESH)
        for j in range(4):
            @pl.when(me != j)
            def _(j=j):
                pl.semaphore_signal(bar, inc=1, device_id=(self.i - me + j, self.c), device_id_type=MESH)
        for zz in range(self.zs):
            @pl.when(self.z != zz)
            def _(zz=zz):
                pl.semaphore_signal(bar, inc=1, device_id=(4 * zz + me, self.c), device_id_type=MESH)
        pl.semaphore_wait(bar, 3 + self.zs)


ORDER_ONE = (
    0, 20, 80, 60, -2, 2, -1, 27, -14, 40, -13, -15, 67, 62, 42, 7, 70, 28, 22, 23,
    47, 10, 30, 8, 29, 24, 50, -3, 68, 25, 48, 9, 11, 31, 82, 12, 69, 33, 13, 32,
    100, 51, 49, 63, 64, 1, -4, -5, 21, -8, 52, 65, 87, -7, 53, -9, -6, 41, -10, 107,
    90, -19, -11, 88, -17, 71, -16, 73, 108, -12, 72, -18, -20, 91, 61, 103, -21, 89, -22, 92,
    109, 104, 102, -23, 93, -24, 105, 81, -26, 112, 111, -25, 110, 113, -27, 101,
)
ORDER_TWO = (
    100, 101, 1, 200, 0, 201, 102, 103, 2, 202, 300, 110, 112, 503, 111, 113, 210, 20, 212, 211,
    301, 21, 310, 502, 22, 213, 120, 30, 311, 121, 220, 203, 302, 410, 31, 613, 32, 501, 51, 313,
    123, 320, 221, 122, 41, 411, 612, 312, 42, 523, 50, 303, 700, 40, 412, 222, 321, 611, 52, 413,
    130, 900, 223, 140, 132, 230, 141, 240, 143, 810, 322, 142, 241, 150, 522, 152, 330, 151, 131, 250,
    153, 340, 252, 251, 543, 60, 521, 242, 243, 61, 430, 341, 350, 542, 232, 133, 231, 633, 62, 70,
    450, 342, 653, 541, 352, 331, 351, 71, 332, 253, 233, 323, 12, 431, 632, 451, 652, 343, 72, 11,
    452, 432, 740, 353, 73, 631, 720, 651, 333, 74, 453, 10, 940, 433, 920, 830, 850, 75,
)
SUM_MIDDLE = (True, False) * 3


def nn(a, b):
    return lax.dot_general(a, b, (((1,), (0,)), ((), ())), preferred_element_type=F32)


def nt(a, b):
    return lax.dot_general(a, b, (((1,), (1,)), ((), ())), preferred_element_type=F32)


def tn(a, b):
    return lax.dot_general(a, b, (((0,), (0,)), ((), ())), preferred_element_type=F32)


def item_rows(i):
    return pl.ds(i * LAT, LAT)


def head_window(hh):
    at = lax.broadcasted_iota(jnp.int32, (1, 256), 1) + hh * 128
    return (at >= hh * HS) & (at < (hh + 1) * HS)


class Gather:
    def __init__(self, p, w, sems, streams):
        self.p, self.w, self.streams = p, w, streams
        self.zsend, self.zrecv, self.asend, self.arecv, self.bsend, self.brecv, self.csend, self.crecv = sems
        self.cols = pl.ds(pl.multiple_of(p.c * 640, 128), 640)

    def sub(self, s, j, n=None):
        k, mid, r0, rows = self.streams[s]
        return self.w.at[k, j if n is None else pl.ds(j, n), pl.ds(r0, rows), self.cols]

    def mid(self, s):
        return self.streams[s][1]

    def send(self, s, j, n, dev, ssem, rsem):
        ref = self.sub(s, j) if n == 1 else self.sub(s, j, n)
        pltpu.make_async_remote_copy(ref, ref, ssem, rsem, device_id=dev, device_id_type=MESH).start()

    def arrived(self, s, n, sem):
        ref = self.sub(s, 0, n)
        pltpu.make_async_copy(ref, ref, sem).wait()

    def members(self, s, zz):
        p = self.p
        base = zz * 4 + p.b * p.sb
        return (base, base + p.sa) if self.mid(s) else (base + p.a * p.sa,)

    def z_send(self, s, zz, upward):
        p = self.p
        dev, d = ((p.up, p.c), 0) if upward else ((p.down, p.c), 1)
        for j in self.members(s, zz):
            self.send(s, j, 1, dev, self.zsend.at[s, d, zz], self.zrecv.at[s, zz])

    def z_first(self, s):
        p = self.p
        pl.when(p.has_up)(lambda: self.z_send(s, p.z, True))
        pl.when(p.has_down)(lambda: self.z_send(s, p.z, False))

    def at_distance(self, d, f):
        p = self.p
        pl.when(p.z - d >= 0)(lambda: f(p.z - d, True))
        pl.when(p.z + d <= p.zs - 1)(lambda: f(p.z + d, False))

    def around(self, d, f):
        if d == 0:
            f(self.p.z)
        else:
            self.at_distance(d, lambda zz, below: f(zz))

    def z_arrive(self, s, d, then):
        p = self.p
        n = len(self.members(s, 0))

        def f(zz, below):
            self.arrived(s, n, self.zrecv.at[s, zz])
            if d < p.zs - 1:
                if below:
                    pl.when(p.has_up)(lambda: self.z_send(s, zz, True))
                else:
                    pl.when(p.has_down)(lambda: self.z_send(s, zz, False))
            then(s, zz)

        self.at_distance(d, f)

    def a_send(self, s, zz):
        p = self.p
        j = zz * 4 + p.b * p.sb + p.a * p.sa
        self.send(s, j, 1, (p.ia, p.c), self.asend.at[s], self.arecv.at[s, zz])

    def a_arrive(self, s, zz, then):
        self.arrived(s, 1, self.arecv.at[s, zz])
        then(s, zz)

    def b_send(self, s, zz):
        p = self.p
        base = zz * 4 + p.b * p.sb
        for j in (base, base + p.sa):
            self.send(s, j, 1, (p.ib, p.c), self.bsend.at[s], self.brecv.at[s, zz])

    def b_arrive(self, s, zz):
        p = self.p
        self.arrived(s, 2, self.brecv.at[s, zz])
        self.send(s, zz * 4, 4, (p.i, 1 - p.c), self.csend.at[s], self.crecv.at[s])

    def do(self, s, ev):
        p = self.p
        if ev == 0:
            if not self.mid(s):
                self.z_first(s)
            self.a_send(s, p.z)
        elif ev == 1:
            self.arrived(s, 4 * p.zs, self.crecv.at[s])
        elif ev >= 10:
            self.around(ev - 10, lambda zz: self.b_arrive(s, zz))
        elif ev >= 6:
            self.z_arrive(s, ev - 6, self.b_send if self.mid(s) else self.a_send)
        elif self.mid(s):
            self.arrived(s, 1, self.arecv.at[s, p.z])
            self.z_first(s)
            self.b_send(s, p.z)
        else:
            self.around(ev - 2, lambda zz: self.a_arrive(s, zz, self.b_send))

    def drain(self, s):
        p = self.p
        n = len(self.members(s, 0))
        for zz in range(p.zs):
            @pl.when(jnp.logical_and(p.has_up, zz <= p.z))
            def _(zz=zz):
                self.arrived(s, n, self.zsend.at[s, 0, zz])

            @pl.when(jnp.logical_and(p.has_down, zz >= p.z))
            def _(zz=zz):
                self.arrived(s, n, self.zsend.at[s, 1, zz])
        self.arrived(s, 1 if self.mid(s) else p.zs, self.asend.at[s])
        self.arrived(s, 2 * p.zs, self.bsend.at[s])
        self.arrived(s, 4 * p.zs, self.csend.at[s])


STREAMS = tuple((k, k % 2 == 0, 0, 80) for k in range(6))
SAVED = ("one_t", "q", "k", "v", "att", "hid", "slope", "two_t", "cot_t", "u1", "u2")
TALL = ("one_t", "two_t", "cot_t")


def forward_kernel(zs, *refs):
    lat_in, cot_in, ids, table = refs[:4]
    vectors, shards = refs[4:12], refs[12:18]
    at = 18
    outs = dict(zip(("w",) + SAVED + ("mid", "inv", "probs"), refs[at:at + 15]))
    at += 15
    bufs = dict(zip(("w",) + SAVED + ("mid", "inv", "probs", "lat", "cot", "one", "two", "hb", "fulls"), refs[at:at + 21]))
    at += 21
    gsems = refs[at:at + 8]
    own, load, save, hsem = refs[at + 8:at + 12]
    p = Place(zs)
    w = bufs["w"]
    g = Gather(p, w, gsems, STREAMS)
    hb = bufs["hb"]
    copies = [pltpu.make_async_copy(shards[k], w.at[k, p.i, :, g.cols], own.at[k]) for k in range(6)]
    for cp in copies:
        cp.start()
    loads = [pltpu.make_async_copy(src.at[item_rows(i)], bufs[n].at[item_rows(i)], load.at[j, i])
             for j, (src, n) in enumerate(((lat_in, "lat"), (cot_in, "cot"))) for i in range(3)]
    for cp in loads:
        cp.start()
    fulls = bufs["fulls"]
    for n in range(5):
        fulls[n:n + 1, :] = vectors[n][...].astype(F32)[None, :]
    for n in range(3):
        hb[n:n + 1, g.cols] = vectors[5 + n][...].astype(F32)[None, :]
    p.barrier()
    half_send = pltpu.make_async_remote_copy(hb.at[:, g.cols], hb.at[:, g.cols], hsem.at[0], hsem.at[1],
                                             device_id=(p.i, 1 - p.c), device_id_type=MESH)
    half_send.start()
    names = ("w",) + SAVED + ("mid", "inv", "probs")
    saves = []

    def keep(name, index=None):
        src, dst = bufs[name], outs[name]
        if index is not None:
            src, dst = src.at[index], dst.at[index]
        n = len(saves)
        assert n < save.shape[0]
        cp = pltpu.make_async_copy(src, dst, save.at[n])
        cp.start()
        saves.append(cp)

    def start_of(i):
        return bufs["lat"][item_rows(i)].astype(F32) + table[pl.ds(ids[i], 1), :]

    def norm(v):
        mean = jnp.mean(v, axis=1, keepdims=True)
        cen = v - mean
        inv = lax.rsqrt(jnp.mean(cen * cen, axis=1, keepdims=True) + EPSILON)
        return cen * inv, inv

    def norm_rows(i, n, rows_of, u_name, out_name, tall_name):
        gain, shift = fulls[2 * n:2 * n + 1, :], fulls[2 * n + 1:2 * n + 2, :]

        def body(r, carry):
            rows = pl.ds(pl.multiple_of(i * LAT + r * 64, 64), 64)
            unit, inv = norm(rows_of(rows))
            bufs[u_name][rows, :] = unit.astype(BF)
            bufs[out_name][rows, :] = (unit * gain + shift).astype(BF)
            bufs["inv"][n, rows, :] = jnp.broadcast_to(inv, (64, 128))
            return carry

        lax.fori_loop(0, 4, body, 0)
        bufs[tall_name][:, item_rows(i)] = bufs[out_name][item_rows(i), :].T

    def whole(k):
        return w[k].reshape(1280, 1280)

    def ln1(i):
        loads[i].wait()
        emb = table[pl.ds(ids[i], 1), :]
        norm_rows(i, 0, lambda rows: bufs["lat"][rows, :].astype(F32) + emb, "u1", "one", "one_t")

    def project(name, k, bias):
        def f(i):
            y = nn(bufs["one"][item_rows(i), :], whole(k))
            if bias is not None:
                y = y + hb[bias:bias + 1, :]
            bufs[name][item_rows(i), :] = y.astype(BF)
        return f

    def cot(i):
        loads[3 + i].wait()
        bufs["cot_t"][:, item_rows(i)] = bufs["cot"][item_rows(i), :].T

    def attend(half):
        def f(i):
            rows = item_rows(i)
            zero = jnp.zeros((), BF)
            acc = [None] * 5
            for hh in range(4):
                lanes = pl.ds(half * 640 + hh * 128, 256)
                mask = head_window(hh)
                qm = jnp.where(mask, bufs["q"][rows, lanes], zero)
                s = nt(qm, bufs["k"][rows, lanes]) * (HS ** -0.5)
                e = jnp.exp(s - jnp.max(s, axis=1, keepdims=True))
                pr = (e / jnp.sum(e, axis=1, keepdims=True)).astype(BF)
                bufs["probs"][i * 8 + half * 4 + hh] = pr
                vm = jnp.where(mask, bufs["v"][rows, lanes], zero)
                a = nn(pr, vm)
                for t in (0, 1):
                    piece = a[:, t * 128:(t + 1) * 128]
                    acc[hh + t] = piece if acc[hh + t] is None else acc[hh + t] + piece
            for t in range(5):
                bufs["att"][rows, pl.ds(half * 640 + t * 128, 128)] = acc[t].astype(BF)
        return f

    def out(i):
        rows = item_rows(i)
        emb = table[pl.ds(ids[i], 1), :]
        y = nt(bufs["att"][rows, :], whole(3))
        bufs["mid"][rows, :] = y + fulls[4:5, :] + (bufs["lat"][rows, :].astype(F32) + emb)
        norm_rows(i, 1, lambda r: bufs["mid"][r, :], "u2", "two", "two_t")

    def up(i):
        rows = item_rows(i)
        pre = nn(bufs["two"][rows, :], whole(4)) + hb[2:3, :]
        cdf = 0.5 * (1.0 + lax.erf(pre * ROOT_HALF))
        bufs["hid"][rows, :] = (pre * cdf).astype(BF)
        bufs["slope"][rows, :] = (cdf + pre * jnp.exp(-0.5 * pre * pre) * INV_ROOT_TWO_PI).astype(BF)

    units = (ln1, project("q", 0, 0), project("k", 1, None), project("v", 2, 1), cot, attend(0), attend(1), out, up)
    after = (("u1", "one_t"), ("q",), ("k",), ("v",), ("cot_t",), (), ("att", "probs"), ("u2", "two_t", "mid", "inv"), ("hid", "slope"))
    seen, full = set(), {}
    for code in ORDER_ONE:
        if code < 0:
            n, i = (-code - 1) // 3, (-code - 1) % 3
            if n == 1 and i == 0:
                half_send.wait_recv()
            units[n](i)
            if i == 2:
                for name in after[n]:
                    keep(name)
            continue
        s, ev = code // 20, code % 20
        k = STREAMS[s][0]
        if k not in seen:
            copies[k].wait()
            seen.add(k)
        g.do(s, ev)
        if ev == 1:
            full[k] = full.get(k, 0) + 1
            if full[k] == sum(t[0] == k for t in STREAMS):
                keep("w", k)
    half_send.wait_send()
    for s in range(len(STREAMS)):
        g.drain(s)
    for cp in saves:
        cp.wait()


def forward(latents, cotangent, ids, table, vectors, shards, zs):
    n = 4 * zs
    rows, width = latents.shape
    s = len(STREAMS)
    DMA = pltpu.SemaphoreType.DMA
    shape = {k: ((width, rows) if k in TALL else (rows, width), BF) for k in SAVED}
    shape["w"] = ((6, n, shards[0].shape[0], width), BF)
    shape["mid"] = ((rows, width), F32)
    shape["inv"] = ((2, rows, 128), F32)
    shape["probs"] = ((24, LAT, LAT), BF)
    for k in ("lat", "cot", "one", "two"):
        shape[k] = ((rows, width), BF)
    shape["hb"] = shape["fulls"] = ((8, width), F32)
    names = ("w",) + SAVED + ("mid", "inv", "probs")
    got = pl.pallas_call(
        functools.partial(forward_kernel, zs),
        out_shape=[jax.ShapeDtypeStruct(*shape[k]) for k in names],
        in_specs=[pl.BlockSpec(memory_space=pl.ANY)] * 2 + [pl.BlockSpec(memory_space=pltpu.SMEM)]
        + [pl.BlockSpec(memory_space=pltpu.VMEM)] * 9 + [pl.BlockSpec(memory_space=pl.ANY)] * 6,
        out_specs=[pl.BlockSpec(memory_space=pl.ANY)] * len(names),
        scratch_shapes=[pltpu.VMEM(*shape[k]) for k in names + ("lat", "cot", "one", "two", "hb", "fulls")] + [
            DMA((s, 2, zs)), DMA((s, zs)), DMA((s,)), DMA((s, zs)), DMA((s,)), DMA((s, zs)), DMA((s,)), DMA((s,)),
            DMA((6,)), DMA((2, 3)), DMA((24,)), DMA((2,)),
        ],
        compiler_params=pltpu.CompilerParams(collective_id=0, has_side_effects=True, vmem_limit_bytes=62 << 20),
        name="gather_and_forward",
    )(latents, cotangent, ids, table, *vectors, *shards)
    return dict(zip(names, got))


NAMES_TWO = ("pool", "tall", "flat", "mg", "probs", "inv", "yb", "sm", "rc", "rb", "rzm", "rzf", "ram", "raf", "arc", "arp", "arz", "tot")


class Scatter:
    def __init__(self, p, g, bufs, outs, sems, middle):
        self.p, self.g, self.middle, self.outs = p, g, middle, outs
        self.rc, self.rb = bufs["rc"], bufs["rb"]
        self.rz, self.ra = (bufs["rzf"], bufs["rzm"]), (bufs["raf"], bufs["ram"])
        (self.csend, self.crecv, self.bsend, self.brecv, self.zsend, self.zrecv, self.asend, self.arecv, self.credit) = sems
        self.cols = pl.ds(pl.multiple_of(p.c * 640, 128), 640)
        self.others = pl.ds(pl.multiple_of((1 - p.c) * 640, 128), 640)

    def plane(self, t):
        val = jnp.int32(FAR[0][t])
        for s in range(1, self.p.zs):
            val = jnp.where(self.p.z == s, FAR[s][t], val)
        return val

    def own(self, k, j):
        return self.g(k).at[pl.ds(pl.multiple_of(j * 80, 80), 80), self.cols]

    def move(self, src, dst, dev, ssem, rsem):
        pltpu.make_async_remote_copy(src, dst, ssem, rsem, device_id=dev, device_id_type=MESH).start()

    def wait(self, ref, sem):
        pltpu.make_async_copy(ref, ref, sem).wait()

    def add(self, ref, val):
        ref[...] = ref[...] + val

    def group(self, t):
        return pl.ds(pl.multiple_of(self.plane(t) * 320, 320), 320)

    def c_send(self, k, t):
        p = self.p
        if k >= 3 and t == 0:
            pl.semaphore_wait(self.credit, 1)
        rows = self.group(t)
        self.move(self.g(k).at[rows, self.others], self.rc.at[k % 3, rows], (p.i, 1 - p.c), self.csend.at[k], self.crecv.at[k, self.plane(t)])

    def c_arrive(self, k, t):
        p = self.p
        zz = self.plane(t)
        rows = self.group(t)
        src = self.rc.at[k % 3, rows]
        self.wait(src, self.crecv.at[k, zz])
        self.add(self.g(k).at[rows, self.cols], src[...])
        if k < 3 and t == 3:
            pl.semaphore_signal(self.credit, inc=1, device_id=(p.i, 1 - p.c), device_id_type=MESH)
        away = zz * 4 + (1 - p.b) * p.sb
        for n, j in enumerate((away, away + p.sa)):
            self.move(self.own(k, j), self.rb.at[k, zz * 2 + n], (p.ib, p.c), self.bsend.at[k], self.brecv.at[k, zz])

    def b_arrive(self, k, t):
        p = self.p
        zz = self.plane(t)
        self.wait(self.rb.at[k, pl.ds(zz * 2, 2)], self.brecv.at[k, zz])
        base = zz * 4 + p.b * p.sb
        for n, j in enumerate((base, base + p.sa)):
            self.add(self.own(k, j), self.rb[k, zz * 2 + n])
        if not self.middle[k]:
            self.move(self.own(k, base + (1 - p.a) * p.sa), self.ra[0].at[k // 2, zz], (p.ia, p.c), self.asend.at[k], self.arecv.at[k, zz])

    def a_arrive(self, k, t):
        p = self.p
        zz = self.plane(t)
        src = self.ra[0].at[k // 2, zz]
        self.wait(src, self.arecv.at[k, zz])
        self.add(self.own(k, zz * 4 + p.b * p.sb + p.a * p.sa), src[...])

    def members(self, k, zz):
        p = self.p
        base = zz * 4 + p.b * p.sb
        return (base, base + p.sa) if self.middle[k] else (base + p.a * p.sa,)

    def slot(self, zz, up, end):
        return zz if up or not end else self.p.zs

    def landing(self, k, zz, up, end):
        return self.rz[self.middle[k]].at[k // 2, self.slot(zz, up, end)]

    def z_take(self, k, zz, up, end):
        src = self.landing(k, zz, up, end)
        self.wait(src, self.zrecv.at[k, self.slot(zz, up, end)])
        for q, j in enumerate(self.members(k, zz)):
            self.add(self.own(k, j), src[q * 80:(q + 1) * 80])

    def z_pass(self, k, zz, up, end):
        p = self.p
        dev = (p.up if up else p.down, p.c)
        for q, j in enumerate(self.members(k, zz)):
            self.move(self.own(k, j), self.landing(k, zz, up, end).at[pl.ds(q * 80, 80)], dev, self.zsend.at[k, zz],
                      self.zrecv.at[k, self.slot(zz, up, end)])

    def z_step(self, k, d):
        p = self.p

        @pl.when(p.z + d <= p.zs - 1)
        def _():
            if d < p.zs - 1:
                pl.when(p.has_down)(lambda: self.z_take(k, p.z + d, True, False))
            self.z_pass(k, p.z + d, True, d == 1)

        @pl.when(p.z - d >= 0)
        def _():
            if d < p.zs - 1:
                pl.when(p.has_up)(lambda: self.z_take(k, p.z - d, False, False))
            self.z_pass(k, p.z - d, False, d == 1)

    def z_end(self, k):
        p = self.p
        pl.when(p.has_down)(lambda: self.z_take(k, p.z, True, True))
        pl.when(p.has_up)(lambda: self.z_take(k, p.z, False, True))
        if self.middle[k]:
            base = p.z * 4 + p.b * p.sb
            self.move(self.own(k, base + (1 - p.a) * p.sa), self.ra[1].at[k // 2], (p.ia, p.c), self.asend.at[k], self.arecv.at[k, 0])
        else:
            self.outs[k][...] = self.own(k, p.i)[...].astype(F32)

    def finish(self, k):
        src = self.ra[1].at[k // 2]
        self.wait(src, self.arecv.at[k, 0])
        self.outs[k][...] = self.own(k, self.p.i)[...].astype(F32) + src[...].astype(F32)

    def drain(self, k):
        p = self.p
        self.wait(self.rc.at[k % 3], self.csend.at[k])
        self.wait(self.rb.at[k], self.bsend.at[k])
        self.wait(self.ra[self.middle[k]].at[k // 2], self.asend.at[k])
        for zz in range(p.zs):
            @pl.when(p.z != zz)
            def _(zz=zz):
                self.wait(self.landing(k, zz, True, False), self.zsend.at[k, zz])


FAR = ((3, 2, 1, 0), (3, 0, 2, 1), (0, 3, 1, 2), (0, 1, 2, 3))
GRADS = ("down", "up", "out", "value", "key", "query")


def backward_kernel(zs, *refs):
    ids, gain_one, gain_two, b_down = refs[:4]
    ins = dict(zip(("w",) + SAVED + ("mid", "inv", "probs", "cot"), refs[4:20]))
    outs = refs[20:26]
    res_out, lat_out, sm_out = refs[26:29]
    bufs = dict(zip(NAMES_TWO, refs[29:47]))
    rsems = refs[47:56]
    lsem, osem, tsem = refs[56:59]
    p = Place(zs)
    pool, tall, flat, mg, probs, inv, yb, sm = (bufs[n] for n in NAMES_TWO[:8])
    tokens = 768
    seat = (2, 3, 4, 5, 2, 3)
    s = Scatter(p, lambda k: pool.at[seat[k]], bufs, outs, rsems, SUM_MIDDLE)
    count = [0]

    def load(src, dst):
        assert count[0] < lsem.shape[0]
        cp = pltpu.make_async_copy(src, dst, lsem.at[count[0]])
        count[0] += 1
        cp.start()
        return cp

    def slot(n, i=None):
        return flat.at[pl.ds(n * tokens, tokens)] if i is None else flat.at[pl.ds(n * tokens + i * LAT, LAT)]

    hid, pre, cot, u2, att, ky = range(6)
    ag, bg, qy, vy, u1 = hid, pre, cot, u2, att
    ready = {}

    def fetch(name, src, dst):
        ready[name] = load(src, dst)

    def need(name):
        cp = ready.pop(name, None)
        if cp is not None:
            cp.wait()

    fetch("hid", ins["hid"], slot(hid))
    fetch("cot_t", ins["cot_t"], tall.at[0])
    fetch("wd", ins["w"].at[5], pool.at[0])
    fetch("cot", ins["cot"], slot(cot))
    fetch("pre", ins["slope"], slot(pre))
    fetch("two_t", ins["two_t"], tall.at[1])
    fetch("wu", ins["w"].at[4], pool.at[1])
    fetch("u2", ins["u2"], slot(u2))
    fetch("inv", ins["inv"], inv)
    fetch("att", ins["att"], slot(att))
    fetch("ky", ins["k"], slot(ky))
    fetch("probs", ins["probs"], probs)
    sm[...] = jnp.zeros(sm.shape, F32)
    p.barrier_wide()
    results = []

    def col_sum(row, val):
        sm[row:row + 1, :] += jnp.sum(val, axis=0, keepdims=True)

    def blocks(i, f):
        def body(r, carry):
            f(pl.ds(pl.multiple_of(r * 64, 64), 64), pl.multiple_of(i * LAT + r * 64, 64))
            return carry
        lax.fori_loop(0, 4, body, 0)

    def at(n, start, size=64):
        return flat.at[pl.ds(n * tokens + start, size)]

    left = {"g0": (0, hid), "g1": (1, pre), "g2": (0, att), "g3": (1, vy), "g4": (1, ky), "g5": (1, qy)}
    before = (("hid", "cot_t"), ("two_t",), ("att",), ("one_t",), (), ())

    def grad(k, t):
        if t == 0:
            for n in before[k]:
                need(n)
            if k >= 4:
                s.drain(k - 4)
        a, b = left["g%d" % k]
        rows = s.group(t)
        pool[seat[k], rows, :] = nn(tall[a, rows, :], slot(b)[...]).astype(BF)
        s.c_send(k, t)

    def unit_p(i):
        for n in ("wd", "cot", "pre"):
            need(n)
        yb[...] = nn(slot(cot, i)[...], pool[0])

        def f(r, start):
            ref = at(pre, start)
            v = (yb[r, :] * ref[...].astype(F32)).astype(BF)
            ref[...] = v
            col_sum(2, v.astype(F32))
            col_sum(4, at(cot, start)[...].astype(F32))

        blocks(i, f)

    def unit_n(i):
        for n in ("wd", "hid", "mid%d" % i):
            need(n)
        yb[...] = nt(slot(vy, i)[...], pool[0])

        def f(r, start):
            at(vy, start)[...] = (mg[pl.ds(start, 64), :] + (yb[r, :] + b_down[...].astype(F32)[None, :])).astype(BF)

        blocks(i, f)
        cp = pltpu.make_async_copy(slot(vy, i), res_out.at[item_rows(i)], osem.at[i])
        cp.start()
        results.append(cp)

    def norm_back(r, n, unit, start, gain_row, shift_row, gain):
        y = yb[r, :]
        v = unit[...].astype(F32)
        sc = y * gain
        m1 = jnp.mean(sc, axis=1, keepdims=True)
        m2 = jnp.mean(sc * v, axis=1, keepdims=True)
        col_sum(gain_row, y * v)
        col_sum(shift_row, y)
        iv = inv[n, pl.ds(start, 64), :][:, 0:1]
        return (sc - m1 - v * m2) * iv

    def unit_t(i):
        for n in ("wu", "u2", "inv"):
            need(n)
        yb[...] = nt(slot(pre, i)[...], pool[1])

        def f(r, start):
            back = norm_back(r, 1, at(u2, start), start, 7, 8, gain_two[...].astype(F32)[None, :])
            m = at(cot, start)[...].astype(F32) + back
            mg[pl.ds(start, 64), :] = m
            b = m.astype(BF)
            at(bg, start)[...] = b
            col_sum(3, b.astype(F32))

        blocks(i, f)
        if i == 0:
            fetch("wo", ins["w"].at[3], pool.at[0])
        tall[0, :, item_rows(i)] = slot(bg, i)[...].T
        if i == 2:
            fetch("wv", ins["w"].at[2], pool.at[1])
            fetch("qy", ins["q"], slot(qy))
            fetch("vy", ins["v"], slot(vy))
            fetch("one_t", ins["one_t"], tall.at[1])

    def unit_y(i):
        need("wo")
        slot(ag, i)[...] = nn(slot(bg, i)[...], pool[0]).astype(BF)
        if i == 2:
            fetch("wk", ins["w"].at[1], pool.at[0])

    def unit_w(half):
        def f(i):
            for n in ("qy", "vy", "ky", "probs"):
                need(n)
            zero = jnp.zeros((), BF)
            accs = [[None] * 5 for _ in range(3)]
            qr, kr, vr, gr = slot(qy, i), slot(ky, i), slot(vy, i), slot(ag, i)
            for hh in range(4):
                lanes = pl.ds(half * 640 + hh * 128, 256)
                mask = head_window(hh)
                gm = jnp.where(mask, gr[:, lanes], zero)
                pb = probs[i * 8 + half * 4 + hh]
                dp = nt(gm, vr[:, lanes])
                pf = pb.astype(F32)
                inner = jnp.sum(dp * pf, axis=1, keepdims=True)
                ds = (pf * (dp - inner)).astype(BF)
                dv = tn(pb, gm)
                dq = nn(ds, jnp.where(mask, kr[:, lanes], zero)) * (HS ** -0.5)
                dk = tn(ds, jnp.where(mask, qr[:, lanes], zero)) * (HS ** -0.5)
                for acc, val in zip(accs, (dq, dk, dv)):
                    for t in (0, 1):
                        piece = val[:, t * 128:(t + 1) * 128]
                        acc[hh + t] = piece if acc[hh + t] is None else acc[hh + t] + piece
            for acc, ref, row in zip(accs, (qr, kr, vr), (0, None, 1)):
                for t in range(5):
                    lanes = pl.ds(half * 640 + t * 128, 128)
                    b = acc[t].astype(BF)
                    ref[:, lanes] = b
                    if row is not None:
                        sm[row:row + 1, lanes] += jnp.sum(b.astype(F32), axis=0, keepdims=True)
            if i == 2 and half == 1:
                fetch("wq", ins["w"].at[0], flat.at[pl.ds(0, 1280)])
                fetch("u1", ins["u1"], slot(u1))
        return f

    def unit_s(i):
        for n in ("wq", "wk", "wv", "u1"):
            need(n)
        yb[...] = nt(slot(qy, i)[...], flat[0:1280, :])
        yb[...] += nt(slot(ky, i)[...], pool[0])
        yb[...] += nt(slot(vy, i)[...], pool[1])
        mark = lax.broadcasted_iota(jnp.int32, (16, 1), 0) == ids[i]

        def f(r, start):
            back = norm_back(r, 0, at(u1, start), start, 5, 6, gain_one[...].astype(F32)[None, :])
            g = mg[pl.ds(start, 64), :] + back
            at(qy, start)[...] = g.astype(BF)
            total = jnp.sum(g, axis=0, keepdims=True)
            sm[16:32, :] += jnp.where(mark, total, 0.0)

        blocks(i, f)
        fetch("mid%d" % i, ins["mid"].at[item_rows(i)], mg.at[item_rows(i)])
        if i == 2:
            fetch("wd", ins["w"].at[5], pool.at[0])
            fetch("hid", ins["hid"], slot(vy))
        cp = pltpu.make_async_copy(slot(qy, i), lat_out.at[item_rows(i)], osem.at[3 + i])
        cp.start()
        results.append(cp)

    arc, arp, arz, tot = (bufs[n] for n in ("arc", "arp", "arz", "tot"))
    pair = (p.i, 1 - p.c)
    me = p.i % 4
    mine = pl.ds(pl.multiple_of(me * 8, 8), 8)

    def others(count, self_at, f):
        for j in range(count):
            pl.when(self_at != j)(functools.partial(f, j))

    def copy(src, dst, dev, n, m):
        return pltpu.make_async_remote_copy(src, dst, tsem.at[n], tsem.at[m], device_id=dev, device_id_type=MESH)

    def local(ref, n):
        pltpu.make_async_copy(ref, ref, tsem.at[n]).wait()

    def total(n):
        half = sm.at[mine, s.cols]
        if n == 0:
            copy(sm.at[:, s.others], arc, pair, 0, 1).start()
        elif n == 1:
            local(arc, 1)
            sm[:, s.cols] += arc[...]
            others(4, me, lambda j: copy(sm.at[pl.ds(8 * j, 8), s.cols], arp.at[me], (p.i - me + j, p.c), 2, 4 + me).start())
            arp[me] = half[...]
        elif n == 2:
            others(4, me, lambda j: local(arp.at[j], 4 + j))
            arz[p.z] = arp[0] + arp[1] + arp[2] + arp[3]
            others(zs, p.z, lambda j: copy(arz.at[p.z], arz.at[p.z], (4 * j + me, p.c), 3, 8 + p.z).start())
        elif n == 3:
            others(zs, p.z, lambda j: local(arz.at[j], 8 + j))
            tot[mine, s.cols] = arz[0] + arz[1] + arz[2] + arz[3]
            part = tot.at[mine, s.cols]
            others(4, me, lambda j: copy(part, part, (p.i - me + j, p.c), 12, 16 + me).start())
        elif n == 4:
            others(4, me, lambda j: local(tot.at[pl.ds(8 * j, 8), s.cols], 16 + j))
            copy(tot.at[:, s.cols], tot.at[:, s.cols], pair, 13, 14).start()
        else:
            local(arc, 14)
            sm_out[...] = tot[...]
            local(arc, 0)
            three = pl.ds(0, 3)
            local(arp.at[three], 2)
            local(arp.at[three], 3)
            local(arp.at[three], 12)
            local(arc, 13)

    units = (unit_p, unit_n, unit_t, unit_y, unit_w(0), unit_w(1), unit_s, total)
    for code in ORDER_TWO:
        kind, k, t = code // 100, code // 10 % 10, code % 10
        if kind == 0:
            units[k](t)
        elif kind == 1:
            grad(k, t)
        elif kind == 2:
            s.c_arrive(k, t)
        elif kind == 3:
            s.b_arrive(k, t)
        elif kind == 4:
            s.a_arrive(k, t)
        elif kind == 5:
            s.z_step(k, t)
        elif kind == 6:
            s.z_step(k, t)
        elif kind == 7:
            s.z_end(k)
        elif kind == 8:
            s.z_end(k)
        else:
            s.finish(k)
    for k in range(2, 6):
        s.drain(k)
    for cp in results:
        cp.wait()


def backward(r, cotangent, ids, vectors, zs):
    rows, width = cotangent.shape
    DMA = pltpu.SemaphoreType.DMA
    n = 4 * zs
    grow = width // n
    half = width // 2
    ins = [r["w"].reshape(6, width, width)] + [r[k] for k in SAVED] + [r["mid"], r["inv"], r["probs"], cotangent]
    shapes = dict(
        pool=((6, width, width), BF), tall=((2, width, rows), BF), flat=((6 * rows, width), BF), mg=((rows, width), F32),
        probs=((24, LAT, LAT), BF), inv=((2, rows, 128), F32), yb=((LAT, width), F32), sm=((32, width), F32),
        rc=((3, width, half), BF), rb=((6, 2 * zs, grow, half), BF), rzm=((3, zs + 1, 2 * grow, half), BF),
        rzf=((3, zs + 1, grow, half), BF), ram=((3, grow, half), BF), raf=((3, zs, grow, half), BF),
        arc=((32, half), F32), arp=((4, 8, half), F32), arz=((zs, 8, half), F32), tot=((32, width), F32))
    ANY, VM = pl.BlockSpec(memory_space=pl.ANY), pl.BlockSpec(memory_space=pltpu.VMEM)
    return pl.pallas_call(
        functools.partial(backward_kernel, zs),
        out_shape=[jax.ShapeDtypeStruct((grow, half), F32)] * 6 + [jax.ShapeDtypeStruct((rows, width), BF)] * 2
        + [jax.ShapeDtypeStruct((32, width), F32)],
        in_specs=[pl.BlockSpec(memory_space=pltpu.SMEM)] + [VM] * 3 + [ANY] * len(ins),
        out_specs=[VM] * 6 + [ANY] * 2 + [VM],
        scratch_shapes=[pltpu.VMEM(*shapes[k]) for k in NAMES_TWO] + [
            DMA((6,)), DMA((6, zs)), DMA((6,)), DMA((6, zs)), DMA((6, zs)), DMA((6, zs + 1)), DMA((6,)), DMA((6, zs)),
            pltpu.SemaphoreType.REGULAR, DMA((32,)), DMA((6,)), DMA((20,)),
        ],
        compiler_params=pltpu.CompilerParams(collective_id=1, has_side_effects=True, vmem_limit_bytes=63 << 20),
        name="backward_and_scatter",
    )(ids, *vectors, *ins)


def hand_out_kernel(*refs):
    small, table, wide, narrow = refs[8], refs[17], refs[18:24], refs[24:27]
    stage, isem, osem = refs[27:35], refs[35], refs[36]
    copies = [(pltpu.make_async_copy(a, v, isem.at[n]), pltpu.make_async_copy(v, b, osem.at[n]))
              for n, (a, v, b) in enumerate(zip(refs[:8], stage, refs[9:17]))]
    for cp, _ in copies:
        cp.start()
    table[...] = small[16:32, :]
    for n, ref in enumerate(wide):
        ref[...] = small[3 + n:4 + n, :].reshape(ref.shape)
    half = narrow[0].shape[0]
    c = lax.axis_index("head")
    cols = pl.ds(pl.multiple_of(c * half, 128), half)
    for n, ref in enumerate(narrow):
        ref[...] = small[n:n + 1, cols].reshape(ref.shape)
    for cp, back in copies:
        cp.wait()
        back.start()
    for _, back in copies:
        back.wait()


def hand_out(large, small):
    width = small.shape[1]
    ANY, VM = pl.BlockSpec(memory_space=pl.ANY), pl.BlockSpec(memory_space=pltpu.VMEM)
    n = len(large)
    like = [jax.ShapeDtypeStruct(a.shape, a.dtype) for a in large]
    return pl.pallas_call(
        hand_out_kernel,
        out_shape=like + [jax.ShapeDtypeStruct((16, width), F32)]
        + [jax.ShapeDtypeStruct((width,), F32)] * 6 + [jax.ShapeDtypeStruct((width // 2,), F32)] * 3,
        in_specs=[ANY] * n + [VM],
        out_specs=[ANY] * n + [VM] * 10,
        scratch_shapes=[pltpu.VMEM(a.shape, a.dtype) for a in large] + [pltpu.SemaphoreType.DMA((n,))] * 2,
        compiler_params=pltpu.CompilerParams(vmem_limit_bytes=63 << 20),
        name="hand_out",
    )(*large, small)


def in_blocks(x, dim, length):
    before, after = (x.shape[:dim], x.shape[dim + 1 :])
    return jnp.moveaxis(x.reshape(*before, length, -1, *after), dim, 0)


def sent_and_summed(x, axis, dim):
    tiles = in_blocks(x, dim, lax.axis_size(axis))
    arrived = lax.all_to_all(tiles, axis, split_axis=0, concat_axis=0, tiled=True)
    return arrived.astype(jnp.float32).sum(axis=0)


def side_by_side(arrays, axis, dim, along):
    ends, at = ([], 0)
    for a in arrays[:-1]:
        at += a.shape[along]
        ends.append(at)
    both = jnp.concatenate(arrays, axis=along)
    return tuple(jnp.split(sent_and_summed(both, axis, dim), ends, axis=along))


def norm_forward(row_block, norm_gain, norm_shift):
    row_mean = jnp.mean(row_block, axis=1, keepdims=True)
    centered = row_block - row_mean
    row_var = jnp.mean(centered * centered, axis=1, keepdims=True)
    inverse = lax.rsqrt(row_var + EPSILON)
    normed = centered * inverse
    return (normed * norm_gain + norm_shift, normed, inverse)


def norm_backward(grad_rows, normed, inverse, norm_gain):
    scaled = grad_rows * norm_gain
    first_moment = jnp.mean(scaled, axis=1, keepdims=True)
    second_moment = jnp.mean(scaled * normed, axis=1, keepdims=True)
    grad_input = (scaled - first_moment - normed * second_moment) * inverse
    return (grad_input, jnp.sum(grad_rows * normed, axis=0), jnp.sum(grad_rows, axis=0))


def contract_rows(left, right):
    return lax.dot_general(
        left, right, (((0,), (0,)), ((), ())), preferred_element_type=jnp.float32
    )


def contract_cols(left, right):
    return lax.dot_general(
        left, right, (((1,), (1,)), ((), ())), preferred_element_type=jnp.float32
    )


def split_heads(matrix):
    item_count = matrix.shape[0] // LAT
    return matrix.reshape(item_count, LAT, matrix.shape[1] // HS, HS)


def attend_forward(query_rows, key_rows, value_rows):
    factor = HS ** (-0.5)
    scores = (
        jnp.einsum(
            "iqhc,ikhc->ihqk",
            split_heads(query_rows),
            split_heads(key_rows),
            preferred_element_type=jnp.float32,
        )
        * factor
    )
    row_max = jnp.max(scores, axis=-1, keepdims=True)
    exp_scores = jnp.exp(scores - row_max)
    row_total = jnp.sum(exp_scores, axis=-1, keepdims=True)
    soft_probs = (exp_scores / row_total).astype(jnp.bfloat16)
    attended = jnp.einsum(
        "ihqk,ikhc->iqhc", soft_probs, split_heads(value_rows), preferred_element_type=jnp.float32
    )
    return (attended.reshape(query_rows.shape).astype(jnp.bfloat16), row_max + jnp.log(row_total))


def attend_backward(query_rows, key_rows, value_rows, log_total, attended_grad):
    factor = HS ** (-0.5)
    query_heads = split_heads(query_rows)
    key_heads = split_heads(key_rows)
    value_heads = split_heads(value_rows)
    grad_heads = split_heads(attended_grad)
    scores = (
        jnp.einsum("iqhc,ikhc->ihqk", query_heads, key_heads, preferred_element_type=jnp.float32)
        * factor
    )
    soft_probs = jnp.exp(scores - log_total)
    value_grad = jnp.einsum(
        "ihqk,iqhc->ikhc",
        soft_probs.astype(jnp.bfloat16),
        grad_heads,
        preferred_element_type=jnp.float32,
    )
    probs_grad = jnp.einsum(
        "iqhc,ikhc->ihqk", grad_heads, value_heads, preferred_element_type=jnp.float32
    )
    inner_sum = jnp.sum(probs_grad * soft_probs, axis=-1, keepdims=True)
    score_grad = (soft_probs * (probs_grad - inner_sum)).astype(jnp.bfloat16)
    query_grad = (
        jnp.einsum("ihqk,ikhc->iqhc", score_grad, key_heads, preferred_element_type=jnp.float32)
        * factor
    )
    key_grad = (
        jnp.einsum("ihqk,iqhc->ikhc", score_grad, query_heads, preferred_element_type=jnp.float32)
        * factor
    )
    full_shape = query_rows.shape
    return (
        query_grad.reshape(full_shape).astype(jnp.bfloat16),
        key_grad.reshape(full_shape).astype(jnp.bfloat16),
        value_grad.reshape(full_shape).astype(jnp.bfloat16),
    )


def gelu_value(pre_act):
    return 0.5 * pre_act * (1.0 + lax.erf(pre_act * ROOT_HALF))


def gelu_slope(pre_act):
    return (
        0.5 * (1.0 + lax.erf(pre_act * ROOT_HALF))
        + pre_act * jnp.exp(-0.5 * pre_act * pre_act) * INV_ROOT_TWO_PI
    )


def place_slot(piece, head_index, full_len):
    empty = jnp.zeros((full_len,), jnp.float32)
    return lax.dynamic_update_slice_in_dim(empty, piece, head_index * piece.shape[0], 0)


def on_any_mesh(
    latents,
    lang_ids,
    lang_table,
    gain_one,
    shift_one,
    w_query,
    b_query,
    w_key,
    w_value,
    b_value,
    w_out,
    b_out,
    gain_two,
    shift_two,
    w_up,
    b_up,
    w_down,
    b_down,
    cotangent,
):
    own_rows = latents.shape[0]
    model_width = latents.shape[1]
    item_count = lang_ids.shape[0]
    head_index = lax.axis_index("head")
    head_count = lax.axis_size("head")
    w_query, w_key, w_value, w_up, w_out, w_down = (
        lax.all_gather(w_query, "dp", axis=0, tiled=True),
        lax.all_gather(w_key, "dp", axis=0, tiled=True),
        lax.all_gather(w_value, "dp", axis=0, tiled=True),
        lax.all_gather(w_up, "dp", axis=0, tiled=True),
        lax.all_gather(w_out, "dp", axis=1, tiled=True),
        lax.all_gather(w_down, "dp", axis=1, tiled=True),
    )
    one_hot = (lang_ids[:, None] == jnp.arange(LANGS, dtype=jnp.int32)[None, :]).astype(jnp.float32)
    embedded = jnp.dot(one_hot, lang_table, precision=HIGHEST)
    start_rows = (
        latents.astype(jnp.float32).reshape(item_count, LAT, model_width) + embedded[:, None, :]
    ).reshape(own_rows, model_width)
    gain_first = gain_one.astype(jnp.float32)
    gain_second = gain_two.astype(jnp.float32)
    normed_one, unit_one, inverse_one = norm_forward(
        start_rows, gain_first, shift_one.astype(jnp.float32)
    )
    input_one = normed_one.astype(jnp.bfloat16)
    group_one = lax.all_gather(input_one, "head", axis=0, tiled=True)
    query_rows = (
        jnp.dot(group_one, w_query, preferred_element_type=jnp.float32)
        + b_query.astype(jnp.float32)
    ).astype(jnp.bfloat16)
    key_rows = jnp.dot(group_one, w_key, preferred_element_type=jnp.float32).astype(jnp.bfloat16)
    value_rows = (
        jnp.dot(group_one, w_value, preferred_element_type=jnp.float32)
        + b_value.astype(jnp.float32)
    ).astype(jnp.bfloat16)
    attended, log_total = attend_forward(query_rows, key_rows, value_rows)
    attn_branch = lax.psum_scatter(
        jnp.dot(attended, w_out, preferred_element_type=jnp.float32),
        "head",
        scatter_dimension=0,
        tiled=True,
    )
    middle_rows = start_rows + (attn_branch + b_out.astype(jnp.float32))
    normed_two, unit_two, inverse_two = norm_forward(
        middle_rows, gain_second, shift_two.astype(jnp.float32)
    )
    input_two = normed_two.astype(jnp.bfloat16)
    group_two = lax.all_gather(input_two, "head", axis=0, tiled=True)
    pre_act = jnp.dot(group_two, w_up, preferred_element_type=jnp.float32) + b_up.astype(
        jnp.float32
    )
    hidden = gelu_value(pre_act).astype(jnp.bfloat16)
    down_branch = lax.psum_scatter(
        jnp.dot(hidden, w_down, preferred_element_type=jnp.float32).astype(jnp.bfloat16),
        "head",
        scatter_dimension=0,
        tiled=True,
    ).astype(jnp.float32)
    result = (middle_rows + (down_branch + b_down.astype(jnp.float32))).astype(jnp.bfloat16)
    group_cot = lax.all_gather(cotangent, "head", axis=0, tiled=True)
    grad_w_down = contract_rows(hidden, group_cot)
    grad_b_down = jnp.sum(cotangent.astype(jnp.float32), axis=0)
    pre_grad = (contract_cols(group_cot, w_down) * gelu_slope(pre_act)).astype(jnp.bfloat16)
    grad_w_up = contract_rows(group_two, pre_grad)
    grad_b_up = jnp.sum(pre_grad.astype(jnp.float32), axis=0)
    grad_two = lax.psum_scatter(
        contract_cols(pre_grad, w_up), "head", scatter_dimension=0, tiled=True
    )
    back_two, grad_gain_two, grad_shift_two = norm_backward(
        grad_two, unit_two, inverse_two, gain_second
    )
    middle_grad = cotangent.astype(jnp.float32) + back_two
    branch_grad = middle_grad.astype(jnp.bfloat16)
    grad_b_out = jnp.sum(branch_grad.astype(jnp.float32), axis=0)
    group_branch = lax.all_gather(branch_grad, "head", axis=0, tiled=True)
    grad_w_out = contract_rows(attended, group_branch)
    attended_grad = contract_cols(group_branch, w_out).astype(jnp.bfloat16)
    query_grad, key_grad, value_grad = attend_backward(
        query_rows, key_rows, value_rows, log_total, attended_grad
    )
    grad_w_query = contract_rows(group_one, query_grad)
    grad_w_key = contract_rows(group_one, key_grad)
    grad_w_value = contract_rows(group_one, value_grad)
    grad_b_query = jnp.sum(query_grad.astype(jnp.float32), axis=0)
    grad_b_value = jnp.sum(value_grad.astype(jnp.float32), axis=0)
    total_term = contract_cols(query_grad, w_query)
    total_term = total_term + contract_cols(key_grad, w_key)
    grad_one = lax.psum_scatter(
        (total_term + contract_cols(value_grad, w_value)).astype(jnp.bfloat16),
        "head",
        scatter_dimension=0,
        tiled=True,
    ).astype(jnp.float32)
    back_one, grad_gain_one, grad_shift_one = norm_backward(
        grad_one, unit_one, inverse_one, gain_first
    )
    start_grad = middle_grad + back_one
    latents_grad = start_grad.astype(jnp.bfloat16)
    item_sums = jnp.sum(start_grad.reshape(item_count, LAT, model_width), axis=1)
    grad_table = jnp.dot(one_hot.T, item_sums, precision=HIGHEST)
    full_b_query = place_slot(grad_b_query, head_index, model_width)
    full_b_value = place_slot(grad_b_value, head_index, model_width)
    full_b_up = place_slot(grad_b_up, head_index, FF)
    grad_w_query, grad_w_key, grad_w_value, grad_w_up, grad_w_out, grad_w_down = (
        *side_by_side(
            (
                grad_w_query.astype(jnp.bfloat16),
                grad_w_key.astype(jnp.bfloat16),
                grad_w_value.astype(jnp.bfloat16),
                grad_w_up.astype(jnp.bfloat16),
            ),
            "dp",
            0,
            1,
        ),
        *side_by_side(
            (grad_w_out.astype(jnp.bfloat16), grad_w_down.astype(jnp.bfloat16)), "dp", 1, 0
        ),
    )
    summed = lax.psum(
        (
            full_b_query,
            full_b_value,
            full_b_up,
            grad_b_out,
            grad_b_down,
            grad_gain_one,
            grad_shift_one,
            grad_gain_two,
            grad_shift_two,
            grad_table,
        ),
        ("dp", "head"),
    )
    local_width = model_width // head_count
    local_hidden = FF // head_count
    out_b_query = lax.dynamic_slice_in_dim(summed[0], head_index * local_width, local_width, 0)
    out_b_value = lax.dynamic_slice_in_dim(summed[1], head_index * local_width, local_width, 0)
    out_b_up = lax.dynamic_slice_in_dim(summed[2], head_index * local_hidden, local_hidden, 0)
    return (
        result,
        latents_grad,
        summed[9],
        summed[5],
        summed[6],
        grad_w_query,
        out_b_query,
        grad_w_key,
        grad_w_value,
        out_b_value,
        grad_w_out,
        summed[3],
        summed[7],
        summed[8],
        grad_w_up,
        out_b_up,
        grad_w_down,
        summed[4],
    )


def on_device(
    latents, lang_ids, lang_table, gain_one, shift_one, w_query, b_query, w_key, w_value, b_value, w_out, b_out,
    gain_two, shift_two, w_up, b_up, w_down, b_down, cotangent,
):
    zs = lax.axis_size("dp") // 4
    r = forward(
        latents, cotangent, lang_ids, lang_table, (gain_one, shift_one, gain_two, shift_two, b_out, b_query, b_value, b_up),
        (w_query, w_key, w_value, w_out.T, w_up, w_down.T), zs)
    *large, small = backward(r, cotangent, lang_ids, (gain_one, gain_two, b_down), zs)
    got = hand_out(large, small)
    down, up, out, value, key, query, result, latents_grad, table = got[:9]
    b_out_g, b_down_g, gain_one_g, shift_one_g, gain_two_g, shift_two_g = got[9:15]
    b_query_g, b_value_g, b_up_g = got[15:]
    return (
        result, latents_grad, table, gain_one_g, shift_one_g, query, b_query_g, key, value, b_value_g, out.T, b_out_g,
        gain_two_g, shift_two_g, up, b_up_g, down.T, b_down_g,
    )

def solution(mesh):
    in_specs = (
        P(("dp", "head"), None),
        P(("dp", "head")),
        P(),
        P(),
        P(),
        P("dp", "head"),
        P("head"),
        P("dp", "head"),
        P("dp", "head"),
        P("head"),
        P("head", "dp"),
        P(),
        P(),
        P(),
        P("dp", "head"),
        P("head"),
        P("head", "dp"),
        P(),
        P(("dp", "head"), None),
    )
    out_specs = (
        P(("dp", "head"), None),
        P(("dp", "head"), None),
        P(),
        P(),
        P(),
        P("dp", "head"),
        P("head"),
        P("dp", "head"),
        P("dp", "head"),
        P("head"),
        P("head", "dp"),
        P(),
        P(),
        P(),
        P("dp", "head"),
        P("head"),
        P("head", "dp"),
        P(),
    )
    fast = mesh.shape["dp"] == 16 and mesh.shape["head"] == 2
    return jax.shard_map(
        on_device if fast else on_any_mesh, mesh=mesh, in_specs=in_specs, out_specs=out_specs, check_vma=False
    )
```

```python
import functools
import jax
import jax.numpy as jnp
from jax import lax
from jax.experimental import pallas as pl
from jax.experimental.pallas import tpu as pltpu
from jax.sharding import PartitionSpec as P

MESH = pl.DeviceIdType.MESH
BF = jnp.bfloat16
F32 = jnp.float32
HS = 160
LAT = 256
LANGS = 16
EPSILON = 1e-05
HIGHEST = lax.Precision.HIGHEST
ROOT_HALF = 0.7071067811865476
INV_ROOT_TWO_PI = 0.3989422804014327
FF = 1280


class Place:
    def __init__(self, zs):
        self.zs = zs
        i = lax.axis_index("dp")
        c = lax.axis_index("head")
        self.i, self.c = i, c
        self.z = i // 4
        self.sa = 1 + c
        self.sb = 2 - c
        x = i % 2
        y = (i // 2) % 2
        self.a = jnp.where(c == 0, x, y)
        self.b = jnp.where(c == 0, y, x)
        self.ia = i + self.sa * (1 - 2 * self.a)
        self.ib = i + self.sb * (1 - 2 * self.b)
        self.up = jnp.minimum(i + 4, 4 * zs - 1)
        self.down = jnp.maximum(i - 4, 0)
        self.has_up = self.z < zs - 1
        self.has_down = self.z > 0

    def barrier(self):
        bar = pltpu.get_barrier_semaphore()
        i, c = self.i, self.c
        for dev in ((self.ia, c), (self.ib, c), (i, 1 - c)):
            pl.semaphore_signal(bar, inc=1, device_id=dev, device_id_type=MESH)

        @pl.when(self.has_up)
        def _():
            pl.semaphore_signal(bar, inc=1, device_id=(self.up, c), device_id_type=MESH)

        @pl.when(self.has_down)
        def _():
            pl.semaphore_signal(bar, inc=1, device_id=(self.down, c), device_id_type=MESH)

        n = 3 + jnp.where(self.has_up, 1, 0) + jnp.where(self.has_down, 1, 0)
        pl.semaphore_wait(bar, n)

    def barrier_wide(self):
        bar = pltpu.get_barrier_semaphore()
        me = self.i % 4
        for n in range(8):
            @pl.when(jnp.logical_or(me != n // 2, self.c != n % 2))
            def _(n=n):
                pl.semaphore_signal(bar, inc=1, device_id=(self.i - me + n // 2, n % 2), device_id_type=MESH)
        for zz in range(self.zs):
            @pl.when(self.z != zz)
            def _(zz=zz):
                pl.semaphore_signal(bar, inc=1, device_id=(4 * zz + me, self.c), device_id_type=MESH)
        pl.semaphore_wait(bar, 6 + self.zs)


ORDER_ONE = (
    0, 20, 40, 60, 2, -2, 22, -13, 27, -1, 67, 80, 7, 28, 10, 30, 62, 42, 23, 11,
    29, 8, 25, 24, -3, 9, 47, 48, 12, 31, 13, 68, 33, 50, 32, 82, 1, -14, 21, 49,
    -4, -8, 69, 51, 100, 63, -7, -5, 53, 64, -9, 52, 65, 87, -6, 41, -11, -10, -17, 102,
    107, 70, -19, 88, 72, -12, -15, 71, 73, 90, 108, -16, -18, 91, 61, -20, -21, 110, 89, -23,
    109, 103, -22, 104, 92, 93, -24, 105, 81, -25, 111, -26, 112, 113, -27, 101,
)
ORDER_TWO = (
    100, 103, 101, 200, 0, 2, 102, 1, 202, 110, 300, 201, 20, 111, 503, 210, 113, 112, 80, 21,
    203, 81, 301, 22, 502, 310, 211, 82, 212, 30, 31, 302, 410, 613, 120, 122, 213, 311, 32, 220,
    501, 121, 303, 222, 40, 312, 41, 411, 313, 42, 51, 612, 700, 50, 123, 320, 221, 523, 412, 52,
    900, 140, 223, 413, 611, 130, 142, 240, 131, 321, 230, 60, 242, 141, 522, 810, 150, 340, 231, 151,
    330, 241, 322, 543, 153, 152, 90, 132, 331, 430, 633, 250, 521, 61, 232, 91, 431, 251, 143, 350,
    341, 542, 133, 252, 62, 243, 632, 92, 70, 351, 450, 653, 332, 253, 342, 541, 323, 352, 343, 11,
    233, 71, 451, 652, 432, 10, 631, 720, 353, 12, 740, 452, 72, 651, 333, 920, 940, 453, 433, 830,
    73, 850,
)
SUM_MIDDLE = (True, False) * 3


def nn(a, b):
    return lax.dot_general(a, b, (((1,), (0,)), ((), ())), preferred_element_type=F32)


def nt(a, b):
    return lax.dot_general(a, b, (((1,), (1,)), ((), ())), preferred_element_type=F32)


def tn(a, b):
    return lax.dot_general(a, b, (((0,), (0,)), ((), ())), preferred_element_type=F32)


def item_rows(i):
    return pl.ds(i * LAT, LAT)


def head_window(hh):
    at = lax.broadcasted_iota(jnp.int32, (1, 256), 1) + hh * 128
    return (at >= hh * HS) & (at < (hh + 1) * HS)


class Gather:
    def __init__(self, p, w, sems, streams):
        self.p, self.w, self.streams = p, w, streams
        self.zsend, self.zrecv, self.asend, self.arecv, self.bsend, self.brecv, self.csend, self.crecv = sems
        self.cols = pl.ds(pl.multiple_of(p.c * 640, 128), 640)

    def sub(self, s, j, n=None):
        k, mid, r0, rows = self.streams[s]
        return self.w.at[k, j if n is None else pl.ds(j, n), pl.ds(r0, rows), self.cols]

    def mid(self, s):
        return self.streams[s][1]

    def send(self, s, j, n, dev, ssem, rsem):
        ref = self.sub(s, j) if n == 1 else self.sub(s, j, n)
        pltpu.make_async_remote_copy(ref, ref, ssem, rsem, device_id=dev, device_id_type=MESH).start()

    def arrived(self, s, n, sem):
        ref = self.sub(s, 0, n)
        pltpu.make_async_copy(ref, ref, sem).wait()

    def members(self, s, zz):
        p = self.p
        base = zz * 4 + p.b * p.sb
        return (base, base + p.sa) if self.mid(s) else (base + p.a * p.sa,)

    def z_send(self, s, zz, upward):
        p = self.p
        dev, d = ((p.up, p.c), 0) if upward else ((p.down, p.c), 1)
        for j in self.members(s, zz):
            self.send(s, j, 1, dev, self.zsend.at[s, d, zz], self.zrecv.at[s, zz])

    def z_first(self, s):
        p = self.p
        pl.when(p.has_up)(lambda: self.z_send(s, p.z, True))
        pl.when(p.has_down)(lambda: self.z_send(s, p.z, False))

    def at_distance(self, d, f):
        p = self.p
        pl.when(p.z - d >= 0)(lambda: f(p.z - d, True))
        pl.when(p.z + d <= p.zs - 1)(lambda: f(p.z + d, False))

    def around(self, d, f):
        if d == 0:
            f(self.p.z)
        else:
            self.at_distance(d, lambda zz, below: f(zz))

    def z_arrive(self, s, d, then):
        p = self.p
        n = len(self.members(s, 0))

        def f(zz, below):
            self.arrived(s, n, self.zrecv.at[s, zz])
            if d < p.zs - 1:
                if below:
                    pl.when(p.has_up)(lambda: self.z_send(s, zz, True))
                else:
                    pl.when(p.has_down)(lambda: self.z_send(s, zz, False))
            then(s, zz)

        self.at_distance(d, f)

    def a_send(self, s, zz):
        p = self.p
        j = zz * 4 + p.b * p.sb + p.a * p.sa
        self.send(s, j, 1, (p.ia, p.c), self.asend.at[s], self.arecv.at[s, zz])

    def a_arrive(self, s, zz, then):
        self.arrived(s, 1, self.arecv.at[s, zz])
        then(s, zz)

    def b_send(self, s, zz):
        p = self.p
        base = zz * 4 + p.b * p.sb
        for j in (base, base + p.sa):
            self.send(s, j, 1, (p.ib, p.c), self.bsend.at[s], self.brecv.at[s, zz])

    def b_arrive(self, s, zz):
        p = self.p
        self.arrived(s, 2, self.brecv.at[s, zz])
        self.send(s, zz * 4, 4, (p.i, 1 - p.c), self.csend.at[s], self.crecv.at[s])

    def do(self, s, ev):
        p = self.p
        if ev == 0:
            if not self.mid(s):
                self.z_first(s)
            self.a_send(s, p.z)
        elif ev == 1:
            self.arrived(s, 4 * p.zs, self.crecv.at[s])
        elif ev >= 10:
            self.around(ev - 10, lambda zz: self.b_arrive(s, zz))
        elif ev >= 6:
            self.z_arrive(s, ev - 6, self.b_send if self.mid(s) else self.a_send)
        elif self.mid(s):
            self.arrived(s, 1, self.arecv.at[s, p.z])
            self.z_first(s)
            self.b_send(s, p.z)
        else:
            self.around(ev - 2, lambda zz: self.a_arrive(s, zz, self.b_send))

    def drain(self, s):
        p = self.p
        n = len(self.members(s, 0))
        for zz in range(p.zs):
            @pl.when(jnp.logical_and(p.has_up, zz <= p.z))
            def _(zz=zz):
                self.arrived(s, n, self.zsend.at[s, 0, zz])

            @pl.when(jnp.logical_and(p.has_down, zz >= p.z))
            def _(zz=zz):
                self.arrived(s, n, self.zsend.at[s, 1, zz])
        self.arrived(s, 1 if self.mid(s) else p.zs, self.asend.at[s])
        self.arrived(s, 2 * p.zs, self.bsend.at[s])
        self.arrived(s, 4 * p.zs, self.csend.at[s])


STREAMS = tuple((k, k % 2 == 0, 0, 80) for k in range(6))
SAVED = ("ot", "q", "k", "v", "att", "hid", "slope", "tt", "ct", "u1", "u2")
TALL = ("ot", "tt", "ct")


def forward_kernel(zs, *refs):
    lat_in, cot_in, ids, table_in = refs[:4]
    vectors, shards = refs[4:12], refs[12:18]
    at = 18
    outs = dict(zip(("w",) + SAVED + ("mid", "inv", "pr"), refs[at:at + 15]))
    at += 15
    bufs = dict(zip(("w",) + SAVED + ("mid", "inv", "pr", "lat", "cot", "one", "two", "hb", "fulls", "table", "vec", "half"), refs[at:at + 24]))
    at += 24
    gsems = refs[at:at + 8]
    own, load, save, hsem, vsem = refs[at + 8:at + 13]
    p = Place(zs)
    w = bufs["w"]
    g = Gather(p, w, gsems, STREAMS)
    hb = bufs["hb"]
    copies = [pltpu.make_async_copy(shards[k], w.at[k, p.i, :, g.cols], own.at[k]) for k in range(6)]
    for cp in copies:
        cp.start()
    loads = [pltpu.make_async_copy(src.at[item_rows(i)], bufs[n].at[item_rows(i)], load.at[j, i])
             for j, (src, n) in enumerate(((lat_in, "lat"), (cot_in, "cot"))) for i in range(3)]
    for cp in loads:
        cp.start()
    fulls, table, vec, half = (bufs[n] for n in ("fulls", "table", "vec", "half"))
    places = [table] + list(vec) + list(half)
    short = [pltpu.make_async_copy(a, b, vsem.at[n]) for n, (a, b) in enumerate(zip((table_in,) + vectors, places))]
    for cp in short:
        cp.start()
    p.barrier()
    for cp in short:
        cp.wait()
    for n in range(5):
        fulls[n:n + 1, :] = row_of(vec[n])
    for n in range(3):
        hb[n:n + 1, g.cols] = row_of(half[n])
    half_send = pltpu.make_async_remote_copy(hb.at[:, g.cols], hb.at[:, g.cols], hsem.at[0], hsem.at[1],
                                             device_id=(p.i, 1 - p.c), device_id_type=MESH)
    half_send.start()
    names = ("w",) + SAVED + ("mid", "inv", "pr")
    saves = []

    def keep(name, index=None):
        src, dst = bufs[name], outs[name]
        if index is not None:
            src, dst = src.at[index], dst.at[index]
        n = len(saves)
        assert n < save.shape[0]
        cp = pltpu.make_async_copy(src, dst, save.at[n])
        cp.start()
        saves.append(cp)

    def start_of(i):
        return bufs["lat"][item_rows(i)].astype(F32) + table[pl.ds(ids[i], 1), :]

    def norm(v):
        mean = jnp.mean(v, axis=1, keepdims=True)
        cen = v - mean
        inv = lax.rsqrt(jnp.mean(cen * cen, axis=1, keepdims=True) + EPSILON)
        return cen * inv, inv

    def norm_rows(i, n, rows_of, u_name, out_name, tall_name):
        gain, shift = fulls[2 * n:2 * n + 1, :], fulls[2 * n + 1:2 * n + 2, :]

        def body(r, carry):
            rows = pl.ds(pl.multiple_of(i * LAT + r * 64, 64), 64)
            unit, inv = norm(rows_of(rows))
            bufs[u_name][rows, :] = unit.astype(BF)
            bufs[out_name][rows, :] = (unit * gain + shift).astype(BF)
            bufs["inv"][n, rows, :] = jnp.broadcast_to(inv, (64, 128))
            return carry

        lax.fori_loop(0, 4, body, 0)
        bufs[tall_name][:, item_rows(i)] = bufs[out_name][item_rows(i), :].T

    def whole(k):
        return w[k].reshape(1280, 1280)

    def ln1(i):
        loads[i].wait()
        emb = table[pl.ds(ids[i], 1), :]
        norm_rows(i, 0, lambda rows: bufs["lat"][rows, :].astype(F32) + emb, "u1", "one", "ot")

    def project(name, k, bias):
        def f(i):
            y = nn(bufs["one"][item_rows(i), :], whole(k))
            if bias is not None:
                y = y + hb[bias:bias + 1, :]
            bufs[name][item_rows(i), :] = y.astype(BF)
        return f

    def cot(i):
        loads[3 + i].wait()
        bufs["ct"][:, item_rows(i)] = bufs["cot"][item_rows(i), :].T

    def attend(half):
        def f(i):
            rows = item_rows(i)
            zero = jnp.zeros((), BF)
            acc = [None] * 5
            for hh in range(4):
                lanes = pl.ds(half * 640 + hh * 128, 256)
                mask = head_window(hh)
                qm = jnp.where(mask, bufs["q"][rows, lanes], zero)
                s = nt(qm, bufs["k"][rows, lanes]) * (HS ** -0.5)
                e = jnp.exp(s - jnp.max(s, axis=1, keepdims=True))
                pr = (e / jnp.sum(e, axis=1, keepdims=True)).astype(BF)
                bufs["pr"][i * 8 + half * 4 + hh] = pr
                vm = jnp.where(mask, bufs["v"][rows, lanes], zero)
                a = nn(pr, vm)
                for t in (0, 1):
                    piece = a[:, t * 128:(t + 1) * 128]
                    acc[hh + t] = piece if acc[hh + t] is None else acc[hh + t] + piece
            for t in range(5):
                bufs["att"][rows, pl.ds(half * 640 + t * 128, 128)] = acc[t].astype(BF)
        return f

    def out(i):
        rows = item_rows(i)
        emb = table[pl.ds(ids[i], 1), :]
        y = nt(bufs["att"][rows, :], whole(3))
        bufs["mid"][rows, :] = y + fulls[4:5, :] + (bufs["lat"][rows, :].astype(F32) + emb)
        norm_rows(i, 1, lambda r: bufs["mid"][r, :], "u2", "two", "tt")

    def up(i):
        rows = item_rows(i)
        pre = nn(bufs["two"][rows, :], whole(4)) + hb[2:3, :]
        cdf = 0.5 * (1.0 + lax.erf(pre * ROOT_HALF))
        bufs["hid"][rows, :] = (pre * cdf).astype(BF)
        bufs["slope"][rows, :] = (cdf + pre * jnp.exp(-0.5 * pre * pre) * INV_ROOT_TWO_PI).astype(BF)

    units = (ln1, project("q", 0, 0), project("k", 1, None), project("v", 2, 1), cot, attend(0), attend(1), out, up)
    after = (("u1", "ot"), ("q",), ("k",), ("v",), ("ct",), (), ("att", "pr"), ("u2", "tt", "mid", "inv"), ("hid", "slope"))
    seen, full = set(), {}
    for code in ORDER_ONE:
        if code < 0:
            n, i = (-code - 1) // 3, (-code - 1) % 3
            if n == 1 and i == 0:
                half_send.wait_recv()
            units[n](i)
            if i == 2:
                for name in after[n]:
                    keep(name)
            continue
        s, ev = code // 20, code % 20
        k = STREAMS[s][0]
        if k not in seen:
            copies[k].wait()
            seen.add(k)
        g.do(s, ev)
        if ev == 1:
            full[k] = full.get(k, 0) + 1
            if full[k] == sum(t[0] == k for t in STREAMS):
                keep("w", k)
    half_send.wait_send()
    for s in range(len(STREAMS)):
        g.drain(s)
    for cp in saves:
        cp.wait()


def forward(latents, cotangent, ids, table, vectors, shards, zs):
    n = 4 * zs
    rows, width = latents.shape
    s = len(STREAMS)
    DMA = pltpu.SemaphoreType.DMA
    shape = {k: ((width, rows) if k in TALL else (rows, width), BF) for k in SAVED}
    shape["w"] = ((6, n, shards[0].shape[0], width), BF)
    shape["mid"] = ((rows, width), F32)
    shape["inv"] = ((2, rows, 128), F32)
    shape["pr"] = ((24, LAT, LAT), BF)
    for k in ("lat", "cot", "one", "two"):
        shape[k] = ((rows, width), BF)
    shape["hb"] = shape["fulls"] = ((8, width), F32)
    shape["table"] = ((LANGS, width), F32)
    names = ("w",) + SAVED + ("mid", "inv", "pr")
    got = pl.pallas_call(
        functools.partial(forward_kernel, zs),
        out_shape=[jax.ShapeDtypeStruct(*shape[k]) for k in names],
        in_specs=[pl.BlockSpec(memory_space=pl.ANY)] * 2 + [pl.BlockSpec(memory_space=pltpu.SMEM)]
        + [pl.BlockSpec(memory_space=pl.ANY)] * 15,
        out_specs=[pl.BlockSpec(memory_space=pl.ANY)] * len(names),
        scratch_shapes=[pltpu.VMEM(*shape[k]) for k in names + ("lat", "cot", "one", "two", "hb", "fulls", "table")] + [
            [pltpu.VMEM((width,), BF)] * 5, [pltpu.VMEM((width // 2,), BF)] * 3,
            DMA((s, 2, zs)), DMA((s, zs)), DMA((s,)), DMA((s, zs)), DMA((s,)), DMA((s, zs)), DMA((s,)), DMA((s,)),
            DMA((6,)), DMA((2, 3)), DMA((24,)), DMA((2,)), DMA((9,)),
        ],
        compiler_params=pltpu.CompilerParams(collective_id=0, has_side_effects=True, vmem_limit_bytes=62 << 20),
        name="gather_and_forward",
    )(latents, cotangent, ids, table, *vectors, *shards)
    return dict(zip(names, got))


NAMES_TWO = ("pool", "tall", "flat", "mg", "pr", "inv", "yb", "sm", "rc", "rb", "rzm", "rzf", "ram", "raf", "arp", "arz", "tot", "gouts", "vecs")


class Scatter:
    def __init__(self, p, g, bufs, outs, sems, middle):
        self.p, self.g, self.middle, self.outs = p, g, middle, outs
        self.rc, self.rb = bufs["rc"], bufs["rb"]
        self.rz, self.ra = (bufs["rzf"], bufs["rzm"]), (bufs["raf"], bufs["ram"])
        (self.csend, self.crecv, self.bsend, self.brecv, self.zsend, self.zrecv, self.asend, self.arecv, self.credit) = sems
        self.cols = pl.ds(pl.multiple_of(p.c * 640, 128), 640)
        self.others = pl.ds(pl.multiple_of((1 - p.c) * 640, 128), 640)

    def plane(self, t):
        val = jnp.int32(FAR[0][t])
        for s in range(1, self.p.zs):
            val = jnp.where(self.p.z == s, FAR[s][t], val)
        return val

    def own(self, k, j):
        return self.g(k).at[pl.ds(pl.multiple_of(j * 80, 80), 80), self.cols]

    def move(self, src, dst, dev, ssem, rsem):
        pltpu.make_async_remote_copy(src, dst, ssem, rsem, device_id=dev, device_id_type=MESH).start()

    def wait(self, ref, sem):
        pltpu.make_async_copy(ref, ref, sem).wait()

    def add(self, ref, val):
        ref[...] = ref[...] + val

    def group(self, t):
        return pl.ds(pl.multiple_of(self.plane(t) * 320, 320), 320)

    def c_send(self, k, t):
        p = self.p
        if k >= 3 and t == 0:
            pl.semaphore_wait(self.credit.at[k % 3], 1)
        rows = self.group(t)
        self.move(self.g(k).at[rows, self.others], self.rc.at[k % 3, rows], (p.i, 1 - p.c), self.csend.at[k], self.crecv.at[k, self.plane(t)])

    def c_arrive(self, k, t):
        p = self.p
        zz = self.plane(t)
        rows = self.group(t)
        src = self.rc.at[k % 3, rows]
        self.wait(src, self.crecv.at[k, zz])
        self.add(self.g(k).at[rows, self.cols], src[...])
        if k < 3 and t == 3:
            pl.semaphore_signal(self.credit.at[k], inc=1, device_id=(p.i, 1 - p.c), device_id_type=MESH)
        away = zz * 4 + (1 - p.b) * p.sb
        for n, j in enumerate((away, away + p.sa)):
            self.move(self.own(k, j), self.rb.at[k, zz * 2 + n], (p.ib, p.c), self.bsend.at[k], self.brecv.at[k, zz])

    def b_arrive(self, k, t):
        p = self.p
        zz = self.plane(t)
        self.wait(self.rb.at[k, pl.ds(zz * 2, 2)], self.brecv.at[k, zz])
        base = zz * 4 + p.b * p.sb
        for n, j in enumerate((base, base + p.sa)):
            self.add(self.own(k, j), self.rb[k, zz * 2 + n])
        if not self.middle[k]:
            self.move(self.own(k, base + (1 - p.a) * p.sa), self.ra[0].at[k // 2, zz], (p.ia, p.c), self.asend.at[k], self.arecv.at[k, zz])

    def a_arrive(self, k, t):
        p = self.p
        zz = self.plane(t)
        src = self.ra[0].at[k // 2, zz]
        self.wait(src, self.arecv.at[k, zz])
        self.add(self.own(k, zz * 4 + p.b * p.sb + p.a * p.sa), src[...])

    def members(self, k, zz):
        p = self.p
        base = zz * 4 + p.b * p.sb
        return (base, base + p.sa) if self.middle[k] else (base + p.a * p.sa,)

    def slot(self, zz, up, end):
        return zz if up or not end else self.p.zs

    def landing(self, k, zz, up, end):
        return self.rz[self.middle[k]].at[k // 2, self.slot(zz, up, end)]

    def z_take(self, k, zz, up, end):
        src = self.landing(k, zz, up, end)
        self.wait(src, self.zrecv.at[k, self.slot(zz, up, end)])
        for q, j in enumerate(self.members(k, zz)):
            self.add(self.own(k, j), src[q * 80:(q + 1) * 80])

    def z_pass(self, k, zz, up, end):
        p = self.p
        dev = (p.up if up else p.down, p.c)
        for q, j in enumerate(self.members(k, zz)):
            self.move(self.own(k, j), self.landing(k, zz, up, end).at[pl.ds(q * 80, 80)], dev, self.zsend.at[k, zz],
                      self.zrecv.at[k, self.slot(zz, up, end)])

    def z_step(self, k, d):
        p = self.p

        @pl.when(p.z + d <= p.zs - 1)
        def _():
            if d < p.zs - 1:
                pl.when(p.has_down)(lambda: self.z_take(k, p.z + d, True, False))
            self.z_pass(k, p.z + d, True, d == 1)

        @pl.when(p.z - d >= 0)
        def _():
            if d < p.zs - 1:
                pl.when(p.has_up)(lambda: self.z_take(k, p.z - d, False, False))
            self.z_pass(k, p.z - d, False, d == 1)

    def z_end(self, k):
        p = self.p
        pl.when(p.has_down)(lambda: self.z_take(k, p.z, True, True))
        pl.when(p.has_up)(lambda: self.z_take(k, p.z, False, True))
        if self.middle[k]:
            base = p.z * 4 + p.b * p.sb
            self.move(self.own(k, base + (1 - p.a) * p.sa), self.ra[1].at[k // 2], (p.ia, p.c), self.asend.at[k], self.arecv.at[k, 0])
        else:
            self.outs[k][...] = self.own(k, p.i)[...].astype(F32)

    def finish(self, k):
        src = self.ra[1].at[k // 2]
        self.wait(src, self.arecv.at[k, 0])
        self.outs[k][...] = self.own(k, self.p.i)[...].astype(F32) + src[...].astype(F32)

    def drain(self, k):
        p = self.p
        self.wait(self.rc.at[k % 3], self.csend.at[k])
        self.wait(self.rb.at[k], self.bsend.at[k])
        self.wait(self.ra[self.middle[k]].at[k // 2], self.asend.at[k])
        for zz in range(p.zs):
            @pl.when(p.z != zz)
            def _(zz=zz):
                self.wait(self.landing(k, zz, True, False), self.zsend.at[k, zz])


FAR = ((3, 2, 1, 0), (3, 0, 2, 1), (0, 3, 1, 2), (0, 1, 2, 3))
GRADS = ("down", "up", "out", "value", "key", "query")


def row_of(ref):
    return ref[...].astype(F32)[None, :]


def backward_kernel(zs, *refs):
    ids = refs[0]
    ins = dict(zip(("w",) + SAVED + ("mid", "inv", "pr", "cot"), refs[4:20]))
    outs = refs[20:26]
    res_out, lat_out, sm_out = refs[26:29]
    bufs = dict(zip(NAMES_TWO, refs[29:48]))
    rsems = refs[48:57]
    lsem, osem, tsem = refs[57:60]
    gain_one, gain_two, b_down = bufs["vecs"]
    p = Place(zs)
    pool, tall, flat, mg, probs, inv, yb, sm = (bufs[n] for n in NAMES_TWO[:8])
    tokens = 768
    seat = (2, 3, 4, 5, 2, 3)
    s = Scatter(p, lambda k: pool.at[seat[k]], bufs, [bufs["gouts"].at[k] for k in range(6)], rsems, SUM_MIDDLE)
    count = [0]

    def load(src, dst):
        assert count[0] < lsem.shape[0]
        cp = pltpu.make_async_copy(src, dst, lsem.at[count[0]])
        count[0] += 1
        cp.start()
        return cp

    def slot(n, i=None):
        return flat.at[pl.ds(n * tokens, tokens)] if i is None else flat.at[pl.ds(n * tokens + i * LAT, LAT)]

    hid, pre, cot, u2, att, ky = range(6)
    ag, bg, qy, vy, u1 = hid, pre, cot, u2, att
    ready = {}

    def fetch(name, src, dst):
        ready[name] = load(src, dst)

    def need(name):
        cp = ready.pop(name, None)
        if cp is not None:
            cp.wait()

    fetch("hid", ins["hid"], slot(hid))
    fetch("ct", ins["ct"], tall.at[0])
    fetch("wd", ins["w"].at[5], pool.at[0])
    fetch("cot", ins["cot"], slot(cot))
    fetch("pre", ins["slope"], slot(pre))
    fetch("tt", ins["tt"], tall.at[1])
    fetch("wu", ins["w"].at[4], pool.at[1])
    fetch("u2", ins["u2"], slot(u2))
    fetch("inv", ins["inv"], inv)
    fetch("att", ins["att"], slot(att))
    fetch("ky", ins["k"], slot(ky))
    fetch("pr", ins["pr"], probs)
    for n, name in enumerate(("g1", "g2", "bd")):
        fetch(name, refs[1 + n], bufs["vecs"][n])
    sm[...] = jnp.zeros(sm.shape, F32)
    p.barrier_wide()
    results = []

    def give(src, dst, n):
        cp = pltpu.make_async_copy(src, dst, osem.at[n])
        cp.start()
        results.append(cp)

    def col_sum(row, val):
        sm[row:row + 1, :] += jnp.sum(val, axis=0, keepdims=True)

    def blocks(i, f):
        def body(r, carry):
            f(pl.ds(pl.multiple_of(r * 64, 64), 64), pl.multiple_of(i * LAT + r * 64, 64))
            return carry
        lax.fori_loop(0, 4, body, 0)

    def at(n, start, size=64):
        return flat.at[pl.ds(n * tokens + start, size)]

    left = {"g0": (0, hid), "g1": (1, pre), "g2": (0, att), "g3": (1, vy), "g4": (1, ky), "g5": (1, qy)}
    before = (("hid", "ct"), ("tt",), ("att",), ("ot",), ("ot",), ("ot",))

    def grad(k, t):
        if t == 0:
            for n in before[k]:
                need(n)
            if k >= 4:
                s.drain(k - 4)
        a, b = left["g%d" % k]
        rows = s.group(t)
        pool[seat[k], rows, :] = nn(tall[a, rows, :], slot(b)[...]).astype(BF)
        s.c_send(k, t)

    def unit_p(i):
        for n in ("wd", "cot", "pre"):
            need(n)
        yb[...] = nn(slot(cot, i)[...], pool[0])

        def f(r, start):
            ref = at(pre, start)
            v = (yb[r, :] * ref[...].astype(F32)).astype(BF)
            ref[...] = v
            col_sum(2, v.astype(F32))
            col_sum(4, at(cot, start)[...].astype(F32))

        blocks(i, f)

    def unit_n(i):
        for n in ("wd", "hid", "bd", "mid%d" % i):
            need(n)
        yb[...] = nt(slot(vy, i)[...], pool[0])

        def f(r, start):
            at(vy, start)[...] = (mg[pl.ds(start, 64), :] + (yb[r, :] + row_of(b_down))).astype(BF)

        blocks(i, f)
        give(slot(vy, i), res_out.at[item_rows(i)], i)

    def norm_back(r, n, unit, start, gain_row, shift_row, gain):
        y = yb[r, :]
        v = unit[...].astype(F32)
        sc = y * gain
        m1 = jnp.mean(sc, axis=1, keepdims=True)
        m2 = jnp.mean(sc * v, axis=1, keepdims=True)
        col_sum(gain_row, y * v)
        col_sum(shift_row, y)
        iv = inv[n, pl.ds(start, 64), :][:, 0:1]
        return (sc - m1 - v * m2) * iv

    def unit_t(i):
        for n in ("wu", "u2", "inv", "g2"):
            need(n)
        yb[...] = nt(slot(pre, i)[...], pool[1])
        if i == 0:
            fetch("wo", ins["w"].at[3], pool.at[0])

    def unit_u(i):
        def f(r, start):
            back = norm_back(r, 1, at(u2, start), start, 7, 8, row_of(gain_two))
            m = at(cot, start)[...].astype(F32) + back
            mg[pl.ds(start, 64), :] = m
            b = m.astype(BF)
            at(bg, start)[...] = b
            col_sum(3, b.astype(F32))

        blocks(i, f)
        tall[0, :, item_rows(i)] = slot(bg, i)[...].T
        if i == 2:
            fetch("wv", ins["w"].at[2], pool.at[1])
            fetch("qy", ins["q"], slot(qy))
            fetch("vy", ins["v"], slot(vy))
            fetch("ot", ins["ot"], tall.at[1])

    def unit_y(i):
        need("wo")
        slot(ag, i)[...] = nn(slot(bg, i)[...], pool[0]).astype(BF)
        if i == 2:
            fetch("wk", ins["w"].at[1], pool.at[0])

    def unit_w(half):
        def f(i):
            for n in ("qy", "vy", "ky", "pr"):
                need(n)
            zero = jnp.zeros((), BF)
            accs = [[None] * 5 for _ in range(3)]
            qr, kr, vr, gr = slot(qy, i), slot(ky, i), slot(vy, i), slot(ag, i)
            for hh in range(4):
                lanes = pl.ds(half * 640 + hh * 128, 256)
                mask = head_window(hh)
                gm = jnp.where(mask, gr[:, lanes], zero)
                pb = probs[i * 8 + half * 4 + hh]
                dp = nt(gm, vr[:, lanes])
                pf = pb.astype(F32)
                inner = jnp.sum(dp * pf, axis=1, keepdims=True)
                ds = (pf * (dp - inner)).astype(BF)
                dv = tn(pb, gm)
                dq = nn(ds, jnp.where(mask, kr[:, lanes], zero)) * (HS ** -0.5)
                dk = tn(ds, jnp.where(mask, qr[:, lanes], zero)) * (HS ** -0.5)
                for acc, val in zip(accs, (dq, dk, dv)):
                    for t in (0, 1):
                        piece = val[:, t * 128:(t + 1) * 128]
                        acc[hh + t] = piece if acc[hh + t] is None else acc[hh + t] + piece
            for acc, ref, row in zip(accs, (qr, kr, vr), (0, None, 1)):
                for t in range(5):
                    lanes = pl.ds(half * 640 + t * 128, 128)
                    b = acc[t].astype(BF)
                    ref[:, lanes] = b
                    if row is not None:
                        sm[row:row + 1, lanes] += jnp.sum(b.astype(F32), axis=0, keepdims=True)
            if i == 2 and half == 1:
                fetch("wq", ins["w"].at[0], flat.at[pl.ds(0, 1280)])
                fetch("u1", ins["u1"], slot(u1))
        return f

    def unit_s(i):
        for n in ("wq", "wk", "wv", "u1", "g1"):
            need(n)
        yb[...] = nt(slot(qy, i)[...], flat[0:1280, :]) + nt(slot(ky, i)[...], pool[0])

    def unit_q(i):
        yb[...] += nt(slot(vy, i)[...], pool[1])
        mark = lax.broadcasted_iota(jnp.int32, (16, 1), 0) == ids[i]

        def f(r, start):
            back = norm_back(r, 0, at(u1, start), start, 5, 6, row_of(gain_one))
            g = mg[pl.ds(start, 64), :] + back
            at(qy, start)[...] = g.astype(BF)
            total = jnp.sum(g, axis=0, keepdims=True)
            sm[16:32, :] += jnp.where(mark, total, 0.0)

        blocks(i, f)
        fetch("mid%d" % i, ins["mid"].at[item_rows(i)], mg.at[item_rows(i)])
        if i == 2:
            fetch("wd", ins["w"].at[5], pool.at[0])
            fetch("hid", ins["hid"], slot(vy))
        give(slot(qy, i), lat_out.at[item_rows(i)], 3 + i)

    arp, arz, tot = (bufs[n] for n in ("arp", "arz", "tot"))
    me = p.i % 4
    mine = pl.ds(pl.multiple_of(me * 8, 8), 8)

    def other_planes(f):
        for j in range(zs):
            pl.when(p.z != j)(functools.partial(f, j))

    def plane_mates(f):
        for n in range(8):
            j, q = n // 2, n % 2
            pl.when(jnp.logical_or(me != j, p.c != q))(functools.partial(f, j, q, n))

    def copy(src, dst, j, q, n, m):
        pltpu.make_async_remote_copy(src, dst, tsem.at[n], tsem.at[m], device_id=(j, q), device_id_type=MESH).start()

    def local(ref, n):
        pltpu.make_async_copy(ref, ref, tsem.at[n]).wait()

    def total(n):
        self_n = me * 2 + p.c
        piece = lambda j, q: tot.at[pl.ds(8 * j, 8), pl.ds(640 * q, 640)]
        if n == 0:
            plane_mates(lambda j, q, m: copy(sm.at[pl.ds(8 * j, 8), pl.ds(640 * q, 640)], arp.at[self_n], p.i - me + j, q, 0, 4 + self_n))
            arp[self_n] = sm[mine, s.cols]
        elif n == 1:
            plane_mates(lambda j, q, m: local(arp.at[m], 4 + m))
            arz[p.z] = ((arp[0] + arp[1]) + (arp[2] + arp[3])) + ((arp[4] + arp[5]) + (arp[6] + arp[7]))
            other_planes(lambda j: copy(arz.at[p.z], arz.at[p.z], 4 * j + me, p.c, 1, 12 + p.z))
        elif n == 2:
            other_planes(lambda j: local(arz.at[j], 12 + j))
            tot[mine, s.cols] = (arz[0] + arz[1]) + (arz[2] + arz[3])
            part = tot.at[mine, s.cols]
            plane_mates(lambda j, q, m: copy(part, part, p.i - me + j, q, 2, 16 + self_n))
        else:
            plane_mates(lambda j, q, m: local(piece(j, q), 16 + m))
            give(tot, sm_out, 12)
            local(arp.at[pl.ds(0, 7)], 0)
            local(arz.at[pl.ds(0, 3)], 1)
            local(arp.at[pl.ds(0, 7)], 2)

    units = (unit_p, unit_n, unit_t, unit_y, unit_w(0), unit_w(1), unit_s, total, unit_u, unit_q)
    for code in ORDER_TWO:
        kind, k, t = code // 100, code // 10 % 10, code % 10
        if kind == 0:
            units[k](t)
        elif kind == 1:
            grad(k, t)
        elif kind == 2:
            s.c_arrive(k, t)
        elif kind == 3:
            s.b_arrive(k, t)
        elif kind == 4:
            s.a_arrive(k, t)
        elif kind == 5:
            s.z_step(k, t)
        elif kind == 6:
            s.z_step(k, t)
        elif kind <= 8:
            s.z_end(k)
        else:
            s.finish(k)
        if kind >= 8:
            give(bufs["gouts"].at[k], outs[k], 6 + k)
    for k in range(2, 6):
        s.drain(k)
    for cp in results:
        cp.wait()


def backward(r, cotangent, ids, vectors, zs):
    rows, width = cotangent.shape
    DMA = pltpu.SemaphoreType.DMA
    n = 4 * zs
    grow = width // n
    half = width // 2
    ins = [r["w"].reshape(6, width, width)] + [r[k] for k in SAVED] + [r["mid"], r["inv"], r["pr"], cotangent]
    shapes = dict(
        pool=((6, width, width), BF), tall=((2, width, rows), BF), flat=((6 * rows, width), BF), mg=((rows, width), F32),
        pr=((24, LAT, LAT), BF), inv=((2, rows, 128), F32), yb=((LAT, width), F32), sm=((32, width), F32),
        rc=((3, width, half), BF), rb=((6, 2 * zs, grow, half), BF), rzm=((3, zs + 1, 2 * grow, half), BF),
        rzf=((3, zs + 1, grow, half), BF), ram=((3, grow, half), BF), raf=((3, zs, grow, half), BF),
        arp=((8, 8, half), F32), arz=((zs, 8, half), F32), tot=((32, width), F32),
        gouts=((6, grow, half), F32))
    ANY = pl.BlockSpec(memory_space=pl.ANY)
    return pl.pallas_call(
        functools.partial(backward_kernel, zs),
        out_shape=[jax.ShapeDtypeStruct((grow, half), F32)] * 6 + [jax.ShapeDtypeStruct((rows, width), BF)] * 2
        + [jax.ShapeDtypeStruct((32, width), F32)],
        in_specs=[pl.BlockSpec(memory_space=pltpu.SMEM)] + [ANY] * (3 + len(ins)),
        out_specs=[ANY] * 9,
        scratch_shapes=[pltpu.VMEM(*shapes[k]) for k in NAMES_TWO[:-1]] + [
            [pltpu.VMEM((width,), BF)] * 3,
            DMA((6,)), DMA((6, zs)), DMA((6,)), DMA((6, zs)), DMA((6, zs)), DMA((6, zs + 1)), DMA((6,)), DMA((6, zs)),
            pltpu.SemaphoreType.REGULAR((3,)), DMA((32,)), DMA((13,)), DMA((24,)),
        ],
        compiler_params=pltpu.CompilerParams(collective_id=1, has_side_effects=True, vmem_limit_bytes=63 << 20),
        name="backward_and_scatter",
    )(ids, *vectors, *ins)


def hand_out_kernel(large, *refs):
    ins, outs = refs[:large + 1], refs[large + 1:2 * large + 11]
    stage, sm, table, wide, narrow, isem, osem = refs[2 * large + 11:]
    half = narrow[0].shape[0]
    first = pltpu.make_async_copy(ins[large], sm, isem.at[0])
    first.start()
    copies = []
    for a, v, b in zip(ins, stage, outs):
        step = min(a.shape[0], LAT)
        for r in range(0, a.shape[0], step):
            rows, n = pl.ds(r, step), len(copies) + 1
            copies.append((pltpu.make_async_copy(a.at[rows], v.at[rows], isem.at[n]), pltpu.make_async_copy(v.at[rows], b.at[rows], osem.at[n])))
    copies.sort(key=lambda pair: -pair[0].src_ref.shape[0])
    for cp, _ in copies:
        cp.start()
    first.wait()
    table[...] = sm[16:32, :]
    back = [pltpu.make_async_copy(table, outs[large], osem.at[0])]
    for n in range(6):
        wide[n][...] = sm[3 + n:4 + n, :].reshape(wide[n].shape)
        back.append(pltpu.make_async_copy(wide[n], outs[large + 1 + n], osem.at[20 + n]))
    cols = pl.ds(pl.multiple_of(lax.axis_index("head") * half, 128), half)
    for n in range(3):
        narrow[n][...] = sm[n:n + 1, cols].reshape(half)
        back.append(pltpu.make_async_copy(narrow[n], outs[large + 7 + n], osem.at[26 + n]))
    for cp in back:
        cp.start()
    for cp, out in copies:
        cp.wait()
        out.start()
        back.append(out)
    for cp in back:
        cp.wait()


def hand_out(large, small):
    width = small.shape[1]
    ANY = pl.BlockSpec(memory_space=pl.ANY)
    n = len(large)
    like = [jax.ShapeDtypeStruct(a.shape, a.dtype) for a in large]
    return pl.pallas_call(
        functools.partial(hand_out_kernel, n),
        out_shape=like + [jax.ShapeDtypeStruct((16, width), F32)]
        + [jax.ShapeDtypeStruct((width,), F32)] * 6 + [jax.ShapeDtypeStruct((width // 2,), F32)] * 3,
        in_specs=[ANY] * (n + 1),
        out_specs=[ANY] * (n + 10),
        scratch_shapes=[[pltpu.VMEM(a.shape, a.dtype) for a in large], pltpu.VMEM(small.shape, F32), pltpu.VMEM((16, width), F32),
                        [pltpu.VMEM((width,), F32)] * 6, [pltpu.VMEM((width // 2,), F32)] * 3] + [pltpu.SemaphoreType.DMA((32,))] * 2,
        compiler_params=pltpu.CompilerParams(vmem_limit_bytes=63 << 20),
        name="hand_out",
    )(*large, small)


def in_blocks(x, dim, length):
    before, after = (x.shape[:dim], x.shape[dim + 1 :])
    return jnp.moveaxis(x.reshape(*before, length, -1, *after), dim, 0)


def sent_and_summed(x, axis, dim):
    tiles = in_blocks(x, dim, lax.axis_size(axis))
    arrived = lax.all_to_all(tiles, axis, split_axis=0, concat_axis=0, tiled=True)
    return arrived.astype(jnp.float32).sum(axis=0)


def side_by_side(arrays, axis, dim, along):
    ends, at = ([], 0)
    for a in arrays[:-1]:
        at += a.shape[along]
        ends.append(at)
    both = jnp.concatenate(arrays, axis=along)
    return tuple(jnp.split(sent_and_summed(both, axis, dim), ends, axis=along))


def norm_forward(row_block, norm_gain, norm_shift):
    row_mean = jnp.mean(row_block, axis=1, keepdims=True)
    centered = row_block - row_mean
    row_var = jnp.mean(centered * centered, axis=1, keepdims=True)
    inverse = lax.rsqrt(row_var + EPSILON)
    normed = centered * inverse
    return (normed * norm_gain + norm_shift, normed, inverse)


def norm_backward(grad_rows, normed, inverse, norm_gain):
    scaled = grad_rows * norm_gain
    first_moment = jnp.mean(scaled, axis=1, keepdims=True)
    second_moment = jnp.mean(scaled * normed, axis=1, keepdims=True)
    grad_input = (scaled - first_moment - normed * second_moment) * inverse
    return (grad_input, jnp.sum(grad_rows * normed, axis=0), jnp.sum(grad_rows, axis=0))


def contract_rows(left, right):
    return lax.dot_general(
        left, right, (((0,), (0,)), ((), ())), preferred_element_type=jnp.float32
    )


def contract_cols(left, right):
    return lax.dot_general(
        left, right, (((1,), (1,)), ((), ())), preferred_element_type=jnp.float32
    )


def split_heads(matrix):
    item_count = matrix.shape[0] // LAT
    return matrix.reshape(item_count, LAT, matrix.shape[1] // HS, HS)


def attend_forward(query_rows, key_rows, value_rows):
    factor = HS ** (-0.5)
    scores = (
        jnp.einsum(
            "iqhc,ikhc->ihqk",
            split_heads(query_rows),
            split_heads(key_rows),
            preferred_element_type=jnp.float32,
        )
        * factor
    )
    row_max = jnp.max(scores, axis=-1, keepdims=True)
    exp_scores = jnp.exp(scores - row_max)
    row_total = jnp.sum(exp_scores, axis=-1, keepdims=True)
    soft_probs = (exp_scores / row_total).astype(jnp.bfloat16)
    attended = jnp.einsum(
        "ihqk,ikhc->iqhc", soft_probs, split_heads(value_rows), preferred_element_type=jnp.float32
    )
    return (attended.reshape(query_rows.shape).astype(jnp.bfloat16), row_max + jnp.log(row_total))


def attend_backward(query_rows, key_rows, value_rows, log_total, attended_grad):
    factor = HS ** (-0.5)
    query_heads = split_heads(query_rows)
    key_heads = split_heads(key_rows)
    value_heads = split_heads(value_rows)
    grad_heads = split_heads(attended_grad)
    scores = (
        jnp.einsum("iqhc,ikhc->ihqk", query_heads, key_heads, preferred_element_type=jnp.float32)
        * factor
    )
    soft_probs = jnp.exp(scores - log_total)
    value_grad = jnp.einsum(
        "ihqk,iqhc->ikhc",
        soft_probs.astype(jnp.bfloat16),
        grad_heads,
        preferred_element_type=jnp.float32,
    )
    probs_grad = jnp.einsum(
        "iqhc,ikhc->ihqk", grad_heads, value_heads, preferred_element_type=jnp.float32
    )
    inner_sum = jnp.sum(probs_grad * soft_probs, axis=-1, keepdims=True)
    score_grad = (soft_probs * (probs_grad - inner_sum)).astype(jnp.bfloat16)
    query_grad = (
        jnp.einsum("ihqk,ikhc->iqhc", score_grad, key_heads, preferred_element_type=jnp.float32)
        * factor
    )
    key_grad = (
        jnp.einsum("ihqk,iqhc->ikhc", score_grad, query_heads, preferred_element_type=jnp.float32)
        * factor
    )
    full_shape = query_rows.shape
    return (
        query_grad.reshape(full_shape).astype(jnp.bfloat16),
        key_grad.reshape(full_shape).astype(jnp.bfloat16),
        value_grad.reshape(full_shape).astype(jnp.bfloat16),
    )


def gelu_value(pre_act):
    return 0.5 * pre_act * (1.0 + lax.erf(pre_act * ROOT_HALF))


def gelu_slope(pre_act):
    return (
        0.5 * (1.0 + lax.erf(pre_act * ROOT_HALF))
        + pre_act * jnp.exp(-0.5 * pre_act * pre_act) * INV_ROOT_TWO_PI
    )


def place_slot(piece, head_index, full_len):
    empty = jnp.zeros((full_len,), jnp.float32)
    return lax.dynamic_update_slice_in_dim(empty, piece, head_index * piece.shape[0], 0)


def on_any_mesh(
    latents,
    lang_ids,
    lang_table,
    gain_one,
    shift_one,
    w_query,
    b_query,
    w_key,
    w_value,
    b_value,
    w_out,
    b_out,
    gain_two,
    shift_two,
    w_up,
    b_up,
    w_down,
    b_down,
    cotangent,
):
    own_rows = latents.shape[0]
    model_width = latents.shape[1]
    item_count = lang_ids.shape[0]
    head_index = lax.axis_index("head")
    head_count = lax.axis_size("head")
    w_query, w_key, w_value, w_up, w_out, w_down = (
        lax.all_gather(w_query, "dp", axis=0, tiled=True),
        lax.all_gather(w_key, "dp", axis=0, tiled=True),
        lax.all_gather(w_value, "dp", axis=0, tiled=True),
        lax.all_gather(w_up, "dp", axis=0, tiled=True),
        lax.all_gather(w_out, "dp", axis=1, tiled=True),
        lax.all_gather(w_down, "dp", axis=1, tiled=True),
    )
    one_hot = (lang_ids[:, None] == jnp.arange(LANGS, dtype=jnp.int32)[None, :]).astype(jnp.float32)
    embedded = jnp.dot(one_hot, lang_table, precision=HIGHEST)
    start_rows = (
        latents.astype(jnp.float32).reshape(item_count, LAT, model_width) + embedded[:, None, :]
    ).reshape(own_rows, model_width)
    gain_first = gain_one.astype(jnp.float32)
    gain_second = gain_two.astype(jnp.float32)
    normed_one, unit_one, inverse_one = norm_forward(
        start_rows, gain_first, shift_one.astype(jnp.float32)
    )
    input_one = normed_one.astype(jnp.bfloat16)
    group_one = lax.all_gather(input_one, "head", axis=0, tiled=True)
    query_rows = (
        jnp.dot(group_one, w_query, preferred_element_type=jnp.float32)
        + b_query.astype(jnp.float32)
    ).astype(jnp.bfloat16)
    key_rows = jnp.dot(group_one, w_key, preferred_element_type=jnp.float32).astype(jnp.bfloat16)
    value_rows = (
        jnp.dot(group_one, w_value, preferred_element_type=jnp.float32)
        + b_value.astype(jnp.float32)
    ).astype(jnp.bfloat16)
    attended, log_total = attend_forward(query_rows, key_rows, value_rows)
    attn_branch = lax.psum_scatter(
        jnp.dot(attended, w_out, preferred_element_type=jnp.float32),
        "head",
        scatter_dimension=0,
        tiled=True,
    )
    middle_rows = start_rows + (attn_branch + b_out.astype(jnp.float32))
    normed_two, unit_two, inverse_two = norm_forward(
        middle_rows, gain_second, shift_two.astype(jnp.float32)
    )
    input_two = normed_two.astype(jnp.bfloat16)
    group_two = lax.all_gather(input_two, "head", axis=0, tiled=True)
    pre_act = jnp.dot(group_two, w_up, preferred_element_type=jnp.float32) + b_up.astype(
        jnp.float32
    )
    hidden = gelu_value(pre_act).astype(jnp.bfloat16)
    down_branch = lax.psum_scatter(
        jnp.dot(hidden, w_down, preferred_element_type=jnp.float32).astype(jnp.bfloat16),
        "head",
        scatter_dimension=0,
        tiled=True,
    ).astype(jnp.float32)
    result = (middle_rows + (down_branch + b_down.astype(jnp.float32))).astype(jnp.bfloat16)
    group_cot = lax.all_gather(cotangent, "head", axis=0, tiled=True)
    grad_w_down = contract_rows(hidden, group_cot)
    grad_b_down = jnp.sum(cotangent.astype(jnp.float32), axis=0)
    pre_grad = (contract_cols(group_cot, w_down) * gelu_slope(pre_act)).astype(jnp.bfloat16)
    grad_w_up = contract_rows(group_two, pre_grad)
    grad_b_up = jnp.sum(pre_grad.astype(jnp.float32), axis=0)
    grad_two = lax.psum_scatter(
        contract_cols(pre_grad, w_up), "head", scatter_dimension=0, tiled=True
    )
    back_two, grad_gain_two, grad_shift_two = norm_backward(
        grad_two, unit_two, inverse_two, gain_second
    )
    middle_grad = cotangent.astype(jnp.float32) + back_two
    branch_grad = middle_grad.astype(jnp.bfloat16)
    grad_b_out = jnp.sum(branch_grad.astype(jnp.float32), axis=0)
    group_branch = lax.all_gather(branch_grad, "head", axis=0, tiled=True)
    grad_w_out = contract_rows(attended, group_branch)
    attended_grad = contract_cols(group_branch, w_out).astype(jnp.bfloat16)
    query_grad, key_grad, value_grad = attend_backward(
        query_rows, key_rows, value_rows, log_total, attended_grad
    )
    grad_w_query = contract_rows(group_one, query_grad)
    grad_w_key = contract_rows(group_one, key_grad)
    grad_w_value = contract_rows(group_one, value_grad)
    grad_b_query = jnp.sum(query_grad.astype(jnp.float32), axis=0)
    grad_b_value = jnp.sum(value_grad.astype(jnp.float32), axis=0)
    total_term = contract_cols(query_grad, w_query)
    total_term = total_term + contract_cols(key_grad, w_key)
    grad_one = lax.psum_scatter(
        (total_term + contract_cols(value_grad, w_value)).astype(jnp.bfloat16),
        "head",
        scatter_dimension=0,
        tiled=True,
    ).astype(jnp.float32)
    back_one, grad_gain_one, grad_shift_one = norm_backward(
        grad_one, unit_one, inverse_one, gain_first
    )
    start_grad = middle_grad + back_one
    latents_grad = start_grad.astype(jnp.bfloat16)
    item_sums = jnp.sum(start_grad.reshape(item_count, LAT, model_width), axis=1)
    grad_table = jnp.dot(one_hot.T, item_sums, precision=HIGHEST)
    full_b_query = place_slot(grad_b_query, head_index, model_width)
    full_b_value = place_slot(grad_b_value, head_index, model_width)
    full_b_up = place_slot(grad_b_up, head_index, FF)
    grad_w_query, grad_w_key, grad_w_value, grad_w_up, grad_w_out, grad_w_down = (
        *side_by_side(
            (
                grad_w_query.astype(jnp.bfloat16),
                grad_w_key.astype(jnp.bfloat16),
                grad_w_value.astype(jnp.bfloat16),
                grad_w_up.astype(jnp.bfloat16),
            ),
            "dp",
            0,
            1,
        ),
        *side_by_side(
            (grad_w_out.astype(jnp.bfloat16), grad_w_down.astype(jnp.bfloat16)), "dp", 1, 0
        ),
    )
    summed = lax.psum(
        (
            full_b_query,
            full_b_value,
            full_b_up,
            grad_b_out,
            grad_b_down,
            grad_gain_one,
            grad_shift_one,
            grad_gain_two,
            grad_shift_two,
            grad_table,
        ),
        ("dp", "head"),
    )
    local_width = model_width // head_count
    local_hidden = FF // head_count
    out_b_query = lax.dynamic_slice_in_dim(summed[0], head_index * local_width, local_width, 0)
    out_b_value = lax.dynamic_slice_in_dim(summed[1], head_index * local_width, local_width, 0)
    out_b_up = lax.dynamic_slice_in_dim(summed[2], head_index * local_hidden, local_hidden, 0)
    return (
        result,
        latents_grad,
        summed[9],
        summed[5],
        summed[6],
        grad_w_query,
        out_b_query,
        grad_w_key,
        grad_w_value,
        out_b_value,
        grad_w_out,
        summed[3],
        summed[7],
        summed[8],
        grad_w_up,
        out_b_up,
        grad_w_down,
        summed[4],
    )


def on_device(
    latents, lang_ids, lang_table, gain_one, shift_one, w_query, b_query, w_key, w_value, b_value, w_out, b_out,
    gain_two, shift_two, w_up, b_up, w_down, b_down, cotangent,
):
    zs = lax.axis_size("dp") // 4
    r = forward(
        latents, cotangent, lang_ids, lang_table, (gain_one, shift_one, gain_two, shift_two, b_out, b_query, b_value, b_up),
        (w_query, w_key, w_value, w_out.T, w_up, w_down.T), zs)
    *large, small = backward(r, cotangent, lang_ids, (gain_one, gain_two, b_down), zs)
    got = hand_out(large, small)
    down, up, out, value, key, query, result, latents_grad, table = got[:9]
    b_out_g, b_down_g, gain_one_g, shift_one_g, gain_two_g, shift_two_g = got[9:15]
    b_query_g, b_value_g, b_up_g = got[15:]
    return (
        result, latents_grad, table, gain_one_g, shift_one_g, query, b_query_g, key, value, b_value_g, out.T, b_out_g,
        gain_two_g, shift_two_g, up, b_up_g, down.T, b_down_g,
    )

def solution(mesh):
    in_specs = (
        P(("dp", "head"), None),
        P(("dp", "head")),
        P(),
        P(),
        P(),
        P("dp", "head"),
        P("head"),
        P("dp", "head"),
        P("dp", "head"),
        P("head"),
        P("head", "dp"),
        P(),
        P(),
        P(),
        P("dp", "head"),
        P("head"),
        P("head", "dp"),
        P(),
        P(("dp", "head"), None),
    )
    out_specs = (
        P(("dp", "head"), None),
        P(("dp", "head"), None),
        P(),
        P(),
        P(),
        P("dp", "head"),
        P("head"),
        P("dp", "head"),
        P("dp", "head"),
        P("head"),
        P("head", "dp"),
        P(),
        P(),
        P(),
        P("dp", "head"),
        P("head"),
        P("head", "dp"),
        P(),
    )
    fast = mesh.shape["dp"] == 16 and mesh.shape["head"] == 2
    return jax.shard_map(
        on_device if fast else on_any_mesh, mesh=mesh, in_specs=in_specs, out_specs=out_specs, check_vma=False
    )
```

```python
import functools
import jax
import jax.numpy as jnp
from jax import lax
from jax.experimental import pallas as pl
from jax.experimental.pallas import tpu as pltpu
from jax.sharding import PartitionSpec as P

MESH = pl.DeviceIdType.MESH
BF = jnp.bfloat16
F32 = jnp.float32
HS = 160
LAT = 256
LANGS = 16
EPSILON = 1e-05
HIGHEST = lax.Precision.HIGHEST
ROOT_HALF = 0.7071067811865476
INV_ROOT_TWO_PI = 0.3989422804014327
FF = 1280


class Place:
    def __init__(self, zs):
        self.zs = zs
        i = lax.axis_index("dp")
        c = lax.axis_index("head")
        self.i, self.c = i, c
        self.z = i // 4
        self.sa = 1 + c
        self.sb = 2 - c
        x = i % 2
        y = (i // 2) % 2
        self.a = jnp.where(c == 0, x, y)
        self.b = jnp.where(c == 0, y, x)
        self.ia = i + self.sa * (1 - 2 * self.a)
        self.ib = i + self.sb * (1 - 2 * self.b)
        self.up = jnp.minimum(i + 4, 4 * zs - 1)
        self.down = jnp.maximum(i - 4, 0)
        self.has_up = self.z < zs - 1
        self.has_down = self.z > 0

    def barrier(self):
        bar = pltpu.get_barrier_semaphore()
        i, c = self.i, self.c
        for dev in ((self.ia, c), (self.ib, c), (i, 1 - c)):
            pl.semaphore_signal(bar, inc=1, device_id=dev, device_id_type=MESH)

        @pl.when(self.has_up)
        def _():
            pl.semaphore_signal(bar, inc=1, device_id=(self.up, c), device_id_type=MESH)

        @pl.when(self.has_down)
        def _():
            pl.semaphore_signal(bar, inc=1, device_id=(self.down, c), device_id_type=MESH)

    def barrier_wait(self):
        n = 3 + jnp.where(self.has_up, 1, 0) + jnp.where(self.has_down, 1, 0)
        pl.semaphore_wait(pltpu.get_barrier_semaphore(), n)

    def barrier_wide(self):
        bar = pltpu.get_barrier_semaphore()
        me = self.i % 4
        for n in range(8):
            @pl.when(jnp.logical_or(me != n // 2, self.c != n % 2))
            def _(n=n):
                pl.semaphore_signal(bar, inc=1, device_id=(self.i - me + n // 2, n % 2), device_id_type=MESH)
        for zz in range(self.zs):
            @pl.when(self.z != zz)
            def _(zz=zz):
                pl.semaphore_signal(bar, inc=1, device_id=(4 * zz + me, self.c), device_id_type=MESH)

    def barrier_wide_wait(self):
        pl.semaphore_wait(pltpu.get_barrier_semaphore(), 6 + self.zs)


ORDER_ONE = (
    0, 40, 60, 20, 80, 2, 42, 27, -1, 10, 67, 7, 23, -14, 22, 28, 47, -2, 68, 24,
    8, -13, 63, 50, 100, 48, 29, 82, 30, 31, 11, -3, 51, -15, 69, 9, 12, 32, 25, 64,
    13, 49, 62, 1, -4, 33, 107, -5, 71, 102, 21, -8, 87, 52, -7, 53, -9, 65, 108, 72,
    90, 41, -11, -17, -10, 88, -6, 103, -19, -16, -12, 70, 109, -20, 73, -18, 110, 91, 89, -21,
    104, 61, -22, -23, 105, 93, 92, -24, 112, 81, 111, -26, -25, 113, -27, 101,
)
ORDER_TWO = (
    100, 101, 2, 200, 1, 202, 0, 201, 110, 300, 503, 203, 20, 111, 211, 80, 210, 21, 301, 81,
    502, 22, 30, 302, 212, 213, 31, 82, 311, 310, 120, 303, 501, 121, 51, 32, 220, 221, 410, 613,
    41, 40, 700, 50, 312, 222, 411, 320, 612, 223, 523, 42, 52, 313, 321, 900, 140, 412, 130, 240,
    611, 131, 230, 241, 522, 413, 60, 231, 340, 232, 810, 322, 150, 543, 141, 151, 250, 330, 521, 251,
    331, 90, 242, 61, 233, 430, 633, 350, 341, 542, 91, 332, 252, 62, 351, 431, 632, 92, 70, 450,
    653, 342, 323, 243, 720, 432, 541, 352, 333, 71, 451, 652, 253, 11, 920, 631, 12, 343, 433, 740,
    452, 72, 651, 353, 10, 940, 830, 453, 73, 850,
)
SUM_MIDDLE = (True, False) * 3


def nn(a, b):
    return lax.dot_general(a, b, (((1,), (0,)), ((), ())), preferred_element_type=F32)


def nt(a, b):
    return lax.dot_general(a, b, (((1,), (1,)), ((), ())), preferred_element_type=F32)


def tn(a, b):
    return lax.dot_general(a, b, (((0,), (0,)), ((), ())), preferred_element_type=F32)


def item_rows(i):
    return pl.ds(i * LAT, LAT)


def head_window(hh):
    at = lax.broadcasted_iota(jnp.int32, (1, 256), 1) + hh * 128
    return (at >= hh * HS) & (at < (hh + 1) * HS)


class Gather:
    def __init__(self, p, w, sems, streams):
        self.p, self.w, self.streams = p, w, streams
        self.zsend, self.zrecv, self.asend, self.arecv, self.bsend, self.brecv, self.csend, self.crecv = sems
        self.cols = pl.ds(pl.multiple_of(p.c * 640, 128), 640)

    def sub(self, s, j, n=None):
        k, mid, r0, rows = self.streams[s]
        return self.w.at[k, j if n is None else pl.ds(j, n), pl.ds(r0, rows), self.cols]

    def mid(self, s):
        return self.streams[s][1]

    def send(self, s, j, n, dev, ssem, rsem):
        ref = self.sub(s, j) if n == 1 else self.sub(s, j, n)
        pltpu.make_async_remote_copy(ref, ref, ssem, rsem, device_id=dev, device_id_type=MESH).start()

    def arrived(self, s, n, sem):
        ref = self.sub(s, 0, n)
        pltpu.make_async_copy(ref, ref, sem).wait()

    def members(self, s, zz):
        p = self.p
        base = zz * 4 + p.b * p.sb
        return (base, base + p.sa) if self.mid(s) else (base + p.a * p.sa,)

    def z_send(self, s, zz, upward):
        p = self.p
        dev, d = ((p.up, p.c), 0) if upward else ((p.down, p.c), 1)
        for j in self.members(s, zz):
            self.send(s, j, 1, dev, self.zsend.at[s, d, zz], self.zrecv.at[s, zz])

    def z_first(self, s):
        p = self.p
        pl.when(p.has_up)(lambda: self.z_send(s, p.z, True))
        pl.when(p.has_down)(lambda: self.z_send(s, p.z, False))

    def at_distance(self, d, f):
        p = self.p
        pl.when(p.z - d >= 0)(lambda: f(p.z - d, True))
        pl.when(p.z + d <= p.zs - 1)(lambda: f(p.z + d, False))

    def around(self, d, f):
        if d == 0:
            f(self.p.z)
        else:
            self.at_distance(d, lambda zz, below: f(zz))

    def z_arrive(self, s, d, then):
        p = self.p
        n = len(self.members(s, 0))

        def f(zz, below):
            self.arrived(s, n, self.zrecv.at[s, zz])
            if d < p.zs - 1:
                if below:
                    pl.when(p.has_up)(lambda: self.z_send(s, zz, True))
                else:
                    pl.when(p.has_down)(lambda: self.z_send(s, zz, False))
            then(s, zz)

        self.at_distance(d, f)

    def a_send(self, s, zz):
        p = self.p
        j = zz * 4 + p.b * p.sb + p.a * p.sa
        self.send(s, j, 1, (p.ia, p.c), self.asend.at[s], self.arecv.at[s, zz])

    def a_arrive(self, s, zz, then):
        self.arrived(s, 1, self.arecv.at[s, zz])
        then(s, zz)

    def b_send(self, s, zz):
        p = self.p
        base = zz * 4 + p.b * p.sb
        for j in (base, base + p.sa):
            self.send(s, j, 1, (p.ib, p.c), self.bsend.at[s], self.brecv.at[s, zz])

    def b_arrive(self, s, zz):
        p = self.p
        self.arrived(s, 2, self.brecv.at[s, zz])
        self.send(s, zz * 4, 4, (p.i, 1 - p.c), self.csend.at[s], self.crecv.at[s])

    def do(self, s, ev):
        p = self.p
        if ev == 0:
            if not self.mid(s):
                self.z_first(s)
            self.a_send(s, p.z)
        elif ev == 1:
            self.arrived(s, 4 * p.zs, self.crecv.at[s])
        elif ev >= 10:
            self.around(ev - 10, lambda zz: self.b_arrive(s, zz))
        elif ev >= 6:
            self.z_arrive(s, ev - 6, self.b_send if self.mid(s) else self.a_send)
        elif self.mid(s):
            self.arrived(s, 1, self.arecv.at[s, p.z])
            self.z_first(s)
            self.b_send(s, p.z)
        else:
            self.around(ev - 2, lambda zz: self.a_arrive(s, zz, self.b_send))

    def drain(self, s):
        p = self.p
        n = len(self.members(s, 0))
        for zz in range(p.zs):
            @pl.when(jnp.logical_and(p.has_up, zz <= p.z))
            def _(zz=zz):
                self.arrived(s, n, self.zsend.at[s, 0, zz])

            @pl.when(jnp.logical_and(p.has_down, zz >= p.z))
            def _(zz=zz):
                self.arrived(s, n, self.zsend.at[s, 1, zz])
        self.arrived(s, 1 if self.mid(s) else p.zs, self.asend.at[s])
        self.arrived(s, 2 * p.zs, self.bsend.at[s])
        self.arrived(s, 4 * p.zs, self.csend.at[s])


STREAMS = tuple((k, k % 2 == 0, 0, 80) for k in range(6))
SAVED = ("ot", "q", "k", "v", "att", "hid", "slope", "tt", "ct", "u1", "u2")
TALL = ("ot", "tt", "ct")


def forward_kernel(zs, *refs):
    lat_in, cot_in, ids, table_in = refs[:4]
    vectors, shards = refs[4:12], refs[12:18]
    at = 18
    outs = dict(zip(("w",) + SAVED + ("mid", "inv", "pr"), refs[at:at + 15]))
    at += 15
    bufs = dict(zip(("w",) + SAVED + ("mid", "inv", "pr", "lat", "cot", "one", "two", "hb", "fulls", "table", "vec", "half"), refs[at:at + 24]))
    at += 24
    gsems = refs[at:at + 8]
    own, load, save, hsem, vsem = refs[at + 8:at + 13]
    p = Place(zs)
    p.barrier()
    w = bufs["w"]
    g = Gather(p, w, gsems, STREAMS)
    hb = bufs["hb"]
    copies = [pltpu.make_async_copy(shards[k], w.at[k, p.i, :, g.cols], own.at[k]) for k in range(6)]
    for cp in copies:
        cp.start()
    loads = [pltpu.make_async_copy(src.at[item_rows(i)], bufs[n].at[item_rows(i)], load.at[j, i])
             for j, (src, n) in enumerate(((lat_in, "lat"), (cot_in, "cot"))) for i in range(3)]
    for cp in loads:
        cp.start()
    fulls, table, vec, half = (bufs[n] for n in ("fulls", "table", "vec", "half"))
    places = [table] + list(vec) + list(half)
    short = [pltpu.make_async_copy(a, b, vsem.at[n]) for n, (a, b) in enumerate(zip((table_in,) + vectors, places))]
    for cp in short:
        cp.start()
    for cp in short:
        cp.wait()
    for n in range(5):
        fulls[n:n + 1, :] = row_of(vec[n])
    for n in range(3):
        hb[n:n + 1, g.cols] = row_of(half[n])
    p.barrier_wait()
    half_send = pltpu.make_async_remote_copy(hb.at[:, g.cols], hb.at[:, g.cols], hsem.at[0], hsem.at[1],
                                             device_id=(p.i, 1 - p.c), device_id_type=MESH)
    half_send.start()
    names = ("w",) + SAVED + ("mid", "inv", "pr")
    saves = []

    def keep(name, index=None):
        src, dst = bufs[name], outs[name]
        if index is not None:
            src, dst = src.at[index], dst.at[index]
        n = len(saves)
        assert n < save.shape[0]
        cp = pltpu.make_async_copy(src, dst, save.at[n])
        cp.start()
        saves.append(cp)

    def start_of(i):
        return bufs["lat"][item_rows(i)].astype(F32) + table[pl.ds(ids[i], 1), :]

    def norm(v):
        mean = jnp.mean(v, axis=1, keepdims=True)
        cen = v - mean
        inv = lax.rsqrt(jnp.mean(cen * cen, axis=1, keepdims=True) + EPSILON)
        return cen * inv, inv

    def norm_rows(i, n, rows_of, u_name, out_name, tall_name):
        gain, shift = fulls[2 * n:2 * n + 1, :], fulls[2 * n + 1:2 * n + 2, :]

        def body(r, carry):
            rows = pl.ds(pl.multiple_of(i * LAT + r * 64, 64), 64)
            unit, inv = norm(rows_of(rows))
            bufs[u_name][rows, :] = unit.astype(BF)
            bufs[out_name][rows, :] = (unit * gain + shift).astype(BF)
            bufs["inv"][n, rows, :] = jnp.broadcast_to(inv, (64, 128))
            return carry

        lax.fori_loop(0, 4, body, 0)
        bufs[tall_name][:, item_rows(i)] = bufs[out_name][item_rows(i), :].T

    def whole(k):
        return w[k].reshape(1280, 1280)

    def ln1(i):
        loads[i].wait()
        emb = table[pl.ds(ids[i], 1), :]
        norm_rows(i, 0, lambda rows: bufs["lat"][rows, :].astype(F32) + emb, "u1", "one", "ot")

    def project(name, k, bias):
        def f(i):
            y = nn(bufs["one"][item_rows(i), :], whole(k))
            if bias is not None:
                y = y + hb[bias:bias + 1, :]
            bufs[name][item_rows(i), :] = y.astype(BF)
        return f

    def cot(i):
        loads[3 + i].wait()
        bufs["ct"][:, item_rows(i)] = bufs["cot"][item_rows(i), :].T

    def attend(half):
        def f(i):
            rows = item_rows(i)
            zero = jnp.zeros((), BF)
            acc = [None] * 5
            for hh in range(4):
                lanes = pl.ds(half * 640 + hh * 128, 256)
                mask = head_window(hh)
                qm = jnp.where(mask, bufs["q"][rows, lanes], zero)
                s = nt(qm, bufs["k"][rows, lanes]) * (HS ** -0.5)
                e = jnp.exp(s - jnp.max(s, axis=1, keepdims=True))
                pr = (e / jnp.sum(e, axis=1, keepdims=True)).astype(BF)
                bufs["pr"][i * 8 + half * 4 + hh] = pr
                vm = jnp.where(mask, bufs["v"][rows, lanes], zero)
                a = nn(pr, vm)
                for t in (0, 1):
                    piece = a[:, t * 128:(t + 1) * 128]
                    acc[hh + t] = piece if acc[hh + t] is None else acc[hh + t] + piece
            for t in range(5):
                bufs["att"][rows, pl.ds(half * 640 + t * 128, 128)] = acc[t].astype(BF)
        return f

    def out(i):
        rows = item_rows(i)
        emb = table[pl.ds(ids[i], 1), :]
        y = nt(bufs["att"][rows, :], whole(3))
        bufs["mid"][rows, :] = y + fulls[4:5, :] + (bufs["lat"][rows, :].astype(F32) + emb)
        norm_rows(i, 1, lambda r: bufs["mid"][r, :], "u2", "two", "tt")

    def up(i):
        rows = item_rows(i)
        pre = nn(bufs["two"][rows, :], whole(4)) + hb[2:3, :]
        cdf = 0.5 * (1.0 + lax.erf(pre * ROOT_HALF))
        bufs["hid"][rows, :] = (pre * cdf).astype(BF)
        bufs["slope"][rows, :] = (cdf + pre * jnp.exp(-0.5 * pre * pre) * INV_ROOT_TWO_PI).astype(BF)

    units = (ln1, project("q", 0, 0), project("k", 1, None), project("v", 2, 1), cot, attend(0), attend(1), out, up)
    after = (("u1", "ot"), ("q",), ("k",), ("v",), ("ct",), (), ("att", "pr"), ("u2", "tt", "mid", "inv"), ("hid", "slope"))
    seen, full = set(), {}
    for code in ORDER_ONE:
        if code < 0:
            n, i = (-code - 1) // 3, (-code - 1) % 3
            if n == 1 and i == 0:
                half_send.wait_recv()
            units[n](i)
            if i == 2:
                for name in after[n]:
                    keep(name)
            continue
        s, ev = code // 20, code % 20
        k = STREAMS[s][0]
        if k not in seen:
            copies[k].wait()
            seen.add(k)
        g.do(s, ev)
        if ev == 1:
            full[k] = full.get(k, 0) + 1
            if full[k] == sum(t[0] == k for t in STREAMS):
                keep("w", k)
    half_send.wait_send()
    for s in range(len(STREAMS)):
        g.drain(s)
    for cp in saves:
        cp.wait()


def forward(latents, cotangent, ids, table, vectors, shards, zs):
    n = 4 * zs
    rows, width = latents.shape
    s = len(STREAMS)
    DMA = pltpu.SemaphoreType.DMA
    shape = {k: ((width, rows) if k in TALL else (rows, width), BF) for k in SAVED}
    shape["w"] = ((6, n, shards[0].shape[0], width), BF)
    shape["mid"] = ((rows, width), F32)
    shape["inv"] = ((2, rows, 128), F32)
    shape["pr"] = ((24, LAT, LAT), BF)
    for k in ("lat", "cot", "one", "two"):
        shape[k] = ((rows, width), BF)
    shape["hb"] = shape["fulls"] = ((8, width), F32)
    shape["table"] = ((LANGS, width), F32)
    names = ("w",) + SAVED + ("mid", "inv", "pr")
    got = pl.pallas_call(
        functools.partial(forward_kernel, zs),
        out_shape=[jax.ShapeDtypeStruct(*shape[k]) for k in names],
        in_specs=[pl.BlockSpec(memory_space=pl.ANY)] * 2 + [pl.BlockSpec(memory_space=pltpu.SMEM)]
        + [pl.BlockSpec(memory_space=pl.ANY)] * 15,
        out_specs=[pl.BlockSpec(memory_space=pl.ANY)] * len(names),
        scratch_shapes=[pltpu.VMEM(*shape[k]) for k in names + ("lat", "cot", "one", "two", "hb", "fulls", "table")] + [
            [pltpu.VMEM((width,), BF)] * 5, [pltpu.VMEM((width // 2,), BF)] * 3,
            DMA((s, 2, zs)), DMA((s, zs)), DMA((s,)), DMA((s, zs)), DMA((s,)), DMA((s, zs)), DMA((s,)), DMA((s,)),
            DMA((6,)), DMA((2, 3)), DMA((24,)), DMA((2,)), DMA((9,)),
        ],
        compiler_params=pltpu.CompilerParams(collective_id=0, has_side_effects=True, vmem_limit_bytes=62 << 20),
        name="gather_and_forward",
    )(latents, cotangent, ids, table, *vectors, *shards)
    return dict(zip(names, got))


NAMES_TWO = ("pool", "tall", "flat", "mg", "pr", "inv", "yb", "sm", "rc", "rb", "rzm", "rzf", "ram", "raf", "arp", "arz", "tot", "gouts", "vecs")


class Scatter:
    def __init__(self, p, g, bufs, outs, sems, middle):
        self.p, self.g, self.middle, self.outs = p, g, middle, outs
        self.rc, self.rb = bufs["rc"], bufs["rb"]
        self.rz, self.ra = (bufs["rzf"], bufs["rzm"]), (bufs["raf"], bufs["ram"])
        (self.csend, self.crecv, self.bsend, self.brecv, self.zsend, self.zrecv, self.asend, self.arecv, self.credit) = sems
        self.cols = pl.ds(pl.multiple_of(p.c * 640, 128), 640)
        self.others = pl.ds(pl.multiple_of((1 - p.c) * 640, 128), 640)

    def plane(self, t):
        val = jnp.int32(FAR[0][t])
        for s in range(1, self.p.zs):
            val = jnp.where(self.p.z == s, FAR[s][t], val)
        return val

    def own(self, k, j):
        return self.g(k).at[pl.ds(pl.multiple_of(j * 80, 80), 80), self.cols]

    def move(self, src, dst, dev, ssem, rsem):
        pltpu.make_async_remote_copy(src, dst, ssem, rsem, device_id=dev, device_id_type=MESH).start()

    def wait(self, ref, sem):
        pltpu.make_async_copy(ref, ref, sem).wait()

    def add(self, ref, val):
        ref[...] = ref[...] + val

    def group(self, t):
        return pl.ds(pl.multiple_of(self.plane(t) * 320, 320), 320)

    def c_send(self, k, t):
        p = self.p
        if k >= 3 and t == 0:
            pl.semaphore_wait(self.credit.at[k % 3], 1)
        rows = self.group(t)
        self.move(self.g(k).at[rows, self.others], self.rc.at[k % 3, rows], (p.i, 1 - p.c), self.csend.at[k], self.crecv.at[k, self.plane(t)])

    def c_arrive(self, k, t):
        p = self.p
        zz = self.plane(t)
        rows = self.group(t)
        src = self.rc.at[k % 3, rows]
        self.wait(src, self.crecv.at[k, zz])
        self.add(self.g(k).at[rows, self.cols], src[...])
        if k < 3 and t == 3:
            pl.semaphore_signal(self.credit.at[k], inc=1, device_id=(p.i, 1 - p.c), device_id_type=MESH)
        away = zz * 4 + (1 - p.b) * p.sb
        for n, j in enumerate((away, away + p.sa)):
            self.move(self.own(k, j), self.rb.at[k, zz * 2 + n], (p.ib, p.c), self.bsend.at[k], self.brecv.at[k, zz])

    def b_arrive(self, k, t):
        p = self.p
        zz = self.plane(t)
        self.wait(self.rb.at[k, pl.ds(zz * 2, 2)], self.brecv.at[k, zz])
        base = zz * 4 + p.b * p.sb
        for n, j in enumerate((base, base + p.sa)):
            self.add(self.own(k, j), self.rb[k, zz * 2 + n])
        if not self.middle[k]:
            self.move(self.own(k, base + (1 - p.a) * p.sa), self.ra[0].at[k // 2, zz], (p.ia, p.c), self.asend.at[k], self.arecv.at[k, zz])

    def a_arrive(self, k, t):
        p = self.p
        zz = self.plane(t)
        src = self.ra[0].at[k // 2, zz]
        self.wait(src, self.arecv.at[k, zz])
        self.add(self.own(k, zz * 4 + p.b * p.sb + p.a * p.sa), src[...])

    def members(self, k, zz):
        p = self.p
        base = zz * 4 + p.b * p.sb
        return (base, base + p.sa) if self.middle[k] else (base + p.a * p.sa,)

    def slot(self, zz, up, end):
        return zz if up or not end else self.p.zs

    def landing(self, k, zz, up, end):
        return self.rz[self.middle[k]].at[k // 2, self.slot(zz, up, end)]

    def z_take(self, k, zz, up, end):
        src = self.landing(k, zz, up, end)
        self.wait(src, self.zrecv.at[k, self.slot(zz, up, end)])
        for q, j in enumerate(self.members(k, zz)):
            self.add(self.own(k, j), src[q * 80:(q + 1) * 80])

    def z_pass(self, k, zz, up, end):
        p = self.p
        dev = (p.up if up else p.down, p.c)
        for q, j in enumerate(self.members(k, zz)):
            self.move(self.own(k, j), self.landing(k, zz, up, end).at[pl.ds(q * 80, 80)], dev, self.zsend.at[k, zz],
                      self.zrecv.at[k, self.slot(zz, up, end)])

    def z_step(self, k, d):
        p = self.p

        @pl.when(p.z + d <= p.zs - 1)
        def _():
            if d < p.zs - 1:
                pl.when(p.has_down)(lambda: self.z_take(k, p.z + d, True, False))
            self.z_pass(k, p.z + d, True, d == 1)

        @pl.when(p.z - d >= 0)
        def _():
            if d < p.zs - 1:
                pl.when(p.has_up)(lambda: self.z_take(k, p.z - d, False, False))
            self.z_pass(k, p.z - d, False, d == 1)

    def z_end(self, k):
        p = self.p
        pl.when(p.has_down)(lambda: self.z_take(k, p.z, True, True))
        pl.when(p.has_up)(lambda: self.z_take(k, p.z, False, True))
        if self.middle[k]:
            base = p.z * 4 + p.b * p.sb
            self.move(self.own(k, base + (1 - p.a) * p.sa), self.ra[1].at[k // 2], (p.ia, p.c), self.asend.at[k], self.arecv.at[k, 0])
        else:
            self.outs[k][...] = self.own(k, p.i)[...].astype(F32)

    def finish(self, k):
        src = self.ra[1].at[k // 2]
        self.wait(src, self.arecv.at[k, 0])
        self.outs[k][...] = self.own(k, self.p.i)[...].astype(F32) + src[...].astype(F32)

    def drain(self, k):
        p = self.p
        self.wait(self.rc.at[k % 3], self.csend.at[k])
        self.wait(self.rb.at[k], self.bsend.at[k])
        self.wait(self.ra[self.middle[k]].at[k // 2], self.asend.at[k])
        for zz in range(p.zs):
            @pl.when(p.z != zz)
            def _(zz=zz):
                self.wait(self.landing(k, zz, True, False), self.zsend.at[k, zz])


FAR = ((3, 2, 1, 0), (3, 2, 0, 1), (0, 1, 3, 2), (0, 1, 2, 3))
GRADS = ("down", "up", "out", "value", "key", "query")


def row_of(ref):
    return ref[...].astype(F32)[None, :]


def backward_kernel(zs, *refs):
    ids = refs[0]
    ins = dict(zip(("w",) + SAVED + ("mid", "inv", "pr", "cot"), refs[4:20]))
    outs = refs[20:26]
    res_out, lat_out, sm_out = refs[26:29]
    bufs = dict(zip(NAMES_TWO, refs[29:48]))
    rsems = refs[48:57]
    lsem, osem, tsem = refs[57:60]
    gain_one, gain_two, b_down = bufs["vecs"]
    p = Place(zs)
    p.barrier_wide()
    pool, tall, flat, mg, probs, inv, yb, sm = (bufs[n] for n in NAMES_TWO[:8])
    tokens = 768
    seat = (2, 3, 4, 5, 2, 3)
    s = Scatter(p, lambda k: pool.at[seat[k]], bufs, [bufs["gouts"].at[k] for k in range(6)], rsems, SUM_MIDDLE)
    count = [0]

    def load(src, dst):
        assert count[0] < lsem.shape[0]
        cp = pltpu.make_async_copy(src, dst, lsem.at[count[0]])
        count[0] += 1
        cp.start()
        return cp

    def slot(n, i=None):
        return flat.at[pl.ds(n * tokens, tokens)] if i is None else flat.at[pl.ds(n * tokens + i * LAT, LAT)]

    hid, pre, cot, u2, att, ky = range(6)
    ag, bg, qy, vy, u1 = hid, pre, cot, u2, att
    ready = {}

    def fetch(name, src, dst):
        ready[name] = load(src, dst)

    def need(name):
        cp = ready.pop(name, None)
        if cp is not None:
            cp.wait()

    fetch("hid", ins["hid"], slot(hid))
    fetch("ct", ins["ct"], tall.at[0])
    fetch("wd", ins["w"].at[5], pool.at[0])
    fetch("cot", ins["cot"], slot(cot))
    fetch("pre", ins["slope"], slot(pre))
    fetch("tt", ins["tt"], tall.at[1])
    fetch("wu", ins["w"].at[4], pool.at[1])
    fetch("u2", ins["u2"], slot(u2))
    fetch("inv", ins["inv"], inv)
    fetch("att", ins["att"], slot(att))
    fetch("ky", ins["k"], slot(ky))
    fetch("pr", ins["pr"], probs)
    for n, name in enumerate(("g1", "g2", "bd")):
        fetch(name, refs[1 + n], bufs["vecs"][n])
    sm[...] = jnp.zeros(sm.shape, F32)
    results, met = [], []

    def give(src, dst, n):
        cp = pltpu.make_async_copy(src, dst, osem.at[n])
        cp.start()
        results.append(cp)

    def col_sum(row, val):
        sm[row:row + 1, :] += jnp.sum(val, axis=0, keepdims=True)

    def blocks(i, f):
        def body(r, carry):
            f(pl.ds(pl.multiple_of(r * 128, 128), 128), pl.multiple_of(i * LAT + r * 128, 128))
            return carry
        lax.fori_loop(0, 2, body, 0)

    def at(n, start, size=128):
        return flat.at[pl.ds(n * tokens + start, size)]

    left = {"g0": (0, hid), "g1": (1, pre), "g2": (0, att), "g3": (1, vy), "g4": (1, ky), "g5": (1, qy)}
    before = (("hid", "ct"), ("tt",), ("att",), ("ot",), ("ot",), ("ot",))

    def grad(k, t):
        if t == 0:
            for n in before[k]:
                need(n)
            if k >= 4:
                s.drain(k - 4)
        a, b = left["g%d" % k]
        low = jnp.where((p.z < 2) == (t == 0), 640, 0)
        rows = pl.ds(pl.multiple_of(low, 640), 640)
        pool[seat[k], rows, :] = nn(tall[a, rows, :], slot(b)[...]).astype(BF)
        if not met:
            p.barrier_wide_wait()
            met.append(k)
        s.c_send(k, 2 * t)
        s.c_send(k, 2 * t + 1)

    def unit_p(i):
        for n in ("wd", "cot", "pre"):
            need(n)
        yb[...] = nn(slot(cot, i)[...], pool[0])

        def f(r, start):
            ref = at(pre, start)
            v = (yb[r, :] * ref[...].astype(F32)).astype(BF)
            ref[...] = v
            col_sum(2, v.astype(F32))
            col_sum(4, at(cot, start)[...].astype(F32))

        blocks(i, f)

    def unit_n(i):
        for n in ("wd", "hid", "bd", "mid%d" % i):
            need(n)
        yb[...] = nt(slot(vy, i)[...], pool[0])

        def f(r, start):
            at(vy, start)[...] = (mg[pl.ds(start, 128), :] + (yb[r, :] + row_of(b_down))).astype(BF)

        blocks(i, f)
        give(slot(vy, i), res_out.at[item_rows(i)], i)

    def norm_back(r, n, unit, start, gain_row, shift_row, gain):
        y = yb[r, :]
        v = unit[...].astype(F32)
        sc = y * gain
        m1 = jnp.mean(sc, axis=1, keepdims=True)
        m2 = jnp.mean(sc * v, axis=1, keepdims=True)
        col_sum(gain_row, y * v)
        col_sum(shift_row, y)
        iv = inv[n, pl.ds(start, 128), :][:, 0:1]
        return (sc - m1 - v * m2) * iv

    def unit_t(i):
        for n in ("wu", "u2", "inv", "g2"):
            need(n)
        yb[...] = nt(slot(pre, i)[...], pool[1])
        if i == 0:
            fetch("wo", ins["w"].at[3], pool.at[0])

    def unit_u(i):
        def f(r, start):
            back = norm_back(r, 1, at(u2, start), start, 7, 8, row_of(gain_two))
            m = at(cot, start)[...].astype(F32) + back
            mg[pl.ds(start, 128), :] = m
            b = m.astype(BF)
            at(bg, start)[...] = b
            col_sum(3, b.astype(F32))

        blocks(i, f)
        tall[0, :, item_rows(i)] = slot(bg, i)[...].T
        if i == 2:
            fetch("vy", ins["v"], slot(vy))
            fetch("qy", ins["q"], slot(qy))
            fetch("ot", ins["ot"], tall.at[1])
            fetch("wv", ins["w"].at[2], pool.at[1])

    def unit_y(i):
        need("wo")
        slot(ag, i)[...] = nn(slot(bg, i)[...], pool[0]).astype(BF)
        if i == 2:
            fetch("wk", ins["w"].at[1], pool.at[0])

    def unit_w(half):
        def f(i):
            for n in ("qy", "vy", "ky", "pr"):
                need(n)
            zero = jnp.zeros((), BF)
            accs = [[None] * 5 for _ in range(3)]
            qr, kr, vr, gr = slot(qy, i), slot(ky, i), slot(vy, i), slot(ag, i)
            for hh in range(4):
                lanes = pl.ds(half * 640 + hh * 128, 256)
                mask = head_window(hh)
                gm = jnp.where(mask, gr[:, lanes], zero)
                pb = probs[i * 8 + half * 4 + hh]
                dp = nt(gm, vr[:, lanes])
                pf = pb.astype(F32)
                inner = jnp.sum(dp * pf, axis=1, keepdims=True)
                ds = (pf * (dp - inner)).astype(BF)
                dv = tn(pb, gm)
                dq = nn(ds, jnp.where(mask, kr[:, lanes], zero)) * (HS ** -0.5)
                dk = tn(ds, jnp.where(mask, qr[:, lanes], zero)) * (HS ** -0.5)
                for acc, val in zip(accs, (dq, dk, dv)):
                    for t in (0, 1):
                        piece = val[:, t * 128:(t + 1) * 128]
                        acc[hh + t] = piece if acc[hh + t] is None else acc[hh + t] + piece
            for acc, ref, row in zip(accs, (qr, kr, vr), (0, None, 1)):
                for t in range(5):
                    lanes = pl.ds(half * 640 + t * 128, 128)
                    b = acc[t].astype(BF)
                    ref[:, lanes] = b
                    if row is not None:
                        sm[row:row + 1, lanes] += jnp.sum(b.astype(F32), axis=0, keepdims=True)
            if i == 2 and half == 1:
                fetch("wq", ins["w"].at[0], flat.at[pl.ds(0, 1280)])
                fetch("u1", ins["u1"], slot(u1))
        return f

    def unit_s(i):
        for n in ("wq", "wk", "wv", "u1", "g1"):
            need(n)
        yb[...] = nt(slot(qy, i)[...], flat[0:1280, :]) + nt(slot(ky, i)[...], pool[0])

    def unit_q(i):
        yb[...] += nt(slot(vy, i)[...], pool[1])
        mark = lax.broadcasted_iota(jnp.int32, (16, 1), 0) == ids[i]

        def f(r, start):
            back = norm_back(r, 0, at(u1, start), start, 5, 6, row_of(gain_one))
            g = mg[pl.ds(start, 128), :] + back
            at(qy, start)[...] = g.astype(BF)
            total = jnp.sum(g, axis=0, keepdims=True)
            sm[16:32, :] += jnp.where(mark, total, 0.0)

        blocks(i, f)
        if i == 2:
            fetch("wd", ins["w"].at[5], pool.at[0])
            fetch("hid", ins["hid"], slot(vy))
        fetch("mid%d" % i, ins["mid"].at[item_rows(i)], mg.at[item_rows(i)])
        give(slot(qy, i), lat_out.at[item_rows(i)], 3 + i)

    arp, arz, tot = (bufs[n] for n in ("arp", "arz", "tot"))
    me = p.i % 4
    mine = pl.ds(pl.multiple_of(me * 8, 8), 8)

    def other_planes(f):
        for j in range(zs):
            pl.when(p.z != j)(functools.partial(f, j))

    def plane_mates(f):
        for n in range(8):
            j, q = n // 2, n % 2
            pl.when(jnp.logical_or(me != j, p.c != q))(functools.partial(f, j, q, n))

    def copy(src, dst, j, q, n, m):
        pltpu.make_async_remote_copy(src, dst, tsem.at[n], tsem.at[m], device_id=(j, q), device_id_type=MESH).start()

    def local(ref, n):
        pltpu.make_async_copy(ref, ref, tsem.at[n]).wait()

    def total(n):
        self_n = me * 2 + p.c
        piece = lambda j, q: tot.at[pl.ds(8 * j, 8), pl.ds(640 * q, 640)]
        if n == 0:
            plane_mates(lambda j, q, m: copy(sm.at[pl.ds(8 * j, 8), pl.ds(640 * q, 640)], arp.at[self_n], p.i - me + j, q, 0, 4 + self_n))
            arp[self_n] = sm[mine, s.cols]
        elif n == 1:
            plane_mates(lambda j, q, m: local(arp.at[m], 4 + m))
            arz[p.z] = ((arp[0] + arp[1]) + (arp[2] + arp[3])) + ((arp[4] + arp[5]) + (arp[6] + arp[7]))
            other_planes(lambda j: copy(arz.at[p.z], arz.at[p.z], 4 * j + me, p.c, 1, 12 + p.z))
        elif n == 2:
            other_planes(lambda j: local(arz.at[j], 12 + j))
            tot[mine, s.cols] = (arz[0] + arz[1]) + (arz[2] + arz[3])
            part = tot.at[mine, s.cols]
            plane_mates(lambda j, q, m: copy(part, part, p.i - me + j, q, 2, 16 + self_n))
        else:
            plane_mates(lambda j, q, m: local(piece(j, q), 16 + m))
            give(tot, sm_out, 12)
            local(arp.at[pl.ds(0, 7)], 0)
            local(arz.at[pl.ds(0, 3)], 1)
            local(arp.at[pl.ds(0, 7)], 2)

    units = (unit_p, unit_n, unit_t, unit_y, unit_w(0), unit_w(1), unit_s, total, unit_u, unit_q)
    for code in ORDER_TWO:
        kind, k, t = code // 100, code // 10 % 10, code % 10
        if kind == 0:
            units[k](t)
        elif kind == 1:
            grad(k, t)
        elif kind == 2:
            s.c_arrive(k, t)
        elif kind == 3:
            s.b_arrive(k, t)
        elif kind == 4:
            s.a_arrive(k, t)
        elif kind == 5:
            s.z_step(k, t)
        elif kind == 6:
            s.z_step(k, t)
        elif kind <= 8:
            s.z_end(k)
        else:
            s.finish(k)
        if kind >= 8:
            give(bufs["gouts"].at[k], outs[k], 6 + k)
    for k in range(2, 6):
        s.drain(k)
    for cp in results:
        cp.wait()


def backward(r, cotangent, ids, vectors, zs):
    rows, width = cotangent.shape
    DMA = pltpu.SemaphoreType.DMA
    n = 4 * zs
    grow = width // n
    half = width // 2
    ins = [r["w"].reshape(6, width, width)] + [r[k] for k in SAVED] + [r["mid"], r["inv"], r["pr"], cotangent]
    shapes = dict(
        pool=((6, width, width), BF), tall=((2, width, rows), BF), flat=((6 * rows, width), BF), mg=((rows, width), F32),
        pr=((24, LAT, LAT), BF), inv=((2, rows, 128), F32), yb=((LAT, width), F32), sm=((32, width), F32),
        rc=((3, width, half), BF), rb=((6, 2 * zs, grow, half), BF), rzm=((3, zs + 1, 2 * grow, half), BF),
        rzf=((3, zs + 1, grow, half), BF), ram=((3, grow, half), BF), raf=((3, zs, grow, half), BF),
        arp=((8, 8, half), F32), arz=((zs, 8, half), F32), tot=((32, width), F32),
        gouts=((6, grow, half), F32))
    ANY = pl.BlockSpec(memory_space=pl.ANY)
    return pl.pallas_call(
        functools.partial(backward_kernel, zs),
        out_shape=[jax.ShapeDtypeStruct((grow, half), F32)] * 6 + [jax.ShapeDtypeStruct((rows, width), BF)] * 2
        + [jax.ShapeDtypeStruct((32, width), F32)],
        in_specs=[pl.BlockSpec(memory_space=pltpu.SMEM)] + [ANY] * (3 + len(ins)),
        out_specs=[ANY] * 9,
        scratch_shapes=[pltpu.VMEM(*shapes[k]) for k in NAMES_TWO[:-1]] + [
            [pltpu.VMEM((width,), BF)] * 3,
            DMA((6,)), DMA((6, zs)), DMA((6,)), DMA((6, zs)), DMA((6, zs)), DMA((6, zs + 1)), DMA((6,)), DMA((6, zs)),
            pltpu.SemaphoreType.REGULAR((3,)), DMA((32,)), DMA((13,)), DMA((24,)),
        ],
        compiler_params=pltpu.CompilerParams(collective_id=1, has_side_effects=True, vmem_limit_bytes=63 << 20),
        name="backward_and_scatter",
    )(ids, *vectors, *ins)


def hand_out_kernel(large, *refs):
    ins, outs = refs[:large + 1], refs[large + 1:2 * large + 11]
    stage, sm, table, wide, narrow, isem, osem = refs[2 * large + 11:]
    half = narrow[0].shape[0]
    first = pltpu.make_async_copy(ins[large], sm, isem.at[0])
    first.start()
    copies = []
    for a, v, b in zip(ins, stage, outs):
        step = min(a.shape[0], LAT)
        for r in range(0, a.shape[0], step):
            rows, n = pl.ds(r, step), len(copies) + 1
            copies.append((pltpu.make_async_copy(a.at[rows], v.at[rows], isem.at[n]), pltpu.make_async_copy(v.at[rows], b.at[rows], osem.at[n])))
    copies.sort(key=lambda pair: -pair[0].src_ref.shape[0])
    for cp, _ in copies:
        cp.start()
    first.wait()
    table[...] = sm[16:32, :]
    back = [pltpu.make_async_copy(table, outs[large], osem.at[0])]
    for n in range(6):
        wide[n][...] = sm[3 + n:4 + n, :].reshape(wide[n].shape)
        back.append(pltpu.make_async_copy(wide[n], outs[large + 1 + n], osem.at[20 + n]))
    cols = pl.ds(pl.multiple_of(lax.axis_index("head") * half, 128), half)
    for n in range(3):
        narrow[n][...] = sm[n:n + 1, cols].reshape(half)
        back.append(pltpu.make_async_copy(narrow[n], outs[large + 7 + n], osem.at[26 + n]))
    for cp in back:
        cp.start()
    for cp, out in copies:
        cp.wait()
        out.start()
        back.append(out)
    for cp in back:
        cp.wait()


def hand_out(large, small):
    width = small.shape[1]
    ANY = pl.BlockSpec(memory_space=pl.ANY)
    n = len(large)
    like = [jax.ShapeDtypeStruct(a.shape, a.dtype) for a in large]
    return pl.pallas_call(
        functools.partial(hand_out_kernel, n),
        out_shape=like + [jax.ShapeDtypeStruct((16, width), F32)]
        + [jax.ShapeDtypeStruct((width,), F32)] * 6 + [jax.ShapeDtypeStruct((width // 2,), F32)] * 3,
        in_specs=[ANY] * (n + 1),
        out_specs=[ANY] * (n + 10),
        scratch_shapes=[[pltpu.VMEM(a.shape, a.dtype) for a in large], pltpu.VMEM(small.shape, F32), pltpu.VMEM((16, width), F32),
                        [pltpu.VMEM((width,), F32)] * 6, [pltpu.VMEM((width // 2,), F32)] * 3] + [pltpu.SemaphoreType.DMA((32,))] * 2,
        compiler_params=pltpu.CompilerParams(vmem_limit_bytes=63 << 20),
        name="hand_out",
    )(*large, small)


def in_blocks(x, dim, length):
    before, after = (x.shape[:dim], x.shape[dim + 1 :])
    return jnp.moveaxis(x.reshape(*before, length, -1, *after), dim, 0)


def sent_and_summed(x, axis, dim):
    tiles = in_blocks(x, dim, lax.axis_size(axis))
    arrived = lax.all_to_all(tiles, axis, split_axis=0, concat_axis=0, tiled=True)
    return arrived.astype(jnp.float32).sum(axis=0)


def side_by_side(arrays, axis, dim, along):
    ends, at = ([], 0)
    for a in arrays[:-1]:
        at += a.shape[along]
        ends.append(at)
    both = jnp.concatenate(arrays, axis=along)
    return tuple(jnp.split(sent_and_summed(both, axis, dim), ends, axis=along))


def norm_forward(row_block, norm_gain, norm_shift):
    row_mean = jnp.mean(row_block, axis=1, keepdims=True)
    centered = row_block - row_mean
    row_var = jnp.mean(centered * centered, axis=1, keepdims=True)
    inverse = lax.rsqrt(row_var + EPSILON)
    normed = centered * inverse
    return (normed * norm_gain + norm_shift, normed, inverse)


def norm_backward(grad_rows, normed, inverse, norm_gain):
    scaled = grad_rows * norm_gain
    first_moment = jnp.mean(scaled, axis=1, keepdims=True)
    second_moment = jnp.mean(scaled * normed, axis=1, keepdims=True)
    grad_input = (scaled - first_moment - normed * second_moment) * inverse
    return (grad_input, jnp.sum(grad_rows * normed, axis=0), jnp.sum(grad_rows, axis=0))


def contract_rows(left, right):
    return lax.dot_general(
        left, right, (((0,), (0,)), ((), ())), preferred_element_type=jnp.float32
    )


def contract_cols(left, right):
    return lax.dot_general(
        left, right, (((1,), (1,)), ((), ())), preferred_element_type=jnp.float32
    )


def split_heads(matrix):
    item_count = matrix.shape[0] // LAT
    return matrix.reshape(item_count, LAT, matrix.shape[1] // HS, HS)


def attend_forward(query_rows, key_rows, value_rows):
    factor = HS ** (-0.5)
    scores = (
        jnp.einsum(
            "iqhc,ikhc->ihqk",
            split_heads(query_rows),
            split_heads(key_rows),
            preferred_element_type=jnp.float32,
        )
        * factor
    )
    row_max = jnp.max(scores, axis=-1, keepdims=True)
    exp_scores = jnp.exp(scores - row_max)
    row_total = jnp.sum(exp_scores, axis=-1, keepdims=True)
    soft_probs = (exp_scores / row_total).astype(jnp.bfloat16)
    attended = jnp.einsum(
        "ihqk,ikhc->iqhc", soft_probs, split_heads(value_rows), preferred_element_type=jnp.float32
    )
    return (attended.reshape(query_rows.shape).astype(jnp.bfloat16), row_max + jnp.log(row_total))


def attend_backward(query_rows, key_rows, value_rows, log_total, attended_grad):
    factor = HS ** (-0.5)
    query_heads = split_heads(query_rows)
    key_heads = split_heads(key_rows)
    value_heads = split_heads(value_rows)
    grad_heads = split_heads(attended_grad)
    scores = (
        jnp.einsum("iqhc,ikhc->ihqk", query_heads, key_heads, preferred_element_type=jnp.float32)
        * factor
    )
    soft_probs = jnp.exp(scores - log_total)
    value_grad = jnp.einsum(
        "ihqk,iqhc->ikhc",
        soft_probs.astype(jnp.bfloat16),
        grad_heads,
        preferred_element_type=jnp.float32,
    )
    probs_grad = jnp.einsum(
        "iqhc,ikhc->ihqk", grad_heads, value_heads, preferred_element_type=jnp.float32
    )
    inner_sum = jnp.sum(probs_grad * soft_probs, axis=-1, keepdims=True)
    score_grad = (soft_probs * (probs_grad - inner_sum)).astype(jnp.bfloat16)
    query_grad = (
        jnp.einsum("ihqk,ikhc->iqhc", score_grad, key_heads, preferred_element_type=jnp.float32)
        * factor
    )
    key_grad = (
        jnp.einsum("ihqk,iqhc->ikhc", score_grad, query_heads, preferred_element_type=jnp.float32)
        * factor
    )
    full_shape = query_rows.shape
    return (
        query_grad.reshape(full_shape).astype(jnp.bfloat16),
        key_grad.reshape(full_shape).astype(jnp.bfloat16),
        value_grad.reshape(full_shape).astype(jnp.bfloat16),
    )


def gelu_value(pre_act):
    return 0.5 * pre_act * (1.0 + lax.erf(pre_act * ROOT_HALF))


def gelu_slope(pre_act):
    return (
        0.5 * (1.0 + lax.erf(pre_act * ROOT_HALF))
        + pre_act * jnp.exp(-0.5 * pre_act * pre_act) * INV_ROOT_TWO_PI
    )


def place_slot(piece, head_index, full_len):
    empty = jnp.zeros((full_len,), jnp.float32)
    return lax.dynamic_update_slice_in_dim(empty, piece, head_index * piece.shape[0], 0)


def on_any_mesh(
    latents,
    lang_ids,
    lang_table,
    gain_one,
    shift_one,
    w_query,
    b_query,
    w_key,
    w_value,
    b_value,
    w_out,
    b_out,
    gain_two,
    shift_two,
    w_up,
    b_up,
    w_down,
    b_down,
    cotangent,
):
    own_rows = latents.shape[0]
    model_width = latents.shape[1]
    item_count = lang_ids.shape[0]
    head_index = lax.axis_index("head")
    head_count = lax.axis_size("head")
    w_query, w_key, w_value, w_up, w_out, w_down = (
        lax.all_gather(w_query, "dp", axis=0, tiled=True),
        lax.all_gather(w_key, "dp", axis=0, tiled=True),
        lax.all_gather(w_value, "dp", axis=0, tiled=True),
        lax.all_gather(w_up, "dp", axis=0, tiled=True),
        lax.all_gather(w_out, "dp", axis=1, tiled=True),
        lax.all_gather(w_down, "dp", axis=1, tiled=True),
    )
    one_hot = (lang_ids[:, None] == jnp.arange(LANGS, dtype=jnp.int32)[None, :]).astype(jnp.float32)
    embedded = jnp.dot(one_hot, lang_table, precision=HIGHEST)
    start_rows = (
        latents.astype(jnp.float32).reshape(item_count, LAT, model_width) + embedded[:, None, :]
    ).reshape(own_rows, model_width)
    gain_first = gain_one.astype(jnp.float32)
    gain_second = gain_two.astype(jnp.float32)
    normed_one, unit_one, inverse_one = norm_forward(
        start_rows, gain_first, shift_one.astype(jnp.float32)
    )
    input_one = normed_one.astype(jnp.bfloat16)
    group_one = lax.all_gather(input_one, "head", axis=0, tiled=True)
    query_rows = (
        jnp.dot(group_one, w_query, preferred_element_type=jnp.float32)
        + b_query.astype(jnp.float32)
    ).astype(jnp.bfloat16)
    key_rows = jnp.dot(group_one, w_key, preferred_element_type=jnp.float32).astype(jnp.bfloat16)
    value_rows = (
        jnp.dot(group_one, w_value, preferred_element_type=jnp.float32)
        + b_value.astype(jnp.float32)
    ).astype(jnp.bfloat16)
    attended, log_total = attend_forward(query_rows, key_rows, value_rows)
    attn_branch = lax.psum_scatter(
        jnp.dot(attended, w_out, preferred_element_type=jnp.float32),
        "head",
        scatter_dimension=0,
        tiled=True,
    )
    middle_rows = start_rows + (attn_branch + b_out.astype(jnp.float32))
    normed_two, unit_two, inverse_two = norm_forward(
        middle_rows, gain_second, shift_two.astype(jnp.float32)
    )
    input_two = normed_two.astype(jnp.bfloat16)
    group_two = lax.all_gather(input_two, "head", axis=0, tiled=True)
    pre_act = jnp.dot(group_two, w_up, preferred_element_type=jnp.float32) + b_up.astype(
        jnp.float32
    )
    hidden = gelu_value(pre_act).astype(jnp.bfloat16)
    down_branch = lax.psum_scatter(
        jnp.dot(hidden, w_down, preferred_element_type=jnp.float32).astype(jnp.bfloat16),
        "head",
        scatter_dimension=0,
        tiled=True,
    ).astype(jnp.float32)
    result = (middle_rows + (down_branch + b_down.astype(jnp.float32))).astype(jnp.bfloat16)
    group_cot = lax.all_gather(cotangent, "head", axis=0, tiled=True)
    grad_w_down = contract_rows(hidden, group_cot)
    grad_b_down = jnp.sum(cotangent.astype(jnp.float32), axis=0)
    pre_grad = (contract_cols(group_cot, w_down) * gelu_slope(pre_act)).astype(jnp.bfloat16)
    grad_w_up = contract_rows(group_two, pre_grad)
    grad_b_up = jnp.sum(pre_grad.astype(jnp.float32), axis=0)
    grad_two = lax.psum_scatter(
        contract_cols(pre_grad, w_up), "head", scatter_dimension=0, tiled=True
    )
    back_two, grad_gain_two, grad_shift_two = norm_backward(
        grad_two, unit_two, inverse_two, gain_second
    )
    middle_grad = cotangent.astype(jnp.float32) + back_two
    branch_grad = middle_grad.astype(jnp.bfloat16)
    grad_b_out = jnp.sum(branch_grad.astype(jnp.float32), axis=0)
    group_branch = lax.all_gather(branch_grad, "head", axis=0, tiled=True)
    grad_w_out = contract_rows(attended, group_branch)
    attended_grad = contract_cols(group_branch, w_out).astype(jnp.bfloat16)
    query_grad, key_grad, value_grad = attend_backward(
        query_rows, key_rows, value_rows, log_total, attended_grad
    )
    grad_w_query = contract_rows(group_one, query_grad)
    grad_w_key = contract_rows(group_one, key_grad)
    grad_w_value = contract_rows(group_one, value_grad)
    grad_b_query = jnp.sum(query_grad.astype(jnp.float32), axis=0)
    grad_b_value = jnp.sum(value_grad.astype(jnp.float32), axis=0)
    total_term = contract_cols(query_grad, w_query)
    total_term = total_term + contract_cols(key_grad, w_key)
    grad_one = lax.psum_scatter(
        (total_term + contract_cols(value_grad, w_value)).astype(jnp.bfloat16),
        "head",
        scatter_dimension=0,
        tiled=True,
    ).astype(jnp.float32)
    back_one, grad_gain_one, grad_shift_one = norm_backward(
        grad_one, unit_one, inverse_one, gain_first
    )
    start_grad = middle_grad + back_one
    latents_grad = start_grad.astype(jnp.bfloat16)
    item_sums = jnp.sum(start_grad.reshape(item_count, LAT, model_width), axis=1)
    grad_table = jnp.dot(one_hot.T, item_sums, precision=HIGHEST)
    full_b_query = place_slot(grad_b_query, head_index, model_width)
    full_b_value = place_slot(grad_b_value, head_index, model_width)
    full_b_up = place_slot(grad_b_up, head_index, FF)
    grad_w_query, grad_w_key, grad_w_value, grad_w_up, grad_w_out, grad_w_down = (
        *side_by_side(
            (
                grad_w_query.astype(jnp.bfloat16),
                grad_w_key.astype(jnp.bfloat16),
                grad_w_value.astype(jnp.bfloat16),
                grad_w_up.astype(jnp.bfloat16),
            ),
            "dp",
            0,
            1,
        ),
        *side_by_side(
            (grad_w_out.astype(jnp.bfloat16), grad_w_down.astype(jnp.bfloat16)), "dp", 1, 0
        ),
    )
    summed = lax.psum(
        (
            full_b_query,
            full_b_value,
            full_b_up,
            grad_b_out,
            grad_b_down,
            grad_gain_one,
            grad_shift_one,
            grad_gain_two,
            grad_shift_two,
            grad_table,
        ),
        ("dp", "head"),
    )
    local_width = model_width // head_count
    local_hidden = FF // head_count
    out_b_query = lax.dynamic_slice_in_dim(summed[0], head_index * local_width, local_width, 0)
    out_b_value = lax.dynamic_slice_in_dim(summed[1], head_index * local_width, local_width, 0)
    out_b_up = lax.dynamic_slice_in_dim(summed[2], head_index * local_hidden, local_hidden, 0)
    return (
        result,
        latents_grad,
        summed[9],
        summed[5],
        summed[6],
        grad_w_query,
        out_b_query,
        grad_w_key,
        grad_w_value,
        out_b_value,
        grad_w_out,
        summed[3],
        summed[7],
        summed[8],
        grad_w_up,
        out_b_up,
        grad_w_down,
        summed[4],
    )


def on_device(
    latents, lang_ids, lang_table, gain_one, shift_one, w_query, b_query, w_key, w_value, b_value, w_out, b_out,
    gain_two, shift_two, w_up, b_up, w_down, b_down, cotangent,
):
    zs = lax.axis_size("dp") // 4
    r = forward(
        latents, cotangent, lang_ids, lang_table, (gain_one, shift_one, gain_two, shift_two, b_out, b_query, b_value, b_up),
        (w_query, w_key, w_value, w_out.T, w_up, w_down.T), zs)
    *large, small = backward(r, cotangent, lang_ids, (gain_one, gain_two, b_down), zs)
    got = hand_out(large, small)
    down, up, out, value, key, query, result, latents_grad, table = got[:9]
    b_out_g, b_down_g, gain_one_g, shift_one_g, gain_two_g, shift_two_g = got[9:15]
    b_query_g, b_value_g, b_up_g = got[15:]
    return (
        result, latents_grad, table, gain_one_g, shift_one_g, query, b_query_g, key, value, b_value_g, out.T, b_out_g,
        gain_two_g, shift_two_g, up, b_up_g, down.T, b_down_g,
    )

def solution(mesh):
    in_specs = (
        P(("dp", "head"), None),
        P(("dp", "head")),
        P(),
        P(),
        P(),
        P("dp", "head"),
        P("head"),
        P("dp", "head"),
        P("dp", "head"),
        P("head"),
        P("head", "dp"),
        P(),
        P(),
        P(),
        P("dp", "head"),
        P("head"),
        P("head", "dp"),
        P(),
        P(("dp", "head"), None),
    )
    out_specs = (
        P(("dp", "head"), None),
        P(("dp", "head"), None),
        P(),
        P(),
        P(),
        P("dp", "head"),
        P("head"),
        P("dp", "head"),
        P("dp", "head"),
        P("head"),
        P("head", "dp"),
        P(),
        P(),
        P(),
        P("dp", "head"),
        P("head"),
        P("head", "dp"),
        P(),
    )
    fast = mesh.shape["dp"] == 16 and mesh.shape["head"] == 2
    return jax.shard_map(
        on_device if fast else on_any_mesh, mesh=mesh, in_specs=in_specs, out_specs=out_specs, check_vma=False
    )
```
